128 devices in a mesh: ctx: 16 (over x_lo, y, core), fsdp: 8 (over z, x_hi).
Axes of the slice: x: 4 (x_hi: 2, x_lo: 2; x = x_hi * 2 + x_lo), y: 4, z: 4, core: 2. Of those that a mesh axis runs over, the one named last changes fastest.
Arguments:
- hidden_in: bfloat16 [8, 2048, 1024], P('fsdp', 'ctx'), may hold values from -6 to 6
- qkv_weight: bfloat16 [1024, 3072], P('fsdp'), may hold values from -0.1875 to 0.1875
- out_weight: bfloat16 [1024, 1024], P('fsdp'), may hold values from -4 to 4
- gate_up_weight: bfloat16 [1024, 5248], P('fsdp'), may hold values from -0.1875 to 0.1875
- down_weight: bfloat16 [2624, 1024], P('fsdp'), may hold values from -0.125 to 0.125
- attn_gain: bfloat16 [1024], P('fsdp'), may hold values from 0.5 to 1.5
- mlp_gain: bfloat16 [1024], P('fsdp'), may hold values from 0.5 to 1.5
- out_grad: bfloat16 [8, 2048, 1024], P('fsdp', 'ctx'), may hold values from -6 to 6
Outputs:
- result: bfloat16 [8, 2048, 1024], P('fsdp', 'ctx')
- input_grad: bfloat16 [8, 2048, 1024], P('fsdp', 'ctx')
- qkv_grad: float32 [1024, 3072], P('fsdp')
- out_weight_grad: float32 [1024, 1024], P('fsdp')
- gate_up_grad: float32 [1024, 5248], P('fsdp')
- down_grad: float32 [2624, 1024], P('fsdp')
- attn_gain_grad: float32 [1024], P('fsdp')
- mlp_gain_grad: float32 [1024], P('fsdp')
The draws below stay inside these ranges and needn't reach their ends.
All inputs are finite; a program needn't handle non-finite values.
Results may differ from the reference program's by a relative error of at most 0.025.
Values may be sent and summed in bfloat16 or wider, within the bound.
A program may use at most 128 MiB of HBM per device.

```python
import jax
import jax.numpy as jnp
from jax import lax

D = 1024
HEADS = 16
FF = 2624
LENGTH = 2048
SEQS = 8


def block_levels(key, extent, shards, low, largest):
    level = 1.0
    for position, blocks in shards:
        heights = jax.random.uniform(jax.random.fold_in(jax.random.fold_in(key, 6), position), (blocks,), jnp.float32, low / len(shards), largest / len(shards))
        level = level * jnp.repeat(jnp.exp(heights), extent[position] // blocks).reshape((-1,) + (1,) * (len(extent) - 1 - position))
    return level


def centred(own_key, dims, width, bound, cuts=(), held_as=jnp.bfloat16):
    result = width * jax.random.normal(own_key, dims, jnp.float32)
    if cuts:
        result = result * block_levels(own_key, dims, cuts, -0.22, 0.18)
    return jnp.clip(result, -bound, bound).astype(held_as)


def setup_inputs(seed: int = 0) -> dict:
    keys = jax.random.split(jax.random.key(seed), 9)
    return {
        "hidden_in": centred(keys[0], (SEQS, LENGTH, D), 1.0, 6.0, ((0, 8), (1, 16))),
        "qkv_weight": centred(keys[1], (D, 3 * D), D ** -0.5, 0.1875, ((0, 8),)),
        "out_weight": centred(keys[2], (D, D), (max(1, D * 4 // LENGTH)) ** -0.5, 4.0, ((0, 8),)),
        "gate_up_weight": centred(keys[3], (D, 2 * FF), D ** -0.5, 0.1875, ((0, 8),)),
        "down_weight": centred(keys[4], (FF, D), FF ** -0.5, 0.125, ((0, 8),)),
        "attn_gain": jnp.clip(1.0 + 0.1 * jax.random.normal(keys[5], (D,), jnp.float32), 0.5, 1.5).astype(jnp.bfloat16),
        "mlp_gain": jnp.clip(1.0 + 0.1 * jax.random.normal(keys[6], (D,), jnp.float32), 0.5, 1.5).astype(jnp.bfloat16),
        "out_grad": centred(keys[7], (SEQS, LENGTH, D), 1.0, 6.0, ((0, 8), (1, 16))),
    }


EPSILON = 1e-05
ROPE_BASE = 160000.0

@jax.custom_vjp
def low(v):
    return lax.optimization_barrier(v.astype(jnp.bfloat16)).astype(jnp.float32)

@jax.custom_vjp
def low_back(v):
    return v

def low_keep(v):
    return (low(v), None)

def low_pass(kept, grad):
    return (grad,)

def back_keep(v):
    return (v, None)

def back_low(kept, grad):
    return (low(grad),)
low.defvjp(low_keep, low_pass)
low_back.defvjp(back_keep, back_low)

def rope_tables(positions, head_size):
    half_size = head_size // 2
    inverse = ROPE_BASE ** (-(jnp.arange(half_size, dtype=jnp.float32) * 2.0) / head_size)
    angles = positions.astype(jnp.float32)[:, None] * inverse[None, :]
    return (jnp.cos(angles)[:, None, :], jnp.sin(angles)[:, None, :])

def rotate_heads(values_in, cos_table, sin_table):
    half_size = values_in.shape[-1] // 2
    first = values_in[..., :half_size]
    second = values_in[..., half_size:]
    return jnp.concatenate([first * cos_table - second * sin_table, second * cos_table + first * sin_table], axis=-1)

def layer_norm(values_in, gain):
    centered = values_in - lax.optimization_barrier(jnp.mean(values_in, axis=-1, keepdims=True))
    return centered * lax.rsqrt(lax.optimization_barrier(jnp.mean(centered * centered, axis=-1, keepdims=True)) + EPSILON) * gain

def head_attend(block):
    query_h, key_h, value_h = block
    scale = query_h.shape[-1] ** (-0.5)
    scores = low_back(jnp.dot(query_h, key_h.T, precision=lax.Precision.HIGHEST) * scale)
    weights = low(jax.nn.softmax(scores, axis=-1))
    return jnp.dot(weights, value_h, precision=lax.Precision.HIGHEST)

def sequence_forward(tokens, w_qkv, w_out, w_gate_up, w_down, gain_one, gain_two):
    seq_len = tokens.shape[0]
    model_width = tokens.shape[1]
    head_size = model_width // HEADS
    cos_table, sin_table = rope_tables(jnp.arange(seq_len), head_size)
    normed_one = low(layer_norm(tokens, gain_one))
    projected = low_back(jnp.dot(normed_one, w_qkv, precision=lax.Precision.HIGHEST))
    queries = projected[:, :model_width].reshape(seq_len, HEADS, head_size)
    keys_part = projected[:, model_width:2 * model_width].reshape(seq_len, HEADS, head_size)
    values_part = projected[:, 2 * model_width:].reshape(seq_len, HEADS, head_size)
    query_b = low(rotate_heads(queries, cos_table, sin_table)).transpose(1, 0, 2)
    key_b = low(rotate_heads(keys_part, cos_table, sin_table)).transpose(1, 0, 2)
    value_b = low(values_part).transpose(1, 0, 2)
    mixed = lax.map(jax.checkpoint(head_attend), (query_b, key_b, value_b))
    attended = low(low_back(mixed.transpose(1, 0, 2).reshape(seq_len, model_width)))
    first_sum = tokens + low_back(jnp.dot(attended, w_out, precision=lax.Precision.HIGHEST))
    normed_two = low(layer_norm(first_sum, gain_two))
    gate_up = low_back(jnp.dot(normed_two, w_gate_up, precision=lax.Precision.HIGHEST))
    hidden_units = w_down.shape[0]
    activated = low(jax.nn.gelu(gate_up[:, :hidden_units], approximate=False) * gate_up[:, hidden_units:])
    return first_sum + low_back(jnp.dot(activated, w_down, precision=lax.Precision.HIGHEST))

def reference(hidden_in, qkv_weight, out_weight, gate_up_weight, down_weight, attn_gain, mlp_gain, out_grad):
    params = tuple((item.astype(jnp.float32) for item in (qkv_weight, out_weight, gate_up_weight, down_weight, attn_gain, mlp_gain)))

    def forward(inputs, w_qkv, w_out, w_gate_up, w_down, gain_one, gain_two):

        def one_sequence(tokens):
            return sequence_forward(tokens, w_qkv, w_out, w_gate_up, w_down, gain_one, gain_two)
        return lax.map(jax.checkpoint(one_sequence), inputs)
    outputs, pullback = jax.vjp(forward, hidden_in.astype(jnp.float32), *params)
    grads = pullback(out_grad.astype(jnp.float32))
    return (outputs.astype(jnp.bfloat16), grads[0].astype(jnp.bfloat16), grads[1], grads[2], grads[3], grads[4], grads[5], grads[6])
```

```python
import jax
import jax.numpy as jnp
import numpy as np
from jax import lax
from jax.experimental import pallas as pl
from jax.experimental.pallas import tpu as pltpu
from jax.sharding import PartitionSpec as P

HEADS = 16
EPSILON = 1e-05
ROPE_BASE = 160000.0
F32 = jnp.float32
BF16 = jnp.bfloat16
MESH = pl.DeviceIdType.MESH
ANY = pl.BlockSpec(memory_space=pl.ANY)
VMEM = pl.BlockSpec(memory_space=pltpu.VMEM)
MIB = 1024 * 1024


class Place:
    def __init__(self):
        c = lax.axis_index("ctx")
        self.c = c
        self.f = lax.axis_index("fsdp")
        k = c % 2
        y = (c // 2) % 4
        xl = c // 8
        self.k = k

        def at(x, row):
            return x * 4 + row % 4

        ox = 1 - xl
        self.other = c + 1 - 2 * k
        self.chip = {
            "S": at(xl, y),
            "P": at(xl, y + 1),
            "M": at(xl, y + 3),
            "F": at(xl, y + 2),
            "X": at(ox, y),
            "XP": at(ox, y + 1),
            "XM": at(ox, y + 3),
            "XF": at(ox, y + 2),
        }

        self.same_core = {name: chip * 2 + k for name, chip in self.chip.items()}
        self.cross_core = {name: chip * 2 + 1 - k for name, chip in self.chip.items()}
        self.ring = [(c + d) % 16 for d in range(16)]
        z, xh = self.f // 2, self.f % 2
        self.twin = z * 2 + 1 - xh
        self.planes = [(z + d) % 4 * 2 + xh for d in range(4)]
        self.twin_planes = [(z + d) % 4 * 2 + 1 - xh for d in range(4)]
        self.fsdp_peers = [{"fsdp": i} for i in [self.twin] + self.planes[1:]]

    def same(self, name):
        return self.same_core[name]

    def cross(self, name):
        return self.cross_core[name]


def lanes_of(f):
    return pl.ds(pl.multiple_of(f * 128, 128), 128)


def on_ctx(index):
    return {"ctx": index}


def greet(peers):
    barrier = pltpu.get_barrier_semaphore()
    for peer in peers:
        pl.semaphore_signal(barrier, inc=1, device_id=peer, device_id_type=MESH)
    pl.semaphore_wait(barrier, len(peers))


class Links:
    def __init__(self, send, recv, peer, like=()):
        self.send, self.recv, self.peer = send, recv, peer
        self.like = {ref.shape: ref for ref in like}
        self.open = []

    def copy(self, i, src, dst, peer):
        return pltpu.make_async_remote_copy(
            src_ref=src, dst_ref=dst, send_sem=self.send.at[i], recv_sem=self.recv.at[i],
            device_id=peer, device_id_type=MESH,
        )

    def put(self, i, src, dst, peer):
        self.copy(i, src, dst, peer).start()
        self.open.append((i, self.like.get(src.shape, src)))

    def got(self, i, dst):
        self.copy(i, dst, dst, self.peer).wait_recv()

    def close(self):
        for i, ref in self.open:
            self.copy(i, ref, ref, self.peer).wait_send()
        self.open = []


def ctx_peers(p):
    return [on_ctx(p.other), on_ctx(p.same("P")), on_ctx(p.same("M")), on_ctx(p.same("X"))]


GATHER_COPIES = 19


def gather_ctx(p, links, base, own, out, rows):
    half = rows // 2
    top, bottom = pl.ds(0, half), pl.ds(half, half)
    to_p, to_m, to_x, to_k = (
        on_ctx(p.same("P")), on_ctx(p.same("M")), on_ctx(p.same("X")), on_ctx(p.other),
    )
    mine = out.at[p.c]

    def put(i, src, dst, peer):
        links.put(base + i, src, dst, peer)

    def got(i, dst):
        links.got(base + i, dst)

    def block(name):
        return out.at[p.same(name)]

    def cross(name):
        return out.at[p.cross(name)]

    put(0, own, mine, to_p)
    put(1, own, mine, to_m)
    put(2, own, mine, to_x)
    put(3, own, mine, to_k)
    yield [p.same("S")]
    got(0, block("M"))
    put(4, block("M").at[top], block("M").at[top], to_p)
    put(10, block("M"), block("M"), to_k)
    got(1, block("P"))
    put(5, block("P").at[bottom], block("P").at[bottom], to_m)
    put(11, block("P"), block("P"), to_k)
    got(2, block("X"))
    put(6, block("X"), block("X"), to_p)
    put(7, block("X"), block("X"), to_m)
    put(12, block("X"), block("X"), to_k)
    got(3, cross("S"))
    yield [p.same("M"), p.same("P"), p.same("X"), p.cross("S")]
    for i, part, to_core in ((4, top, 13), (5, bottom, 14)):
        piece = block("F").at[part]
        got(i, piece)
        put(4 + i, piece, piece, to_x)
        put(to_core, piece, piece, to_k)
    got(10, cross("M"))
    got(11, cross("P"))
    yield [p.same("F"), p.cross("M"), p.cross("P")]
    got(6, block("XM"))
    put(15, block("XM"), block("XM"), to_k)
    got(7, block("XP"))
    put(16, block("XP"), block("XP"), to_k)
    got(12, cross("X"))
    got(13, cross("F").at[top])
    got(14, cross("F").at[bottom])
    yield [p.same("XM"), p.same("XP"), p.cross("X"), p.cross("F")]
    for i, part, to_core in ((8, top, 17), (9, bottom, 18)):
        piece = block("XF").at[part]
        got(i, piece)
        put(to_core, piece, piece, to_k)
    got(15, cross("XM"))
    got(16, cross("XP"))
    yield [p.same("XF"), p.cross("XM"), p.cross("XP")]
    got(17, cross("XF").at[top])
    got(18, cross("XF").at[bottom])
    yield [p.cross("XF")]


def gather_fsdp(p, links, base, own, slot):
    links.put(base, own, slot(p.f), {"fsdp": p.twin})
    for d in (1, 3, 2):
        links.put(base + d, own, slot(p.f), {"fsdp": p.planes[d]})
    yield []
    twin = slot(p.twin)
    links.got(base, twin)
    for d in (1, 3, 2):
        links.put(base + 3 + d, twin, twin, {"fsdp": p.planes[d]})
    yield [p.twin]
    for d in (1, 3, 2):
        links.got(base + d, slot(p.planes[4 - d]))
    for d in (1, 3, 2):
        links.got(base + 3 + d, slot(p.twin_planes[4 - d]))
    yield [p.planes[d] for d in (3, 1, 2)] + [p.twin_planes[d] for d in (3, 1, 2)]


def scatter_fsdp(p, links, base, part, along, across, keep, total, rows):
    for n, d in enumerate((1, 3, 2)):
        links.put(base + n, part(p.planes[d]), along.at[n], {"fsdp": p.planes[d]})
        links.put(base + 3 + n, part(p.twin_planes[d]), along.at[3 + n], {"fsdp": p.planes[d]})
    yield
    for n in range(6):
        links.got(base + n, along.at[n])
    terms = [(along.at[3 + n], 0) for n in range(3)]
    add_rows(across.at[0], [(part(p.twin), 0)] + terms, rows)
    links.put(base + 6, across.at[0], across.at[1], {"fsdp": p.twin})
    add_rows(keep, [(part(p.f), 0)] + [(along.at[n], 0) for n in range(3)], rows)
    yield
    links.got(base + 6, across.at[1])
    add_rows(total, [(keep, 0), (across.at[1], 0)], rows)


def run_all(stages):
    live = list(stages)
    while live:
        left = []
        for stage in live:
            try:
                next(stage)
                left.append(stage)
            except StopIteration:
                pass
        live = left


SCATTER_COPIES = 16
SCATTER_ORDER = ("XF", "XP", "XM", "F", "X", "P", "M", "S")


def add_rows(dst, terms, rows, at=0):
    step = 16

    def one(i, _):
        r = pl.multiple_of(i * step, step)
        total = None
        for ref, off in terms:
            part = ref[pl.ds(r + off, step), :].astype(F32)
            total = part if total is None else total + part
        dst[pl.ds(r + at, step), :] = total.astype(dst.dtype)
        return 0

    lax.fori_loop(0, rows // step, one, 0)


def scatter_ctx(p, links, base, part, total, core_in, mid, far, rows):
    half = rows // 2
    to_p, to_m, to_x, to_k = (
        on_ctx(p.same("P")), on_ctx(p.same("M")), on_ctx(p.same("X")), on_ctx(p.other),
    )

    def put(i, src, dst, peer):
        links.put(base + i, src, dst, peer)

    def got(i, dst):
        links.got(base + i, dst)

    for i, name in enumerate(SCATTER_ORDER):
        put(i, part.at[p.cross(name)], core_in.at[i], to_k)
    yield

    def pair(i):
        got(i, core_in.at[i])
        return [(part.at[p.same(SCATTER_ORDER[i])], 0), (core_in.at[i], 0)]

    for i, peer in ((0, to_x), (1, to_p), (2, to_m)):
        add_rows(mid.at[i], pair(i), rows)
        put(8 + i, mid.at[i], far.at[i], peer)
    yield
    terms = pair(3)
    got(8, far.at[0])
    add_rows(mid.at[3], terms + [(far.at[0], 0)], rows)
    put(11, mid.at[3, pl.ds(0, half)], far.at[3, pl.ds(0, half)], to_p)
    put(12, mid.at[3, pl.ds(half, half)], far.at[3, pl.ds(half, half)], to_m)
    yield
    terms = pair(4)
    got(9, far.at[1])
    got(10, far.at[2])
    add_rows(mid.at[4], terms + [(far.at[1], 0), (far.at[2], 0)], rows)
    put(13, mid.at[4], far.at[4], to_x)
    yield
    terms = pair(5)
    got(11, far.at[3, pl.ds(0, half)])
    add_rows(mid.at[5], terms + [(far.at[3], 0)], half)
    add_rows(mid.at[5], [(r, half) for r, _ in terms], half, half)
    put(14, mid.at[5], far.at[5], to_p)
    terms = pair(6)
    got(12, far.at[3, pl.ds(half, half)])
    add_rows(mid.at[6], terms, half)
    add_rows(mid.at[6], [(r, half) for r, _ in terms] + [(far.at[3], half)], half, half)
    put(15, mid.at[6], far.at[6], to_m)
    yield
    terms = pair(7)
    got(13, far.at[4])
    got(14, far.at[5])
    got(15, far.at[6])
    add_rows(total, terms + [(far.at[4], 0), (far.at[5], 0), (far.at[6], 0)], rows)


def scatter_scratch(rows, cols):
    return [
        pltpu.VMEM((8, rows, cols), BF16),
        pltpu.VMEM((7, rows, cols), BF16),
        pltpu.VMEM((7, rows, cols), BF16),
    ]


def dma(n):
    return pltpu.SemaphoreType.DMA((n,))


def params(cid, mib=60):
    return pltpu.CompilerParams(
        collective_id=cid, has_side_effects=True, vmem_limit_bytes=mib * MIB
    )


Q_BLOCK = 256


def pick_rows(select, matrix):
    return nt(select.astype(BF16), matrix).astype(BF16)


def ones_at(rows, cols, shift, valid):
    row = lax.broadcasted_iota(jnp.int32, (rows, cols), 0)
    col = lax.broadcasted_iota(jnp.int32, (rows, cols), 1)
    return jnp.where((col == row + shift) & (row < valid), 1.0, 0.0)


def unit_of(row, c):
    shard = sum(((row >= 21 * n).astype(jnp.int32) for n in range(1, 8)), 0)
    place = row - 21 * shard
    inside = (row < 168) & ((place < 20) | (c < 8))
    return jnp.where(inside, 328 * shard + 16 * place + c, -1)


def iota(dims, axis):
    return lax.broadcasted_iota(jnp.int32, dims, axis)


def forward_kernel(
    h_ref, dy_ref, wqkv_ref, wout_ref, wgu_ref, wdown_ref, g1_ref, g2_ref, cos_ref, sin_ref,
    att_ref, dyall_ref, wq_ref, gu_ref, woutall_ref, downall_ref, n1_ref,
    qt_ref, kt_ref, vt_ref, qr_ref, kr_ref, vr_ref, ot_ref, lse_ref,
    hall, n1, qkv_win, gu_acc, qkv_cols, gu_cols, down_rows, ob, send, recv, local,
):
    p = Place()
    links = Links(
        send, recv, on_ctx(p.other),
        [hall.at[0], hall.at[0, pl.ds(0, 64)], qkv_cols, gu_cols, down_rows,
         ob.at[:, pl.ds(0, 128)]],
    )
    wins = [
        pltpu.make_async_copy(
            wqkv_ref.at[:, pl.ds(pl.multiple_of(part * 1024 + (p.c // 2) * 128, 128), 128)],
            qkv_win.at[part], local.at[part],
        )
        for part in range(3)
    ]
    own_h = pltpu.make_async_copy(h_ref, hall.at[p.c], local.at[5])
    for copy in wins:
        copy.start()
    own_h.start()
    for i in range(3):
        wins[i].wait()
        qkv_cols[pl.ds(64 * i, 64), :] = pick_rows(
            ones_at(64, 128, (p.c % 2) * 64, 64), qkv_win[i]
        )
    row = iota((16, 128), 0)
    gains = jnp.where(row == 0, g1_ref[...].astype(F32), 0.0)
    gains = jnp.where(row == 1, g2_ref[...].astype(F32), gains)
    qkv_cols[pl.ds(192, 16), :] = gains.astype(BF16)
    greet([on_ctx(p.ring[d]) for d in range(1, 16)] + p.fsdp_peers)
    gather_wq = gather_fsdp(p, links, 38, qkv_cols, lambda f: wq_ref.at[:, lanes_of(f)])
    next(gather_wq)
    gather_h = gather_ctx(p, links, 0, h_ref, hall, 128)
    ready = next(gather_h)
    lanes = lanes_of(p.f)
    wq_ref[:, lanes] = qkv_cols[...]
    for half in range(2):
        want = unit_of(iota((176, 1), 0), p.c)
        want = jnp.where(want < 0, -1, want + 64 * half)
        gu_acc[...] = jnp.zeros_like(gu_acc)

        def pick(i, _):
            cols = pl.ds(pl.multiple_of(2560 * half + i * 896, 128), 896)
            select = jnp.where(iota((176, 896), 1) + i * 896 == want, 1.0, 0.0)
            gu_acc[...] += nt(select.astype(BF16), wgu_ref[:, cols])
            return 0

        lax.fori_loop(0, 3, pick, 0)
        gu_cols[pl.ds(176 * half, 176), :] = gu_acc[...].astype(BF16)
    place = iota((32, 328), 0)
    select = (iota((32, 328), 1) == 16 * place + p.c) & (place < 21)
    down_rows[...] = nn(jnp.where(select, 1.0, 0.0).astype(BF16), wdown_ref[...]).astype(BF16)
    own_h.wait()
    next(gather_wq)
    ready += next(gather_h)
    next(gather_wq)
    saves = []

    def project(b):
        gain = wq_ref[pl.ds(192, 1), :].astype(F32)

        def norm(i, _):
            r = pl.ds(pl.multiple_of(i * 32, 32), 32)
            xhat, _unused = normalize(hall[b, r, :].astype(F32))
            n1[b, r, :] = (xhat * gain).astype(BF16)
            return 0

        lax.fori_loop(0, 4, norm, 0)
        proj = nt(wq_ref[pl.ds(0, 192), :], n1[b])
        at = pl.ds(pl.multiple_of(b * 128, 128), 128)
        cos, sin = cos_ref[:, at], sin_ref[:, at]
        q = rope_t(proj[:64], cos, sin).astype(BF16) * jnp.asarray(0.125, BF16)
        k = rope_t(proj[64:128], cos, sin).astype(BF16)
        v = proj[128:192].astype(BF16)
        qt_ref[:, at] = q
        kt_ref[:, at] = k
        vt_ref[:, at] = v
        qr_ref[at, :] = q.astype(F32).T.astype(BF16)
        kr_ref[at, :] = k.astype(F32).T.astype(BF16)
        vr_ref[at, :] = v.astype(F32).T.astype(BF16)
        copy = pltpu.make_async_copy(n1.at[b], n1_ref.at[b], local.at[10 + len(saves)])
        copy.start()
        saves.append(copy)

    for b in ready:
        project(b)
    for b in next(gather_h):
        project(b)
    for b in next(gather_h):
        project(b)
    gather_gu = gather_fsdp(p, links, 45, gu_cols, lambda f: gu_ref.at[:, lanes_of(f)])
    next(gather_gu)
    def down_slot(f):
        return downall_ref.at[pl.ds(pl.multiple_of(f * 32, 32), 32)]

    gather_down = gather_fsdp(p, links, 83, down_rows, down_slot)
    next(gather_down)
    locals_ = [
        pltpu.make_async_copy(dy_ref, dyall_ref.at[p.c], local.at[6]),
        pltpu.make_async_copy(gu_cols, gu_ref.at[:, lanes], local.at[7]),
        pltpu.make_async_copy(
            wout_ref, woutall_ref.at[pl.ds(pl.multiple_of(p.f * 128, 128), 128)], local.at[8]
        ),
        pltpu.make_async_copy(down_rows, down_slot(p.f), local.at[3]),
    ]
    for copy in locals_:
        copy.start()
    half = pl.ds(pl.multiple_of(p.k * 64, 64), 64)

    def out_half(f, k):
        return woutall_ref.at[pl.ds(pl.multiple_of(f * 128 + k * 64, 64), 64)]

    gather_out = gather_fsdp(p, links, 53, wout_ref.at[half], lambda f: out_half(f, p.k))
    next(gather_out)
    while ready is not None:
        ready = next(gather_h, None)
        for b in ready or ():
            project(b)
    next(gather_gu)
    next(gather_down)
    twins = next(gather_out)
    gather_dy = gather_ctx(p, links, 19, dy_ref, dyall_ref, 128)
    next(gather_dy)
    stages = 6

    def attend(i, _):
        j = (p.c // 2 + i) % 8
        at = pl.ds(pl.multiple_of(j * Q_BLOCK, Q_BLOCK), Q_BLOCK)
        scores = nn(kr_ref[...], qt_ref[:, at])
        top = jnp.max(scores, axis=0, keepdims=True)
        weights = jnp.exp(scores - top)
        total = jnp.sum(weights, axis=0, keepdims=True)
        mixed = nn(vt_ref[...], weights.astype(BF16)) / total
        ot_ref[:, at] = mixed
        lse_ref[:, at] = top + jnp.log(total)
        ob[:, at] = mixed.astype(BF16)

        @pl.when(i > 0)
        def _():
            for e in range(2):
                to = 2 * j + e
                piece = ob.at[:, pl.ds(pl.multiple_of(to * 128, 128), 128)]
                links.copy(67 + 2 * i + e - p.k, piece, att_ref.at[p.c], on_ctx(to)).start()

        @pl.when(i == 0)
        def _():
            piece = ob.at[:, pl.ds(pl.multiple_of(p.c * 128, 128), 128)]
            copy = pltpu.make_async_copy(piece, att_ref.at[p.c], local.at[9])
            copy.start()
            copy.wait()
            piece = ob.at[:, pl.ds(pl.multiple_of(p.other * 128, 128), 128)]
            links.copy(67 + (p.other - p.c + 16) % 16, piece, att_ref.at[p.c], on_ctx(p.other)).start()

        for s in range(stages):

            @pl.when(i == s + 2)
            def _():
                next(gather_dy, None)

        return 0

    lax.fori_loop(0, 8, attend, 0)
    for _ in gather_dy:
        pass
    next(gather_gu)
    next(gather_down)
    others = twins + next(gather_out)
    for i, f in enumerate(others):
        links.put(60 + i, out_half(f, p.k), out_half(f, p.k), on_ctx(p.other))
    for d in range(1, 16):
        links.got(67 + d, att_ref.at[p.ring[16 - d]])
        links.open.append((67 + d, ob.at[:, pl.ds(0, 128)]))
    for i, f in enumerate(others):
        links.got(60 + i, out_half(f, 1 - p.k))

    for copy in locals_ + saves:
        copy.wait()
    links.close()


def shape(dims, dtype=BF16):
    return jax.ShapeDtypeStruct(dims, dtype)


def forward(hidden, grad, wqkv, wout, wgu, wdown, g1, g2, cos, sin):
    return pl.pallas_call(
        forward_kernel,
        name="forward",
        out_shape=(
            shape((16, 64, 128)), shape((16, 128, 1024)), shape((208, 1024)), shape((352, 1024)),
            shape((1024, 1024)), shape((256, 1024)), shape((16, 128, 1024)),
            shape((64, 2048)), shape((64, 2048)), shape((64, 2048)),
            shape((2048, 64)), shape((2048, 64)), shape((2048, 64)),
            shape((64, 2048), F32), shape((1, 2048), F32),
        ),
        in_specs=[VMEM, VMEM, ANY] + [VMEM] * 7,
        out_specs=(ANY, ANY, VMEM, ANY, ANY, ANY, ANY) + (VMEM,) * 8,
        scratch_shapes=[
            pltpu.VMEM((16, 128, 1024), BF16),
            pltpu.VMEM((16, 128, 1024), BF16),
            pltpu.VMEM((3, 128, 128), BF16),
            pltpu.VMEM((176, 128), F32),
            pltpu.VMEM((208, 128), BF16),
            pltpu.VMEM((352, 128), BF16),
            pltpu.VMEM((32, 1024), BF16),
            pltpu.VMEM((64, 2048), BF16),
            dma(90), dma(90), dma(26),
        ],
        compiler_params=params(1, 56),
    )(hidden, grad, wqkv, wout, wgu, wdown, g1, g2, cos, sin)


def middle_kernel(
    h_ref, att_ref, wout_ref, wq_ref, gu_ref, downall_ref, dy_ref, dyall_ref,
    h1_ref, dh1_ref, dot_ref, downpart_ref, ggu_ref, gdown_ref, ggain_ref, gout_ref,
    nall, dyall, act, dgu, down_w, part, downpart, total, core_in, mid, far, dat,
    send, recv, local,
):
    p = Place()
    links = Links(send, recv, on_ctx(p.other))
    load = pltpu.make_async_copy(dyall_ref, dyall, local.at[0])
    load.start()
    peers = [on_ctx(p.ring[d]) for d in range(1, 16)]
    greet(peers)
    gain = wq_ref[pl.ds(193, 1), :].astype(F32)
    att = att_ref[...].reshape(1024, 128)
    h1 = h_ref[...].astype(F32) + tn(att, wout_ref[...])
    h1_ref[...] = h1
    xhat, _unused = normalize(h1)
    nall[p.c] = (xhat * gain).astype(BF16)
    gather = gather_ctx(p, links, 0, nall.at[p.c], nall, 128)
    ready = next(gather)
    pick = iota((176, 256), 1)
    row = iota((176, 1), 0)
    shard = sum(((row >= 21 * n).astype(jnp.int32) for n in range(1, 8)), 0)
    want = jnp.where(row < 168, row + 11 * shard, -1)
    down_w[...] = nn(jnp.where(pick == want, 1.0, 0.0).astype(BF16), downall_ref[...]).astype(BF16)
    load.wait()

    def feed(b):
        n2 = nall[b]
        gu = nt(gu_ref[...], n2)
        d_act = nt(down_w[...], dyall[b])
        gate, up = gu[:176], gu[176:]
        cdf = 0.5 * (1.0 + lax.erf(gate * 2.0 ** (-0.5)))
        gelu = gate * cdf
        pdf = jnp.exp(-0.5 * gate * gate) * (2.0 * np.pi) ** (-0.5)
        d_gate = d_act * up * (cdf + gate * pdf)
        d_gu = jnp.concatenate([d_gate, d_act * gelu], axis=0).astype(BF16)
        at = pl.ds(pl.multiple_of(b * 128, 128), 128)
        act[:, at] = (gelu * up).astype(BF16)
        dgu[:, at] = d_gu
        part[b] = tn(d_gu, gu_ref[...]).astype(BF16)

    while ready is not None:
        for b in ready:
            feed(b)
        ready = next(gather, None)
    scatter = scatter_ctx(p, links, 19, part, total, core_in, mid, far, 128)
    next(scatter)
    next(scatter)
    ggain = []
    for half in range(2):
        cols = pl.ds(512 * half, 512)
        g = nn(dgu[...], nall[:, :, cols].reshape(2048, 512))
        ggu_ref[:, cols] = g.astype(BF16)
        ggain.append(jnp.sum(g * gu_ref[:, cols].astype(F32), axis=0, keepdims=True))
    ggain_ref[...] = jnp.concatenate(ggain, axis=1) / gain
    next(scatter)
    row = iota((256, 1), 0)
    shard = row // 32
    place = row - 32 * shard
    want = jnp.where(place < 21, 21 * shard + place, -1)
    spread = jnp.where(iota((256, 176), 1) == want, 1.0, 0.0).astype(BF16)
    for half in range(2):
        cols = pl.ds(512 * half, 512)
        g = nn(act[...], dyall[:, :, cols].reshape(2048, 512)).astype(BF16)
        gdown_ref[:, cols] = nn(spread, g).astype(BF16)
    next(scatter)

    def down(b, _):
        at = pl.ds(pl.multiple_of(b * 128, 128), 128)
        downpart[b] = tn(act[:, at], down_w[...]).astype(BF16)
        return 0

    next(scatter)
    lax.fori_loop(0, 16, down, 0)
    store = pltpu.make_async_copy(downpart, downpart_ref, local.at[1])
    store.start()
    next(scatter, None)
    h1 = h1_ref[...]
    xhat, inv = normalize(h1)
    d_h1 = dy_ref[...].astype(F32) + norm_back(total[...], xhat, inv, gain)
    dh1_ref[...] = d_h1
    d_h1_b = d_h1.astype(BF16)
    dat[...] = nt(wout_ref[...], d_h1_b).astype(BF16).reshape(16, 64, 128)
    lanes = pl.ds(pl.multiple_of(p.c * 128, 128), 128)
    for d in range(1, 16):
        links.put(34 + d, dat.at[p.ring[d]], dot_ref.at[:, lanes], peers[d - 1])
    dot_ref[:, lanes] = dat[p.c]
    att = att_ref[...]
    for g in range(4):
        rows = att[4 * g : 4 * g + 4].reshape(256, 128)
        block = nn(rows, d_h1_b).reshape(2, 16, 8, 1024).transpose(1, 0, 2, 3)
        gout_ref[:, pl.ds(16 * g, 16), :] = block.reshape(16, 16, 1024).astype(BF16)
    for d in range(1, 16):
        links.got(34 + d, dot_ref.at[:, pl.ds(pl.multiple_of(p.ring[16 - d] * 128, 128), 128)])
    store.wait()
    links.close()


def middle(hidden, att, w_out, w_q, w_gu, down_all, grad, dy_all):
    return pl.pallas_call(
        middle_kernel,
        name="middle",
        out_shape=(
            shape((128, 1024), F32), shape((128, 1024), F32), shape((64, 2048)),
            shape((16, 128, 1024)), shape((352, 1024)), shape((256, 1024)),
            shape((1, 1024), F32), shape((16, 64, 1024)),
        ),
        in_specs=[VMEM] * 7 + [ANY],
        out_specs=(VMEM,) * 3 + (ANY,) + (VMEM,) * 4,
        scratch_shapes=[
            pltpu.VMEM((16, 128, 1024), BF16),
            pltpu.VMEM((16, 128, 1024), BF16),
            pltpu.VMEM((176, 2048), BF16),
            pltpu.VMEM((352, 2048), BF16),
            pltpu.VMEM((176, 1024), BF16),
            pltpu.VMEM((16, 128, 1024), BF16),
            pltpu.VMEM((16, 128, 1024), BF16),
            pltpu.VMEM((128, 1024), F32),
        ] + scatter_scratch(128, 1024) + [
            pltpu.VMEM((16, 64, 128), BF16),
            dma(50), dma(50), dma(2),
        ],
        compiler_params=params(2),
    )(hidden, att, w_out, w_q, w_gu, down_all, grad, dy_all)


LATE = 224


def backward_kernel(
    k_ref, v_ref, kt_ref, qt_ref, q_ref, dot_ref, ot_ref, lse_ref, cos_ref, sin_ref,
    n1_ref, wq_ref, h_ref, h1_ref, dh1_ref, downpart_ref, ggu_ref, gdown_ref, ggain_ref, gout_ref,
    result_ref, dinput_ref, gupieces_ref, rowpieces_ref, latepieces_ref,
    n1, downpart, dproj, dk, dv, part, late, rows_in,
    total, gout, gu_sum, row_sum, late_sum, *rest,
):
    (
        core_a, mid_a, far_a, core_b, mid_b, far_b, core_c, mid_c, far_c,
        gu_along, gu_across, gu_keep, row_along, row_across, row_keep,
        late_along, late_across, late_keep, send, recv, local,
    ) = rest
    p = Place()
    links = Links(
        send, recv, on_ctx(p.other),
        [part.at[0], part.at[0, pl.ds(0, 64)], part.at[0, pl.ds(0, 32)], gu_keep,
         gu_keep.at[pl.ds(0, 176)], late_keep, late_keep.at[pl.ds(0, LATE // 2)]],
    )
    loads = [
        pltpu.make_async_copy(downpart_ref, downpart, local.at[0]),
        pltpu.make_async_copy(n1_ref, n1, local.at[1]),
    ]
    for copy in loads:
        copy.start()
    greet(ctx_peers(p) + p.fsdp_peers)
    loads[0].wait()
    down = scatter_ctx(p, links, 0, downpart, total.at[0], core_a, mid_a, far_a, 128)
    next(down)
    sum_gu = scatter_fsdp(
        p, links, 48, lambda f: ggu_ref.at[:, lanes_of(f)], gu_along, gu_across, gu_keep, gu_sum, 352
    )
    next(sum_gu)
    sum_out = scatter_ctx(p, links, 16, gout_ref, gout, core_b, mid_b, far_b, 64)
    all_gu = gather_ctx(p, links, 69, gu_sum, gupieces_ref, 352)
    mine = [
        pltpu.make_async_copy(gu_sum, gupieces_ref.at[p.c], local.at[2]),
        pltpu.make_async_copy(row_sum, rowpieces_ref.at[p.c], local.at[3]),
        pltpu.make_async_copy(late_sum, latepieces_ref.at[p.c], local.at[4]),
    ]

    def begin_gu():
        next(sum_gu, None)
        next(all_gu)

    def step(stages):
        return lambda: next(stages, None)

    plan = {
        1: [step(down)], 2: [step(sum_out)], 3: [step(sum_gu)], 4: [step(down)],
        5: [step(down), begin_gu], 6: [step(down)], 7: [step(sum_out), step(all_gu)],
    }
    dk[...] = jnp.zeros_like(dk)
    dv[...] = jnp.zeros_like(dv)

    def attend(i, _):
        at = pl.ds(pl.multiple_of(i * Q_BLOCK, Q_BLOCK), Q_BLOCK)
        scores = nn(k_ref[...], qt_ref[:, at])
        prob = jnp.exp(scores - lse_ref[:, at])
        dout = dot_ref[:, at]
        d_prob = nn(v_ref[...], dout)
        delta = jnp.sum(dout.astype(F32) * ot_ref[:, at], axis=0, keepdims=True)
        d_scores = (prob * (d_prob - delta)).astype(BF16)
        d_query = nn(kt_ref[...], d_scores) * 0.125
        dproj[pl.ds(0, 64), at] = unrope_t(d_query, cos_ref[:, at], sin_ref[:, at]).astype(BF16)
        dk[...] += nn(d_scores, q_ref[at, :])
        dv[...] += nn(prob.astype(BF16), dout.astype(F32).T.astype(BF16))
        for n, steps in plan.items():

            @pl.when(i == n)
            def _():
                for run in steps:
                    run()

        return 0

    lax.fori_loop(0, 8, attend, 0)

    def project(b, _):
        at = pl.ds(pl.multiple_of(b * 128, 128), 128)
        d_key = unrope_t(dk[at, :].T, cos_ref[:, at], sin_ref[:, at])
        dproj[pl.ds(64, 64), at] = d_key.astype(BF16)
        dproj[pl.ds(128, 64), at] = dv[at, :].T.astype(BF16)
        part[b] = tn(dproj[:, at], wq_ref[pl.ds(0, 192), :]).astype(BF16)
        return 0

    lax.fori_loop(0, 16, project, 0)
    back = scatter_ctx(p, links, 32, part, total.at[1], core_c, mid_c, far_c, 128)
    next(back)
    next(back)
    next(down, None)
    result_ref[...] = (h1_ref[...] + total[0]).astype(BF16)
    loads[1].wait()
    gain = wq_ref[pl.ds(192, 1), :].astype(F32)
    late[...] = jnp.zeros_like(late)
    ggain = []
    for half in range(2):
        cols = pl.ds(512 * half, 512)
        g = nn(dproj[...], n1[:, :, cols].reshape(2048, 512))
        late[pl.ds(0, 192), cols] = g.astype(BF16)
        ggain.append(jnp.sum(g * wq_ref[pl.ds(0, 192), cols].astype(F32), axis=0, keepdims=True))
    gain_row = jnp.concatenate(ggain, axis=1) / gain
    row = iota((16, 1024), 0)
    gains = jnp.where(row == 0, gain_row, 0.0)
    late[pl.ds(192, 16), :] = jnp.where(row == 1, ggain_ref[...], gains).astype(BF16)
    sum_late = scatter_fsdp(
        p, links, 62, lambda f: late.at[:, lanes_of(f)],
        late_along, late_across, late_keep, late_sum, LATE,
    )
    next(sum_late)
    next(back)
    next(sum_out, None)
    next(all_gu, None)
    next(back)
    for _ in sum_out:
        pass
    for f in range(8):
        rows_in[f, pl.ds(0, 16), :] = gdown_ref[pl.ds(32 * f, 16), :]
        tail = gdown_ref[pl.ds(32 * f + 16, 16), :].astype(F32)[:8]
        outs = gout[pl.ds(8 * f, 8), :]
        rows_in[f, pl.ds(16, 16), :] = jnp.concatenate([tail, outs], axis=0).astype(BF16)
    sum_rows = scatter_fsdp(
        p, links, 55, lambda f: rows_in.at[f], row_along, row_across, row_keep, row_sum, 32
    )
    next(sum_rows)
    next(back)
    next(sum_late)
    next(all_gu, None)
    next(back, None)
    xhat, inv = normalize(h_ref[...].astype(F32))
    d_in = norm_back(total[1], xhat, inv, gain)
    dinput_ref[...] = (dh1_ref[...] + d_in).astype(BF16)
    next(sum_late, None)
    all_late = gather_ctx(p, links, 107, late_sum, latepieces_ref, LATE)
    next(all_late)
    next(sum_rows)
    next(sum_rows, None)
    all_rows = gather_ctx(p, links, 88, row_sum, rowpieces_ref, 32)
    next(all_rows)
    for copy in mine:
        copy.start()
    run_all([all_gu, all_late, all_rows])
    for copy in mine:
        copy.wait()
    links.close()


def backward(*args):
    return pl.pallas_call(
        backward_kernel,
        name="backward",
        out_shape=(
            shape((128, 1024)), shape((128, 1024)), shape((16, 352, 128)),
            shape((16, 32, 1024)), shape((16, LATE, 128)),
        ),
        in_specs=[VMEM] * 10 + [ANY] + [VMEM] * 4 + [ANY] + [VMEM] * 4,
        out_specs=(VMEM, VMEM, ANY, ANY, ANY),
        scratch_shapes=[
            pltpu.VMEM((16, 128, 1024), BF16),
            pltpu.VMEM((16, 128, 1024), BF16),
            pltpu.VMEM((192, 2048), BF16),
            pltpu.VMEM((2048, 64), F32),
            pltpu.VMEM((2048, 64), F32),
            pltpu.VMEM((16, 128, 1024), BF16),
            pltpu.VMEM((LATE, 1024), BF16),
            pltpu.VMEM((8, 32, 1024), BF16),
            pltpu.VMEM((2, 128, 1024), F32),
            pltpu.VMEM((64, 1024), F32),
            pltpu.VMEM((352, 128), BF16),
            pltpu.VMEM((32, 1024), BF16),
            pltpu.VMEM((LATE, 128), BF16),
        ] + scatter_scratch(128, 1024) + scatter_scratch(64, 1024) + scatter_scratch(128, 1024)
        + fsdp_scratch(352, 128) + fsdp_scratch(32, 1024) + fsdp_scratch(LATE, 128)
        + [dma(126), dma(126), dma(5)],
        compiler_params=params(3),
    )(*args)


def fsdp_scratch(rows, cols):
    return [
        pltpu.VMEM((6, rows, cols), BF16),
        pltpu.VMEM((2, rows, cols), BF16),
        pltpu.VMEM((rows, cols), BF16),
    ]


def nt(a, b):
    return lax.dot_general(a, b, (((1,), (1,)), ((), ())), preferred_element_type=F32)


def tn(a, b):
    return lax.dot_general(a, b, (((0,), (0,)), ((), ())), preferred_element_type=F32)


def nn(a, b):
    return jnp.dot(a, b, preferred_element_type=F32)


def normalize(v):
    centered = v - jnp.mean(v, axis=-1, keepdims=True)
    inv = lax.rsqrt(jnp.mean(centered * centered, axis=-1, keepdims=True) + EPSILON)
    return centered * inv, inv


def norm_back(e, xhat, inv, gain):
    eg = e * gain
    return inv * (
        eg - jnp.mean(eg, axis=-1, keepdims=True)
        - xhat * jnp.mean(eg * xhat, axis=-1, keepdims=True)
    )


def rope_t(v, cos, sin):
    a, b = v[:32], v[32:]
    return jnp.concatenate([a * cos - b * sin, b * cos + a * sin], axis=0)


def unrope_t(v, cos, sin):
    a, b = v[:32], v[32:]
    return jnp.concatenate([a * cos + b * sin, b * cos - a * sin], axis=0)


def rope_tables():
    inverse = np.float32(ROPE_BASE) ** (-(np.arange(32, dtype=np.float32) * 2.0) / 64)
    angles = inverse[:, None].astype(np.float32) * np.arange(2048, dtype=np.float32)[None, :]
    return np.cos(angles).astype(np.float32), np.sin(angles).astype(np.float32)


def body(
    hidden_in, qkv_weight, out_weight, gate_up_weight, down_weight, attn_gain, mlp_gain, out_grad
):
    hidden_b, grad_b = hidden_in[0], out_grad[0]
    cos, sin = rope_tables()
    cos, sin = jnp.asarray(cos), jnp.asarray(sin)
    (
        att_t, dy_all, w_q, w_gu, w_out, down_all, n1, q_t, k_t, v_t, queries, keys, values, o_t, lse
    ) = forward(
        hidden_b, grad_b, qkv_weight, out_weight, gate_up_weight, down_weight,
        attn_gain[None], mlp_gain[None], cos, sin,
    )
    h1, d_h1, do_t, down_part, g_gu, g_down, g_gain_two, g_out = middle(
        hidden_b, att_t, w_out, w_q, w_gu, down_all, grad_b, dy_all
    )
    result, input_grad, gu_pieces, row_pieces, late_pieces = backward(
        keys, values, k_t, q_t, queries, do_t, o_t, lse, cos, sin,
        n1, w_q, hidden_b, h1, d_h1, down_part, g_gu, g_down, g_gain_two, g_out,
    )
    late_pieces = late_pieces.astype(F32)
    qkv_grad = (
        late_pieces[:, :192].reshape(16, 3, 64, 128).transpose(3, 1, 0, 2).reshape(128, 3072)
    )
    gain_grads = jnp.sum(late_pieces[:, 192:194], axis=0)
    gate_up = gu_pieces.reshape(16, 2, 176, 128)[:, :, :168].transpose(1, 2, 0, 3)
    gate_up = gate_up.reshape(2, 8, 336, 128)[:, :, :328].reshape(5248, 128)
    gate_up_grad = gate_up.astype(F32).T
    down_grad = (
        row_pieces[:, :21].transpose(1, 0, 2).reshape(336, 1024)[:328].astype(F32)
    )
    out_weight_grad = row_pieces[:, 24:].reshape(128, 1024).astype(F32)
    return (
        result[None], input_grad[None], qkv_grad, out_weight_grad, gate_up_grad, down_grad,
        gain_grads[0], gain_grads[1],
    )


def solution(mesh):
    return jax.shard_map(
        body,
        mesh=mesh,
        in_specs=(
            P("fsdp", "ctx", None), P("fsdp", None), P("fsdp", None), P("fsdp", None),
            P("fsdp", None), P("fsdp"), P("fsdp"), P("fsdp", "ctx", None),
        ),
        out_specs=(
            P("fsdp", "ctx", None), P("fsdp", "ctx", None), P("fsdp", None), P("fsdp", None),
            P("fsdp", None), P("fsdp", None), P("fsdp"), P("fsdp"),
        ),
        check_vma=False,
    )
```

```python
import jax
import jax.numpy as jnp
import numpy as np
from jax import lax
from jax.experimental import pallas as pl
from jax.experimental.pallas import tpu as pltpu
from jax.sharding import PartitionSpec as P

HEADS = 16
EPSILON = 1e-05
ROPE_BASE = 160000.0
F32 = jnp.float32
BF16 = jnp.bfloat16
MESH = pl.DeviceIdType.MESH
ANY = pl.BlockSpec(memory_space=pl.ANY)
VMEM = pl.BlockSpec(memory_space=pltpu.VMEM)
MIB = 1024 * 1024


class Place:
    def __init__(self):
        c = lax.axis_index("ctx")
        self.c = c
        self.f = lax.axis_index("fsdp")
        k = c % 2
        y = (c // 2) % 4
        xl = c // 8
        self.k = k

        def at(x, row):
            return x * 4 + row % 4

        ox = 1 - xl
        self.other = c + 1 - 2 * k
        self.chip = {
            "S": at(xl, y),
            "P": at(xl, y + 1),
            "M": at(xl, y + 3),
            "F": at(xl, y + 2),
            "X": at(ox, y),
            "XP": at(ox, y + 1),
            "XM": at(ox, y + 3),
            "XF": at(ox, y + 2),
        }

        self.same_core = {name: chip * 2 + k for name, chip in self.chip.items()}
        self.cross_core = {name: chip * 2 + 1 - k for name, chip in self.chip.items()}
        self.ring = [(c + d) % 16 for d in range(16)]
        z, xh = self.f // 2, self.f % 2
        self.twin = z * 2 + 1 - xh
        self.planes = [(z + d) % 4 * 2 + xh for d in range(4)]
        self.twin_planes = [(z + d) % 4 * 2 + 1 - xh for d in range(4)]
        self.fsdp_peers = [{"fsdp": i} for i in [self.twin] + self.planes[1:]]

    def same(self, name):
        return self.same_core[name]

    def cross(self, name):
        return self.cross_core[name]


def lanes_of(f):
    return pl.ds(pl.multiple_of(f * 128, 128), 128)


def on_ctx(index):
    return {"ctx": index}


def greet(peers):
    barrier = pltpu.get_barrier_semaphore()
    for peer in peers:
        pl.semaphore_signal(barrier, inc=1, device_id=peer, device_id_type=MESH)
    pl.semaphore_wait(barrier, len(peers))


class Links:
    def __init__(self, send, recv, peer, like=()):
        self.send, self.recv, self.peer = send, recv, peer
        self.like = {ref.shape: ref for ref in like}
        self.open = []

    def copy(self, i, src, dst, peer):
        return pltpu.make_async_remote_copy(
            src_ref=src, dst_ref=dst, send_sem=self.send.at[i], recv_sem=self.recv.at[i],
            device_id=peer, device_id_type=MESH,
        )

    def put(self, i, src, dst, peer):
        self.copy(i, src, dst, peer).start()
        self.open.append((i, self.like.get(src.shape, src)))

    def got(self, i, dst):
        self.copy(i, dst, dst, self.peer).wait_recv()

    def close(self, below=1000):
        for i, ref in self.open:
            if i < below:
                self.copy(i, ref, ref, self.peer).wait_send()
        self.open = [(i, ref) for i, ref in self.open if i >= below]


def ctx_peers(p):
    return [on_ctx(p.other), on_ctx(p.same("P")), on_ctx(p.same("M")), on_ctx(p.same("X"))]


GATHER_COPIES = 19


def gather_ctx(p, links, base, own, out, rows):
    half = rows // 2
    top, bottom = pl.ds(0, half), pl.ds(half, half)
    to_p, to_m, to_x, to_k = (
        on_ctx(p.same("P")), on_ctx(p.same("M")), on_ctx(p.same("X")), on_ctx(p.other),
    )
    mine = out.at[p.c]

    def put(i, src, dst, peer):
        links.put(base + i, src, dst, peer)

    def got(i, dst):
        links.got(base + i, dst)

    def block(name):
        return out.at[p.same(name)]

    def cross(name):
        return out.at[p.cross(name)]

    put(0, own, mine, to_p)
    put(1, own, mine, to_m)
    put(2, own, mine, to_x)
    put(3, own, mine, to_k)
    yield [p.same("S")]
    got(0, block("M"))
    put(4, block("M").at[top], block("M").at[top], to_p)
    put(10, block("M"), block("M"), to_k)
    got(1, block("P"))
    put(5, block("P").at[bottom], block("P").at[bottom], to_m)
    put(11, block("P"), block("P"), to_k)
    got(2, block("X"))
    put(6, block("X"), block("X"), to_p)
    put(7, block("X"), block("X"), to_m)
    put(12, block("X"), block("X"), to_k)
    got(3, cross("S"))
    yield [p.same("M"), p.same("P"), p.same("X"), p.cross("S")]
    for i, part, to_core in ((4, top, 13), (5, bottom, 14)):
        piece = block("F").at[part]
        got(i, piece)
        put(4 + i, piece, piece, to_x)
        put(to_core, piece, piece, to_k)
    got(10, cross("M"))
    got(11, cross("P"))
    yield [p.same("F"), p.cross("M"), p.cross("P")]
    got(6, block("XM"))
    put(15, block("XM"), block("XM"), to_k)
    got(7, block("XP"))
    put(16, block("XP"), block("XP"), to_k)
    got(12, cross("X"))
    got(13, cross("F").at[top])
    got(14, cross("F").at[bottom])
    yield [p.same("XM"), p.same("XP"), p.cross("X"), p.cross("F")]
    for i, part, to_core in ((8, top, 17), (9, bottom, 18)):
        piece = block("XF").at[part]
        got(i, piece)
        put(to_core, piece, piece, to_k)
    got(15, cross("XM"))
    got(16, cross("XP"))
    yield [p.same("XF"), p.cross("XM"), p.cross("XP")]
    got(17, cross("XF").at[top])
    got(18, cross("XF").at[bottom])
    yield [p.cross("XF")]


def gather_fsdp(p, links, base, own, slot):
    links.put(base, own, slot(p.f), {"fsdp": p.twin})
    for d in (1, 3, 2):
        links.put(base + d, own, slot(p.f), {"fsdp": p.planes[d]})
    yield []
    twin = slot(p.twin)
    links.got(base, twin)
    for d in (1, 3, 2):
        links.put(base + 3 + d, twin, twin, {"fsdp": p.planes[d]})
    yield [p.twin]
    for d in (1, 3, 2):
        links.got(base + d, slot(p.planes[4 - d]))
    for d in (1, 3, 2):
        links.got(base + 3 + d, slot(p.twin_planes[4 - d]))
    yield [p.planes[d] for d in (3, 1, 2)] + [p.twin_planes[d] for d in (3, 1, 2)]


def scatter_fsdp(p, links, base, part, along, across, keep, total, rows):
    for n, d in enumerate((1, 3, 2)):
        links.put(base + n, part(p.planes[d]), along.at[n], {"fsdp": p.planes[d]})
        links.put(base + 3 + n, part(p.twin_planes[d]), along.at[3 + n], {"fsdp": p.planes[d]})
    yield
    for n in range(6):
        links.got(base + n, along.at[n])
    terms = [(along.at[3 + n], 0) for n in range(3)]
    add_rows(across.at[0], [(part(p.twin), 0)] + terms, rows)
    links.put(base + 6, across.at[0], across.at[1], {"fsdp": p.twin})
    add_rows(keep, [(part(p.f), 0)] + [(along.at[n], 0) for n in range(3)], rows)
    yield
    links.got(base + 6, across.at[1])
    add_rows(total, [(keep, 0), (across.at[1], 0)], rows)


def run_all(stages):
    live = list(stages)
    while live:
        left = []
        for stage in live:
            try:
                next(stage)
                left.append(stage)
            except StopIteration:
                pass
        live = left


SCATTER_COPIES = 16
SCATTER_ORDER = ("XF", "XP", "XM", "F", "X", "P", "M", "S")


def add_rows(dst, terms, rows, at=0):
    step = 16

    def one(i, _):
        r = pl.multiple_of(i * step, step)
        total = None
        for ref, off in terms:
            part = ref[pl.ds(r + off, step), :].astype(F32)
            total = part if total is None else total + part
        dst[pl.ds(r + at, step), :] = total.astype(dst.dtype)
        return 0

    lax.fori_loop(0, rows // step, one, 0)


def scatter_ctx(p, links, base, part, total, core_in, far, rows):
    half = rows // 2
    to_p, to_m, to_x, to_k = (
        on_ctx(p.same("P")), on_ctx(p.same("M")), on_ctx(p.same("X")), on_ctx(p.other),
    )

    def put(i, src, dst, peer):
        links.put(base + i, src, dst, peer)

    def got(i, dst):
        links.got(base + i, dst)

    mid = [part.at[p.same(name)] for name in SCATTER_ORDER]
    for i, name in enumerate(SCATTER_ORDER):
        put(i, part.at[p.cross(name)], core_in.at[i], to_k)
    yield

    def pair(i):
        got(i, core_in.at[i])
        return [(mid[i], 0), (core_in.at[i], 0)]

    for i, peer in ((0, to_x), (1, to_p), (2, to_m)):
        add_rows(mid[i], pair(i), rows)
        put(8 + i, mid[i], far.at[i], peer)
    yield
    terms = pair(3)
    got(8, far.at[0])
    add_rows(mid[3], terms + [(far.at[0], 0)], rows)
    put(11, mid[3].at[pl.ds(0, half)], far.at[3, pl.ds(0, half)], to_p)
    put(12, mid[3].at[pl.ds(half, half)], far.at[3, pl.ds(half, half)], to_m)
    yield
    terms = pair(4)
    got(9, far.at[1])
    got(10, far.at[2])
    add_rows(mid[4], terms + [(far.at[1], 0), (far.at[2], 0)], rows)
    put(13, mid[4], far.at[4], to_x)
    yield
    terms = pair(5)
    got(11, far.at[3, pl.ds(0, half)])
    add_rows(mid[5], terms + [(far.at[3], 0)], half)
    add_rows(mid[5], [(r, half) for r, _ in terms], half, half)
    put(14, mid[5], far.at[5], to_p)
    terms = pair(6)
    got(12, far.at[3, pl.ds(half, half)])
    add_rows(mid[6], terms, half)
    add_rows(mid[6], [(r, half) for r, _ in terms] + [(far.at[3], half)], half, half)
    put(15, mid[6], far.at[6], to_m)
    yield
    terms = pair(7)
    got(13, far.at[4])
    got(14, far.at[5])
    got(15, far.at[6])
    add_rows(total, terms + [(far.at[4], 0), (far.at[5], 0), (far.at[6], 0)], rows)


def scatter_scratch(rows, cols):
    return [
        pltpu.VMEM((8, rows, cols), BF16),
        pltpu.VMEM((7, rows, cols), BF16),
    ]


def dma(n):
    return pltpu.SemaphoreType.DMA((n,))


def params(cid, mib=60):
    return pltpu.CompilerParams(
        collective_id=cid, has_side_effects=True, vmem_limit_bytes=mib * MIB
    )


Q_BLOCK = 256


def pick_rows(select, matrix):
    return nt(select.astype(BF16), matrix).astype(BF16)


def ones_at(rows, cols, shift, valid):
    row = lax.broadcasted_iota(jnp.int32, (rows, cols), 0)
    col = lax.broadcasted_iota(jnp.int32, (rows, cols), 1)
    return jnp.where((col == row + shift) & (row < valid), 1.0, 0.0)


def unit_of(row, c):
    shard = sum(((row >= 21 * n).astype(jnp.int32) for n in range(1, 8)), 0)
    place = row - 21 * shard
    inside = (row < 168) & ((place < 20) | (c < 8))
    return jnp.where(inside, 328 * shard + 16 * place + c, -1)


def iota(dims, axis):
    return lax.broadcasted_iota(jnp.int32, dims, axis)


def front_kernel(
    h_ref, dy_ref, wqkv_ref, wout_ref, wgu_ref, wdown_ref, g1_ref, g2_ref, cos_ref, sin_ref,
    wq_ref, h1_ref, dh1_ref, dot_ref, ggu_ref, gdown_ref, ggain_ref, gout_ref,
    n1_ref, downpart_ref, qt_out, kt_out, qr_out, kr_out, vr_out, ot_out, lse_out,
    hall, n1, dyall, nall, part, qt_ref, kt_ref, vt_ref, qr_ref, kr_ref, vr_ref, ot_ref, lse_ref,
    qkv_win, gu_acc, qkv_cols, gu_cols, down_rows, ob, att_ref, dat,
    woutall, gu_ref, downall, down_w, act, dgu, total, core_in, far, send, recv, local,
):
    p = Place()
    links = Links(
        send, recv, on_ctx(p.other),
        [hall.at[0], hall.at[0, pl.ds(0, 64)], qkv_cols, gu_cols, down_rows,
         ob.at[:, pl.ds(0, 128)]],
    )
    wins = [
        pltpu.make_async_copy(
            wqkv_ref.at[:, pl.ds(pl.multiple_of(part * 1024 + (p.c // 2) * 128, 128), 128)],
            qkv_win.at[part], local.at[part],
        )
        for part in range(3)
    ]
    own_h = pltpu.make_async_copy(h_ref, hall.at[p.c], local.at[5])
    for copy in wins:
        copy.start()
    own_h.start()
    for i in range(3):
        wins[i].wait()
        qkv_cols[pl.ds(64 * i, 64), :] = pick_rows(
            ones_at(64, 128, (p.c % 2) * 64, 64), qkv_win[i]
        )
    row = iota((16, 128), 0)
    gains = jnp.where(row == 0, g1_ref[...].astype(F32), 0.0)
    gains = jnp.where(row == 1, g2_ref[...].astype(F32), gains)
    qkv_cols[pl.ds(192, 16), :] = gains.astype(BF16)
    greet([on_ctx(p.ring[d]) for d in range(1, 16)] + p.fsdp_peers)
    gather_wq = gather_fsdp(p, links, 38, qkv_cols, lambda f: wq_ref.at[:, lanes_of(f)])
    next(gather_wq)
    gather_h = gather_ctx(p, links, 0, h_ref, hall, 128)
    ready = next(gather_h)
    lanes = lanes_of(p.f)
    wq_ref[:, lanes] = qkv_cols[...]
    for half in range(2):
        want = unit_of(iota((176, 1), 0), p.c)
        want = jnp.where(want < 0, -1, want + 64 * half)
        gu_acc[...] = jnp.zeros_like(gu_acc)

        def pick(i, _):
            cols = pl.ds(pl.multiple_of(2560 * half + i * 896, 128), 896)
            select = jnp.where(iota((176, 896), 1) + i * 896 == want, 1.0, 0.0)
            gu_acc[...] += nt(select.astype(BF16), wgu_ref[:, cols])
            return 0

        lax.fori_loop(0, 3, pick, 0)
        gu_cols[pl.ds(176 * half, 176), :] = gu_acc[...].astype(BF16)
    place = iota((32, 328), 0)
    select = (iota((32, 328), 1) == 16 * place + p.c) & (place < 21)
    down_rows[...] = nn(jnp.where(select, 1.0, 0.0).astype(BF16), wdown_ref[...]).astype(BF16)
    own_h.wait()
    next(gather_wq)
    ready += next(gather_h)
    next(gather_wq)
    gather_gu = gather_fsdp(p, links, 45, gu_cols, lambda f: gu_ref.at[:, lanes_of(f)])
    next(gather_gu)
    def down_slot(f):
        return downall.at[pl.ds(pl.multiple_of(f * 32, 32), 32)]

    gather_down = gather_fsdp(p, links, 83, down_rows, down_slot)
    next(gather_down)
    locals_ = [
        pltpu.make_async_copy(dy_ref, dyall.at[p.c], local.at[6]),
        pltpu.make_async_copy(
            wout_ref, woutall.at[pl.ds(pl.multiple_of(p.f * 128, 128), 128)], local.at[8]
        ),
        pltpu.make_async_copy(down_rows, down_slot(p.f), local.at[3]),
    ]
    for copy in locals_:
        copy.start()
    gu_ref[:, lanes] = gu_cols[...]
    half = pl.ds(pl.multiple_of(p.k * 64, 64), 64)

    def out_half(f, k):
        return woutall.at[pl.ds(pl.multiple_of(f * 128 + k * 64, 64), 64)]

    gather_out = gather_fsdp(p, links, 53, wout_ref.at[half], lambda f: out_half(f, p.k))
    next(gather_out)
    saves = []

    def project(b):
        gain = wq_ref[pl.ds(192, 1), :].astype(F32)

        def norm(i, _):
            r = pl.ds(pl.multiple_of(i * 32, 32), 32)
            xhat, _unused = normalize(hall[b, r, :].astype(F32))
            n1[b, r, :] = (xhat * gain).astype(BF16)
            return 0

        lax.fori_loop(0, 4, norm, 0)
        proj = nt(wq_ref[pl.ds(0, 192), :], n1[b])
        at = pl.ds(pl.multiple_of(b * 128, 128), 128)
        cos, sin = cos_ref[:, at], sin_ref[:, at]
        q = rope_t(proj[:64], cos, sin).astype(BF16) * jnp.asarray(0.125, BF16)
        k = rope_t(proj[64:128], cos, sin).astype(BF16)
        v = proj[128:192].astype(BF16)
        qt_ref[:, at] = q
        kt_ref[:, at] = k
        vt_ref[:, at] = v
        qr_ref[at, :] = q.astype(F32).T.astype(BF16)
        kr_ref[at, :] = k.astype(F32).T.astype(BF16)
        vr_ref[at, :] = v.astype(F32).T.astype(BF16)
        copy = pltpu.make_async_copy(n1.at[b], n1_ref.at[b], local.at[10 + len(saves)])
        copy.start()
        saves.append(copy)

    for b in ready:
        project(b)
    for b in next(gather_h):
        project(b)
    ready = next(gather_h)
    gather_dy = gather_ctx(p, links, 19, dy_ref, dyall, 128)
    next(gather_dy)
    for b in ready:
        project(b)
    while ready is not None:
        ready = next(gather_h, None)
        for b in ready or ():
            project(b)
    next(gather_gu)
    next(gather_down)
    twins = next(gather_out)
    plan = {1: gather_dy, 3: gather_dy, 4: gather_out, 6: gather_dy}

    def attend(i, _):
        j = (p.c // 2 + i) % 8
        at = pl.ds(pl.multiple_of(j * Q_BLOCK, Q_BLOCK), Q_BLOCK)
        scores = nn(kr_ref[...], qt_ref[:, at])
        top = jnp.max(scores, axis=0, keepdims=True)
        weights = jnp.exp(scores - top)
        total = jnp.sum(weights, axis=0, keepdims=True)
        mixed = nn(vt_ref[...], weights.astype(BF16)) / total
        ot_ref[:, at] = mixed
        lse_ref[:, at] = top + jnp.log(total)
        ob[:, at] = mixed.astype(BF16)

        @pl.when(i > 0)
        def _():
            for e in range(2):
                to = 2 * j + e
                piece = ob.at[:, pl.ds(pl.multiple_of(to * 128, 128), 128)]
                links.copy(67 + 2 * i + e - p.k, piece, att_ref.at[p.c], on_ctx(to)).start()

        @pl.when(i == 0)
        def _():
            piece = ob.at[:, pl.ds(pl.multiple_of(p.c * 128, 128), 128)]
            copy = pltpu.make_async_copy(piece, att_ref.at[p.c], local.at[9])
            copy.start()
            copy.wait()
            piece = ob.at[:, pl.ds(pl.multiple_of(p.other * 128, 128), 128)]
            links.copy(67 + (p.other - p.c + 16) % 16, piece, att_ref.at[p.c], on_ctx(p.other)).start()

        for s, stages in plan.items():

            @pl.when(i == s)
            def _():
                next(stages)

        return 0

    lax.fori_loop(0, 8, attend, 0)
    saves += [
        pltpu.make_async_copy(src, dst, local.at[26 + n])
        for n, (src, dst) in enumerate((
            (qt_ref, qt_out), (kt_ref, kt_out), (qr_ref, qr_out), (kr_ref, kr_out),
            (vr_ref, vr_out), (ot_ref, ot_out), (lse_ref, lse_out),
        ))
    ]
    for copy in saves[16:]:
        copy.start()
    others = twins + [p.planes[d] for d in (3, 1, 2)] + [p.twin_planes[d] for d in (3, 1, 2)]
    for i, f in enumerate(others):
        links.put(60 + i, out_half(f, p.k), out_half(f, p.k), on_ctx(p.other))
    for d in range(1, 16):
        links.got(67 + d, att_ref.at[p.ring[16 - d]])
        links.open.append((67 + d, ob.at[:, pl.ds(0, 128)]))
    for copy in locals_:
        copy.wait()
    for i, f in enumerate(others):
        links.got(60 + i, out_half(f, 1 - p.k))

    gain = wq_ref[pl.ds(193, 1), :].astype(F32)
    att = att_ref[...].reshape(1024, 128)
    h1 = h_ref[...].astype(F32) + tn(att, woutall[...])
    h1_ref[...] = h1
    xhat, _unused = normalize(h1)
    nall[p.c] = (xhat * gain).astype(BF16)
    gather = gather_ctx(p, links, 90, nall.at[p.c], nall, 128)
    ready = next(gather)
    next(gather_gu)
    next(gather_down)
    pick = iota((176, 256), 1)
    row = iota((176, 1), 0)
    shard = sum(((row >= 21 * n).astype(jnp.int32) for n in range(1, 8)), 0)
    want = jnp.where(row < 168, row + 11 * shard, -1)
    down_w[...] = nn(jnp.where(pick == want, 1.0, 0.0).astype(BF16), downall[...]).astype(BF16)
    for _ in gather_dy:
        pass

    def feed(b):
        n2 = nall[b]
        gu = nt(gu_ref[...], n2)
        d_act = nt(down_w[...], dyall[b])
        gate, up = gu[:176], gu[176:]
        cdf = 0.5 * (1.0 + lax.erf(gate * 2.0 ** (-0.5)))
        gelu = gate * cdf
        pdf = jnp.exp(-0.5 * gate * gate) * (2.0 * np.pi) ** (-0.5)
        d_gate = d_act * up * (cdf + gate * pdf)
        d_gu = jnp.concatenate([d_gate, d_act * gelu], axis=0).astype(BF16)
        at = pl.ds(pl.multiple_of(b * 128, 128), 128)
        act[:, at] = (gelu * up).astype(BF16)
        dgu[:, at] = d_gu
        part[b] = tn(d_gu, gu_ref[...]).astype(BF16)

    while ready is not None:
        for b in ready:
            feed(b)
        ready = next(gather, None)
    scatter = scatter_ctx(p, links, 109, part, total, core_in, far, 128)
    next(scatter)
    next(scatter)
    ggain = []
    for half in range(2):
        cols = pl.ds(512 * half, 512)
        g = nn(dgu[...], nall[:, :, cols].reshape(2048, 512))
        ggu_ref[:, cols] = g.astype(BF16)
        ggain.append(jnp.sum(g * gu_ref[:, cols].astype(F32), axis=0, keepdims=True))
    ggain_ref[...] = jnp.concatenate(ggain, axis=1) / gain
    next(scatter)
    row = iota((256, 1), 0)
    shard = row // 32
    place = row - 32 * shard
    want = jnp.where(place < 21, 21 * shard + place, -1)
    spread = jnp.where(iota((256, 176), 1) == want, 1.0, 0.0).astype(BF16)
    for half in range(2):
        cols = pl.ds(512 * half, 512)
        g = nn(act[...], dyall[:, :, cols].reshape(2048, 512)).astype(BF16)
        gdown_ref[:, cols] = nn(spread, g).astype(BF16)
    next(scatter)

    def down(b, _):
        at = pl.ds(pl.multiple_of(b * 128, 128), 128)
        hall[b] = tn(act[:, at], down_w[...]).astype(BF16)
        return 0

    next(scatter)
    links.close(90)
    lax.fori_loop(0, 16, down, 0)
    store = pltpu.make_async_copy(hall, downpart_ref, local.at[4])
    store.start()
    next(scatter, None)
    h1 = h1_ref[...]
    xhat, inv = normalize(h1)
    d_h1 = dy_ref[...].astype(F32) + norm_back(total[...], xhat, inv, gain)
    dh1_ref[...] = d_h1
    d_h1_b = d_h1.astype(BF16)
    dat[...] = nt(woutall[...], d_h1_b).astype(BF16).reshape(16, 64, 128)
    lanes = pl.ds(pl.multiple_of(p.c * 128, 128), 128)
    for d in range(1, 16):
        links.put(124 + d, dat.at[p.ring[d]], dot_ref.at[:, lanes], on_ctx(p.ring[d]))
    dot_ref[:, lanes] = dat[p.c]
    att = att_ref[...]
    for g in range(4):
        rows = att[4 * g : 4 * g + 4].reshape(256, 128)
        block = nn(rows, d_h1_b).reshape(2, 16, 8, 1024).transpose(1, 0, 2, 3)
        gout_ref[:, pl.ds(16 * g, 16), :] = block.reshape(16, 16, 1024).astype(BF16)
    for d in range(1, 16):
        links.got(124 + d, dot_ref.at[:, pl.ds(pl.multiple_of(p.ring[16 - d] * 128, 128), 128)])
    for copy in saves + [store]:
        copy.wait()
    links.close()


def shape(dims, dtype=BF16):
    return jax.ShapeDtypeStruct(dims, dtype)


def front(hidden, grad, wqkv, wout, wgu, wdown, g1, g2, cos, sin):
    heads = [
        shape((64, 2048)), shape((64, 2048)), shape((2048, 64)), shape((2048, 64)),
        shape((2048, 64)), shape((64, 2048), F32), shape((1, 2048), F32),
    ]
    blocks = pltpu.VMEM((16, 128, 1024), BF16)
    return pl.pallas_call(
        front_kernel,
        name="front",
        out_shape=(
            shape((208, 1024)), shape((128, 1024), F32), shape((128, 1024), F32),
            shape((64, 2048)), shape((352, 1024)), shape((256, 1024)), shape((1, 1024), F32),
            shape((16, 64, 1024)), shape((16, 128, 1024)), shape((16, 128, 1024)), *heads,
        ),
        in_specs=[VMEM, VMEM, ANY] + [VMEM] * 7,
        out_specs=(VMEM,) * 8 + (ANY,) * 9,
        scratch_shapes=[
            blocks, blocks, blocks, blocks, blocks,
            pltpu.VMEM((64, 2048), BF16),
            pltpu.VMEM((64, 2048), BF16),
            pltpu.VMEM((64, 2048), BF16),
            pltpu.VMEM((2048, 64), BF16),
            pltpu.VMEM((2048, 64), BF16),
            pltpu.VMEM((2048, 64), BF16),
            pltpu.VMEM((64, 2048), F32),
            pltpu.VMEM((1, 2048), F32),
            pltpu.VMEM((3, 128, 128), BF16),
            pltpu.VMEM((176, 128), F32),
            pltpu.VMEM((208, 128), BF16),
            pltpu.VMEM((352, 128), BF16),
            pltpu.VMEM((32, 1024), BF16),
            pltpu.VMEM((64, 2048), BF16),
            pltpu.VMEM((16, 64, 128), BF16),
            pltpu.VMEM((16, 64, 128), BF16),
            pltpu.VMEM((1024, 1024), BF16),
            pltpu.VMEM((352, 1024), BF16),
            pltpu.VMEM((256, 1024), BF16),
            pltpu.VMEM((176, 1024), BF16),
            pltpu.VMEM((176, 2048), BF16),
            pltpu.VMEM((352, 2048), BF16),
            pltpu.VMEM((128, 1024), F32),
        ] + scatter_scratch(128, 1024) + [dma(140), dma(140), dma(33)],
        compiler_params=params(1),
    )(hidden, grad, wqkv, wout, wgu, wdown, g1, g2, cos, sin)


LATE = 224


def backward_kernel(
    k_ref, v_ref, kt_ref, qt_ref, q_ref, dot_ref, ot_ref, lse_ref, cos_ref, sin_ref,
    n1_ref, wq_ref, h_ref, h1_ref, dh1_ref, downpart_ref, ggu_ref, gdown_ref, ggain_ref, gout_ref,
    result_ref, dinput_ref, gupieces_ref, rowpieces_ref, latepieces_ref,
    n1, downpart, gsum, dproj, dk, dv, part, late, rows_in,
    total, gout, gu_sum, row_sum, late_sum, *rest,
):
    (
        core_a, far_a, core_b, far_b, core_c, far_c,
        gu_along, gu_across, gu_keep, row_along, row_across, row_keep,
        late_along, late_across, late_keep, send, recv, local,
    ) = rest
    p = Place()
    links = Links(
        send, recv, on_ctx(p.other),
        [part.at[0], part.at[0, pl.ds(0, 64)], part.at[0, pl.ds(0, 32)], gu_keep,
         gu_keep.at[pl.ds(0, 176)], late_keep, late_keep.at[pl.ds(0, LATE // 2)]],
    )
    loads = [
        pltpu.make_async_copy(gout_ref, gsum, local.at[5]),
        pltpu.make_async_copy(downpart_ref, downpart, local.at[0]),
        pltpu.make_async_copy(n1_ref, n1, local.at[1]),
    ]
    for copy in loads:
        copy.start()
    greet(ctx_peers(p) + p.fsdp_peers)
    loads[0].wait()
    sum_out = scatter_ctx(p, links, 16, gsum, gout, core_b, far_b, 64)
    next(sum_out)
    sum_gu = scatter_fsdp(
        p, links, 48, lambda f: ggu_ref.at[:, lanes_of(f)], gu_along, gu_across, gu_keep, gu_sum, 352
    )
    next(sum_gu)
    loads[1].wait()
    down = scatter_ctx(p, links, 0, downpart, total.at[0], core_a, far_a, 128)
    next(down)
    sum_rows = scatter_fsdp(
        p, links, 55, lambda f: rows_in.at[f], row_along, row_across, row_keep, row_sum, 32
    )
    all_gu = gather_ctx(p, links, 69, gu_sum, gupieces_ref, 352)
    mine = [
        pltpu.make_async_copy(gu_sum, gupieces_ref.at[p.c], local.at[2]),
        pltpu.make_async_copy(row_sum, rowpieces_ref.at[p.c], local.at[3]),
        pltpu.make_async_copy(late_sum, latepieces_ref.at[p.c], local.at[4]),
    ]

    def begin_gu():
        next(sum_gu, None)
        next(all_gu)

    def step(stages):
        return lambda: next(stages, None)

    def begin_rows():
        next(sum_out, None)
        for f in range(8):
            rows_in[f, pl.ds(0, 16), :] = gdown_ref[pl.ds(32 * f, 16), :]
            tail = gdown_ref[pl.ds(32 * f + 16, 16), :].astype(F32)[:8]
            outs = gout[pl.ds(8 * f, 8), :]
            rows_in[f, pl.ds(16, 16), :] = jnp.concatenate([tail, outs], axis=0).astype(BF16)
        next(sum_rows)

    plan = {
        0: [step(sum_out)], 1: [step(down)], 2: [step(sum_out)], 3: [step(sum_out)],
        4: [step(sum_gu), step(sum_out)], 5: [step(down), begin_rows], 6: [step(down), begin_gu],
        7: [step(down)],
    }
    dk[...] = jnp.zeros_like(dk)
    dv[...] = jnp.zeros_like(dv)

    def attend(i, _):
        at = pl.ds(pl.multiple_of(i * Q_BLOCK, Q_BLOCK), Q_BLOCK)
        scores = nn(k_ref[...], qt_ref[:, at])
        prob = jnp.exp(scores - lse_ref[:, at])
        dout = dot_ref[:, at]
        d_prob = nn(v_ref[...], dout)
        delta = jnp.sum(dout.astype(F32) * ot_ref[:, at], axis=0, keepdims=True)
        d_scores = (prob * (d_prob - delta)).astype(BF16)
        d_query = nn(kt_ref[...], d_scores) * 0.125
        dproj[pl.ds(0, 64), at] = unrope_t(d_query, cos_ref[:, at], sin_ref[:, at]).astype(BF16)
        dk[...] += nn(d_scores, q_ref[at, :])
        dv[...] += nn(prob.astype(BF16), dout.astype(F32).T.astype(BF16))
        for n, steps in plan.items():

            @pl.when(i == n)
            def _():
                for run in steps:
                    run()

        return 0

    lax.fori_loop(0, 8, attend, 0)

    def project(b, _):
        at = pl.ds(pl.multiple_of(b * 128, 128), 128)
        d_key = unrope_t(dk[at, :].T, cos_ref[:, at], sin_ref[:, at])
        dproj[pl.ds(64, 64), at] = d_key.astype(BF16)
        dproj[pl.ds(128, 64), at] = dv[at, :].T.astype(BF16)
        part[b] = tn(dproj[:, at], wq_ref[pl.ds(0, 192), :]).astype(BF16)
        return 0

    lax.fori_loop(0, 16, project, 0)
    back = scatter_ctx(p, links, 32, part, total.at[1], core_c, far_c, 128)
    next(back)
    next(back)
    next(down, None)
    result_ref[...] = (h1_ref[...] + total[0]).astype(BF16)
    next(sum_rows)
    next(all_gu)
    loads[2].wait()
    gain = wq_ref[pl.ds(192, 1), :].astype(F32)
    late[...] = jnp.zeros_like(late)
    ggain = []
    for half in range(2):
        cols = pl.ds(512 * half, 512)
        g = nn(dproj[...], n1[:, :, cols].reshape(2048, 512))
        late[pl.ds(0, 192), cols] = g.astype(BF16)
        ggain.append(jnp.sum(g * wq_ref[pl.ds(0, 192), cols].astype(F32), axis=0, keepdims=True))
    gain_row = jnp.concatenate(ggain, axis=1) / gain
    row = iota((16, 1024), 0)
    gains = jnp.where(row == 0, gain_row, 0.0)
    late[pl.ds(192, 16), :] = jnp.where(row == 1, ggain_ref[...], gains).astype(BF16)
    sum_late = scatter_fsdp(
        p, links, 62, lambda f: late.at[:, lanes_of(f)],
        late_along, late_across, late_keep, late_sum, LATE,
    )
    next(sum_late)
    next(back)
    next(sum_rows, None)
    all_rows = gather_ctx(p, links, 88, row_sum, rowpieces_ref, 32)
    next(all_rows)
    next(all_gu)
    next(back)
    next(sum_late)
    next(back)
    next(all_rows)
    next(all_gu)
    next(sum_late, None)
    all_late = gather_ctx(p, links, 107, late_sum, latepieces_ref, LATE)
    next(all_late)
    next(back, None)
    xhat, inv = normalize(h_ref[...].astype(F32))
    d_in = norm_back(total[1], xhat, inv, gain)
    dinput_ref[...] = (dh1_ref[...] + d_in).astype(BF16)
    for copy in mine:
        copy.start()
    run_all([all_gu, all_late, all_rows])
    for copy in mine:
        copy.wait()
    links.close()


def backward(*args):
    return pl.pallas_call(
        backward_kernel,
        name="backward",
        out_shape=(
            shape((128, 1024)), shape((128, 1024)), shape((16, 352, 128)),
            shape((16, 32, 1024)), shape((16, LATE, 128)),
        ),
        in_specs=[VMEM] * 10 + [ANY] + [VMEM] * 4 + [ANY] + [VMEM] * 3 + [ANY],
        out_specs=(VMEM, VMEM, ANY, ANY, ANY),
        scratch_shapes=[
            pltpu.VMEM((16, 128, 1024), BF16),
            pltpu.VMEM((16, 128, 1024), BF16),
            pltpu.VMEM((16, 64, 1024), BF16),
            pltpu.VMEM((192, 2048), BF16),
            pltpu.VMEM((2048, 64), F32),
            pltpu.VMEM((2048, 64), F32),
            pltpu.VMEM((16, 128, 1024), BF16),
            pltpu.VMEM((LATE, 1024), BF16),
            pltpu.VMEM((8, 32, 1024), BF16),
            pltpu.VMEM((2, 128, 1024), F32),
            pltpu.VMEM((64, 1024), F32),
            pltpu.VMEM((352, 128), BF16),
            pltpu.VMEM((32, 1024), BF16),
            pltpu.VMEM((LATE, 128), BF16),
        ] + scatter_scratch(128, 1024) + scatter_scratch(64, 1024) + scatter_scratch(128, 1024)
        + fsdp_scratch(352, 128) + fsdp_scratch(32, 1024) + fsdp_scratch(LATE, 128)
        + [dma(126), dma(126), dma(6)],
        compiler_params=params(3),
    )(*args)


def fsdp_scratch(rows, cols):
    return [
        pltpu.VMEM((6, rows, cols), BF16),
        pltpu.VMEM((2, rows, cols), BF16),
        pltpu.VMEM((rows, cols), BF16),
    ]


def nt(a, b):
    return lax.dot_general(a, b, (((1,), (1,)), ((), ())), preferred_element_type=F32)


def tn(a, b):
    return lax.dot_general(a, b, (((0,), (0,)), ((), ())), preferred_element_type=F32)


def nn(a, b):
    return jnp.dot(a, b, preferred_element_type=F32)


def normalize(v):
    centered = v - jnp.mean(v, axis=-1, keepdims=True)
    inv = lax.rsqrt(jnp.mean(centered * centered, axis=-1, keepdims=True) + EPSILON)
    return centered * inv, inv


def norm_back(e, xhat, inv, gain):
    eg = e * gain
    return inv * (
        eg - jnp.mean(eg, axis=-1, keepdims=True)
        - xhat * jnp.mean(eg * xhat, axis=-1, keepdims=True)
    )


def rope_t(v, cos, sin):
    a, b = v[:32], v[32:]
    return jnp.concatenate([a * cos - b * sin, b * cos + a * sin], axis=0)


def unrope_t(v, cos, sin):
    a, b = v[:32], v[32:]
    return jnp.concatenate([a * cos + b * sin, b * cos - a * sin], axis=0)


def rope_tables():
    inverse = np.float32(ROPE_BASE) ** (-(np.arange(32, dtype=np.float32) * 2.0) / 64)
    angles = inverse[:, None].astype(np.float32) * np.arange(2048, dtype=np.float32)[None, :]
    return np.cos(angles).astype(np.float32), np.sin(angles).astype(np.float32)


def body(
    hidden_in, qkv_weight, out_weight, gate_up_weight, down_weight, attn_gain, mlp_gain, out_grad
):
    hidden_b, grad_b = hidden_in[0], out_grad[0]
    cos, sin = rope_tables()
    cos, sin = jnp.asarray(cos), jnp.asarray(sin)
    (
        w_q, h1, d_h1, do_t, g_gu, g_down, g_gain_two, g_out,
        n1, down_part, q_t, k_t, queries, keys, values, o_t, lse,
    ) = front(
        hidden_b, grad_b, qkv_weight, out_weight, gate_up_weight, down_weight,
        attn_gain[None], mlp_gain[None], cos, sin,
    )
    result, input_grad, gu_pieces, row_pieces, late_pieces = backward(
        keys, values, k_t, q_t, queries, do_t, o_t, lse, cos, sin,
        n1, w_q, hidden_b, h1, d_h1, down_part, g_gu, g_down, g_gain_two, g_out,
    )
    late_pieces = late_pieces.astype(F32)
    qkv_grad = (
        late_pieces[:, :192].reshape(16, 3, 64, 128).transpose(3, 1, 0, 2).reshape(128, 3072)
    )
    gain_grads = jnp.sum(late_pieces[:, 192:194], axis=0)
    gate_up = gu_pieces.reshape(16, 2, 176, 128)[:, :, :168].transpose(1, 2, 0, 3)
    gate_up = gate_up.reshape(2, 8, 336, 128)[:, :, :328].reshape(5248, 128)
    gate_up_grad = gate_up.astype(F32).T
    down_grad = (
        row_pieces[:, :21].transpose(1, 0, 2).reshape(336, 1024)[:328].astype(F32)
    )
    out_weight_grad = row_pieces[:, 24:].reshape(128, 1024).astype(F32)
    return (
        result[None], input_grad[None], qkv_grad, out_weight_grad, gate_up_grad, down_grad,
        gain_grads[0], gain_grads[1],
    )


def solution(mesh):
    return jax.shard_map(
        body,
        mesh=mesh,
        in_specs=(
            P("fsdp", "ctx", None), P("fsdp", None), P("fsdp", None), P("fsdp", None),
            P("fsdp", None), P("fsdp"), P("fsdp"), P("fsdp", "ctx", None),
        ),
        out_specs=(
            P("fsdp", "ctx", None), P("fsdp", "ctx", None), P("fsdp", None), P("fsdp", None),
            P("fsdp", None), P("fsdp", None), P("fsdp"), P("fsdp"),
        ),
        check_vma=False,
    )
```

```python
import jax
import jax.numpy as jnp
import numpy as np
from jax import lax
from jax.experimental import pallas as pl
from jax.experimental.pallas import tpu as pltpu
from jax.sharding import PartitionSpec as P

HEADS = 16
EPSILON = 1e-05
ROPE_BASE = 160000.0
F32 = jnp.float32
BF16 = jnp.bfloat16
MESH = pl.DeviceIdType.MESH
ANY = pl.BlockSpec(memory_space=pl.ANY)
VMEM = pl.BlockSpec(memory_space=pltpu.VMEM)
MIB = 1024 * 1024


class Place:
    def __init__(self):
        c = lax.axis_index("ctx")
        self.c = c
        self.f = lax.axis_index("fsdp")
        k = c % 2
        y = (c // 2) % 4
        xl = c // 8
        self.k = k

        def at(x, row):
            return x * 4 + row % 4

        ox = 1 - xl
        self.other = c + 1 - 2 * k
        self.chip = {
            "S": at(xl, y),
            "P": at(xl, y + 1),
            "M": at(xl, y + 3),
            "F": at(xl, y + 2),
            "X": at(ox, y),
            "XP": at(ox, y + 1),
            "XM": at(ox, y + 3),
            "XF": at(ox, y + 2),
        }

        self.same_core = {name: chip * 2 + k for name, chip in self.chip.items()}
        self.cross_core = {name: chip * 2 + 1 - k for name, chip in self.chip.items()}
        self.xl = xl
        self.t = c % 8
        self.column = {name: chip % 4 * 2 + k for name, chip in self.chip.items()}
        self.cross_column = {name: chip % 4 * 2 + 1 - k for name, chip in self.chip.items()}
        self.ring = [(c + d) % 16 for d in range(16)]
        z, xh = self.f // 2, self.f % 2
        self.twin = z * 2 + 1 - xh
        self.planes = [(z + d) % 4 * 2 + xh for d in range(4)]
        self.twin_planes = [(z + d) % 4 * 2 + 1 - xh for d in range(4)]
        self.fsdp_peers = [{"fsdp": i} for i in [self.twin] + self.planes[1:]]

    def same(self, name):
        return self.same_core[name]

    def cross(self, name):
        return self.cross_core[name]


def lanes_of(f):
    return pl.ds(pl.multiple_of(f * 128, 128), 128)


def on_ctx(index):
    return {"ctx": index}


def greet(peers):
    barrier = pltpu.get_barrier_semaphore()
    for peer in peers:
        pl.semaphore_signal(barrier, inc=1, device_id=peer, device_id_type=MESH)
    pl.semaphore_wait(barrier, len(peers))


class Links:
    def __init__(self, send, recv, peer, like=()):
        self.send, self.recv, self.peer = send, recv, peer
        self.like = {ref.shape: ref for ref in like}
        self.open = []

    def copy(self, i, src, dst, peer):
        return pltpu.make_async_remote_copy(
            src_ref=src, dst_ref=dst, send_sem=self.send.at[i], recv_sem=self.recv.at[i],
            device_id=peer, device_id_type=MESH,
        )

    def put(self, i, src, dst, peer):
        self.copy(i, src, dst, peer).start()
        self.open.append((i, self.like.get(src.shape, src)))

    def got(self, i, dst):
        self.copy(i, dst, dst, self.peer).wait_recv()

    def close(self, below=1000):
        for i, ref in self.open:
            if i < below:
                self.copy(i, ref, ref, self.peer).wait_send()
        self.open = [(i, ref) for i, ref in self.open if i >= below]


def ctx_peers(p):
    return [on_ctx(p.other), on_ctx(p.same("P")), on_ctx(p.same("M")), on_ctx(p.same("X"))]


GATHER_COPIES = 19


def gather_ctx(p, links, base, own, out, rows, off=None):
    half = rows // 2
    top, bottom = pl.ds(0, half), pl.ds(half, half)
    to_p, to_m, to_x, to_k = (
        on_ctx(p.same("P")), on_ctx(p.same("M")), on_ctx(p.same("X")), on_ctx(p.other),
    )

    def rows_of(ref):
        return ref if off is None else ref.at[pl.ds(off, rows)]

    own = rows_of(own)
    mine = rows_of(out.at[p.c])

    def put(i, src, dst, peer):
        links.put(base + i, src, dst, peer)

    def got(i, dst):
        links.got(base + i, dst)

    def block(name):
        return rows_of(out.at[p.same(name)])

    def cross(name):
        return rows_of(out.at[p.cross(name)])

    put(0, own, mine, to_p)
    put(1, own, mine, to_m)
    put(2, own, mine, to_x)
    put(3, own, mine, to_k)
    yield [p.same("S")]
    got(0, block("M"))
    put(4, block("M").at[top], block("M").at[top], to_p)
    put(10, block("M"), block("M"), to_k)
    got(1, block("P"))
    put(5, block("P").at[bottom], block("P").at[bottom], to_m)
    put(11, block("P"), block("P"), to_k)
    got(2, block("X"))
    put(6, block("X"), block("X"), to_p)
    put(7, block("X"), block("X"), to_m)
    put(12, block("X"), block("X"), to_k)
    got(3, cross("S"))
    yield [p.same("M"), p.same("P"), p.same("X"), p.cross("S")]
    for i, part, to_core in ((4, top, 13), (5, bottom, 14)):
        piece = block("F").at[part]
        got(i, piece)
        put(4 + i, piece, piece, to_x)
        put(to_core, piece, piece, to_k)
    got(10, cross("M"))
    got(11, cross("P"))
    yield [p.same("F"), p.cross("M"), p.cross("P")]
    got(6, block("XM"))
    put(15, block("XM"), block("XM"), to_k)
    got(7, block("XP"))
    put(16, block("XP"), block("XP"), to_k)
    got(12, cross("X"))
    got(13, cross("F").at[top])
    got(14, cross("F").at[bottom])
    yield [p.same("XM"), p.same("XP"), p.cross("X"), p.cross("F")]
    for i, part, to_core in ((8, top, 17), (9, bottom, 18)):
        piece = block("XF").at[part]
        got(i, piece)
        put(to_core, piece, piece, to_k)
    got(15, cross("XM"))
    got(16, cross("XP"))
    yield [p.same("XF"), p.cross("XM"), p.cross("XP")]
    got(17, cross("XF").at[top])
    got(18, cross("XF").at[bottom])
    yield [p.cross("XF")]


def gather_column(p, links, base, own, out, rows):
    half = rows // 2
    top, bottom = pl.ds(0, half), pl.ds(half, half)
    to_p, to_m, to_k = on_ctx(p.same("P")), on_ctx(p.same("M")), on_ctx(p.other)
    same, cross = p.column, p.cross_column

    def put(i, src, dst, peer):
        links.put(base + i, src, dst, peer)

    def got(i, dst):
        links.got(base + i, dst)

    mine = out.at[same["S"]]
    put(0, own, mine, to_p)
    put(1, own, mine, to_m)
    put(2, own, mine, to_k)
    yield [same["S"]]
    got(0, out.at[same["M"]])
    put(3, out.at[same["M"], top], out.at[same["M"], top], to_p)
    put(5, out.at[same["M"]], out.at[same["M"]], to_k)
    got(1, out.at[same["P"]])
    put(4, out.at[same["P"], bottom], out.at[same["P"], bottom], to_m)
    put(6, out.at[same["P"]], out.at[same["P"]], to_k)
    got(2, out.at[cross["S"]])
    yield [cross["S"], same["M"], same["P"]]
    got(5, out.at[cross["M"]])
    got(3, out.at[same["F"], top])
    put(7, out.at[same["F"], top], out.at[same["F"], top], to_k)
    got(4, out.at[same["F"], bottom])
    put(8, out.at[same["F"], bottom], out.at[same["F"], bottom], to_k)
    got(6, out.at[cross["P"]])
    yield [same["F"], cross["M"], cross["P"]]
    got(7, out.at[cross["F"], top])
    got(8, out.at[cross["F"], bottom])
    yield [cross["F"]]


def scatter_column(p, links, base, part, total, core_in, far, rows):
    half = rows // 2
    whole, top, bottom = pl.ds(0, rows), pl.ds(0, half), pl.ds(half, half)
    to_p, to_m, to_k = on_ctx(p.same("P")), on_ctx(p.same("M")), on_ctx(p.other)
    order = ("F", "P", "M", "S")
    mid = [part.at[p.column[name]] for name in order]

    def put(i, src, dst, peer):
        links.put(base + i, src, dst, peer)

    def got(i, dst):
        links.got(base + i, dst)

    for i, name in enumerate(order):
        put(i, part.at[p.cross_column[name]], core_in.at[i], to_k)
    yield

    def pair(i):
        got(i, core_in.at[i])
        return [(mid[i], 0), (core_in.at[i], 0)]

    add_rows(mid[0], pair(0), rows)
    put(4, mid[0].at[top], far.at[0, top], to_p)
    put(5, mid[0].at[bottom], far.at[0, bottom], to_m)
    yield
    terms = pair(1)
    got(4, far.at[0, top])
    add_rows(mid[1], terms + [(far.at[0], 0)], half)
    add_rows(mid[1], terms, half, half)
    put(6, mid[1], far.at[1], to_p)
    terms = pair(2)
    got(5, far.at[0, bottom])
    add_rows(mid[2], terms, half)
    add_rows(mid[2], terms + [(far.at[0], 0)], half, half)
    put(7, mid[2], far.at[2], to_m)
    yield
    terms = pair(3)
    got(6, far.at[1])
    got(7, far.at[2])
    add_rows(total, terms + [(far.at[1], 0), (far.at[2], 0)], rows)


def gather_fsdp(p, links, base, own, slot):
    links.put(base, own, slot(p.f), {"fsdp": p.twin})
    for d in (1, 3, 2):
        links.put(base + d, own, slot(p.f), {"fsdp": p.planes[d]})
    yield []
    twin = slot(p.twin)
    links.got(base, twin)
    for d in (1, 3, 2):
        links.put(base + 3 + d, twin, twin, {"fsdp": p.planes[d]})
    yield [p.twin]
    for d in (1, 3, 2):
        links.got(base + d, slot(p.planes[4 - d]))
    for d in (1, 3, 2):
        links.got(base + 3 + d, slot(p.twin_planes[4 - d]))
    yield [p.planes[d] for d in (3, 1, 2)] + [p.twin_planes[d] for d in (3, 1, 2)]


def gather_ring(p, links, base, own, slot):
    up, down = {"fsdp": p.planes[1]}, {"fsdp": p.planes[3]}
    links.put(base + 1, own, slot(p.f), up)
    links.put(base + 2, own, slot(p.f), down)
    links.put(base, own, slot(p.f), {"fsdp": p.twin})
    yield []
    links.got(base, slot(p.twin))
    links.put(base + 4, slot(p.twin), slot(p.twin), up)
    links.put(base + 5, slot(p.twin), slot(p.twin), down)
    below = slot(p.planes[3])
    links.got(base + 1, below)
    links.put(base + 3, below, below, up)
    yield []
    above = slot(p.twin_planes[1])
    links.got(base + 5, above)
    links.put(base + 6, above, above, down)
    yield []
    links.got(base + 2, slot(p.planes[1]))
    links.got(base + 3, slot(p.planes[2]))
    links.got(base + 4, slot(p.twin_planes[3]))
    links.got(base + 6, slot(p.twin_planes[2]))
    yield []


def scatter_fsdp(p, links, base, part, along, across, keep, total, rows):
    for n, d in enumerate((1, 3, 2)):
        links.put(base + n, part(p.planes[d]), along.at[n], {"fsdp": p.planes[d]})
        links.put(base + 3 + n, part(p.twin_planes[d]), along.at[3 + n], {"fsdp": p.planes[d]})
    yield
    for n in range(6):
        links.got(base + n, along.at[n])
    terms = [(along.at[3 + n], 0) for n in range(3)]
    add_rows(across.at[0], [(part(p.twin), 0)] + terms, rows)
    links.put(base + 6, across.at[0], across.at[1], {"fsdp": p.twin})
    add_rows(keep, [(part(p.f), 0)] + [(along.at[n], 0) for n in range(3)], rows)
    yield
    links.got(base + 6, across.at[1])
    add_rows(total, [(keep, 0), (across.at[1], 0)], rows)


def run_all(stages):
    live = list(stages)
    while live:
        left = []
        for stage in live:
            try:
                next(stage)
                left.append(stage)
            except StopIteration:
                pass
        live = left


SCATTER_COPIES = 16
SCATTER_ORDER = ("XF", "XP", "XM", "F", "X", "P", "M", "S")


def add_rows(dst, terms, rows, at=0):
    step = 16

    def one(i, _):
        r = pl.ds(pl.multiple_of(i * step, step) + at, step)
        total = None
        for ref, _unused in terms:
            part = ref[r, :].astype(F32)
            total = part if total is None else total + part
        dst[r, :] = total.astype(dst.dtype)
        return 0

    lax.fori_loop(0, rows // step, one, 0)


def lockstep(*stages):
    while True:
        found = []
        ended = 0
        for one in stages:
            try:
                found += next(one) or []
            except StopIteration:
                ended += 1
        if ended == len(stages):
            return
        yield found


def scatter_ctx(p, links, base, part, total, core_in, far, rows, off=0):
    half = rows // 2
    to_p, to_m, to_x, to_k = (
        on_ctx(p.same("P")), on_ctx(p.same("M")), on_ctx(p.same("X")), on_ctx(p.other),
    )

    def put(i, src, dst, peer):
        links.put(base + i, src, dst, peer)

    def got(i, dst):
        links.got(base + i, dst)

    whole = pl.ds(off, rows)
    top, bottom = pl.ds(off, half), pl.ds(off + half, half)
    mid = [part.at[p.same(name)] for name in SCATTER_ORDER]
    for i, name in enumerate(SCATTER_ORDER):
        put(i, part.at[p.cross(name), whole], core_in.at[i, whole], to_k)
    yield

    def pair(i):
        got(i, core_in.at[i, whole])
        return [(mid[i], 0), (core_in.at[i], 0)]

    for i, peer in ((0, to_x), (1, to_p), (2, to_m)):
        add_rows(mid[i], pair(i), rows, off)
        put(8 + i, mid[i].at[whole], far.at[i, whole], peer)
    yield
    terms = pair(3)
    got(8, far.at[0, whole])
    add_rows(mid[3], terms + [(far.at[0], 0)], rows, off)
    put(11, mid[3].at[top], far.at[3, top], to_p)
    put(12, mid[3].at[bottom], far.at[3, bottom], to_m)
    yield
    terms = pair(4)
    got(9, far.at[1, whole])
    got(10, far.at[2, whole])
    add_rows(mid[4], terms + [(far.at[1], 0), (far.at[2], 0)], rows, off)
    put(13, mid[4].at[whole], far.at[4, whole], to_x)
    yield
    terms = pair(5)
    got(11, far.at[3, top])
    add_rows(mid[5], terms + [(far.at[3], 0)], half, off)
    add_rows(mid[5], terms, half, off + half)
    put(14, mid[5].at[whole], far.at[5, whole], to_p)
    terms = pair(6)
    got(12, far.at[3, bottom])
    add_rows(mid[6], terms, half, off)
    add_rows(mid[6], terms + [(far.at[3], 0)], half, off + half)
    put(15, mid[6].at[whole], far.at[6, whole], to_m)
    yield
    terms = pair(7)
    got(13, far.at[4, whole])
    got(14, far.at[5, whole])
    got(15, far.at[6, whole])
    add_rows(total, terms + [(far.at[4], 0), (far.at[5], 0), (far.at[6], 0)], rows, off)


def scatter_scratch(rows, cols):
    return [
        pltpu.VMEM((8, rows, cols), BF16),
        pltpu.VMEM((7, rows, cols), BF16),
    ]


def column_scratch(rows, cols):
    return [pltpu.VMEM((4, rows, cols), BF16), pltpu.VMEM((3, rows, cols), BF16)]


def dma(n):
    return pltpu.SemaphoreType.DMA((n,))


def params(cid, mib=60):
    return pltpu.CompilerParams(
        collective_id=cid, has_side_effects=True, vmem_limit_bytes=mib * MIB
    )


Q_BLOCK = 256
UNITS = 352


def pick_rows(select, matrix):
    return nt(select.astype(BF16), matrix).astype(BF16)


def ones_at(rows, cols, shift, valid):
    row = lax.broadcasted_iota(jnp.int32, (rows, cols), 0)
    col = lax.broadcasted_iota(jnp.int32, (rows, cols), 1)
    return jnp.where((col == row + shift) & (row < valid), 1.0, 0.0)


def shard_of(row):
    return sum(((row >= 41 * n).astype(jnp.int32) for n in range(1, 8)), 0)


def iota(dims, axis):
    return lax.broadcasted_iota(jnp.int32, dims, axis)


def front_kernel(
    h_ref, dy_ref, wqkv_ref, wout_ref, wgu_ref, wdown_ref, g1_ref, g2_ref, cos_ref, sin_ref,
    wq_ref, result_ref, dh1_ref, dot_ref, gusum_ref, gdown_ref, ggain_ref, gout_ref,
    n1_ref, qt_out, kt_out, qr_out, kr_out, vr_out, ot_out, lse_out,
    hall, n1, dyall, nall, part, downsum, qt_ref, kt_ref, vt_ref, qr_ref, kr_ref, vr_ref, ot_ref, lse_ref,
    qkv_win, gu_acc, qkv_cols, gu_cols, down_rows, ob, att_ref, dat,
    woutall, gu_ref, downall, down_w, act, dgu, total, core_in, far, ggu, gu_along, gu_across, gu_keep,
    h1_ref, down_total, core_down, far_down, send, recv, local,
):
    p = Place()
    links = Links(
        send, recv, on_ctx(p.other),
        [hall.at[0], hall.at[0, pl.ds(0, 64)], qkv_cols, gu_cols, down_rows,
         ob.at[:, pl.ds(0, 128)]],
    )
    wins = [
        pltpu.make_async_copy(
            wqkv_ref.at[:, pl.ds(pl.multiple_of(part * 1024 + (p.c // 2) * 128, 128), 128)],
            qkv_win.at[part], local.at[part],
        )
        for part in range(3)
    ]
    own_h = pltpu.make_async_copy(h_ref, hall.at[p.c], local.at[5])
    for copy in wins:
        copy.start()
    own_h.start()
    for i in range(3):
        wins[i].wait()
        qkv_cols[pl.ds(64 * i, 64), :] = pick_rows(
            ones_at(64, 128, (p.c % 2) * 64, 64), qkv_win[i]
        )
    row = iota((16, 128), 0)
    gains = jnp.where(row == 0, g1_ref[...].astype(F32), 0.0)
    gains = jnp.where(row == 1, g2_ref[...].astype(F32), gains)
    qkv_cols[pl.ds(192, 16), :] = gains.astype(BF16)
    greet([on_ctx(p.ring[d]) for d in range(1, 16)] + p.fsdp_peers)
    gather_wq = gather_fsdp(p, links, 38, qkv_cols, lambda f: wq_ref.at[:, lanes_of(f)])
    next(gather_wq)
    gather_h = gather_ctx(p, links, 0, h_ref, hall, 128)
    ready = next(gather_h)
    lanes = lanes_of(p.f)
    half = pl.ds(pl.multiple_of(p.k * 64, 64), 64)

    def out_half(f, k):
        return woutall.at[pl.ds(pl.multiple_of(f * 128 + k * 64, 64), 64)]

    gather_out = gather_ring(p, links, 53, wout_ref.at[half], lambda f: out_half(f, p.k))
    next(gather_out)
    wq_ref[:, lanes] = qkv_cols[...]
    for half in range(2):
        row = iota((UNITS, 1), 0)
        want = jnp.where(row < 328, 8 * row + p.t + 64 * half, -1)
        gu_acc[...] = jnp.zeros_like(gu_acc)

        def pick(i, _):
            cols = pl.ds(pl.multiple_of(2560 * half + i * 896, 128), 896)
            select = jnp.where(iota((UNITS, 896), 1) + i * 896 == want, 1.0, 0.0)
            gu_acc[...] += nt(select.astype(BF16), wgu_ref[:, cols])
            return 0

        lax.fori_loop(0, 3, pick, 0)
        gu_cols[pl.ds(UNITS * half, UNITS), :] = gu_acc[...].astype(BF16)
    place = iota((48, 328), 0)
    select = (iota((48, 328), 1) == 8 * place + p.t) & (place < 41)
    down_rows[...] = nn(jnp.where(select, 1.0, 0.0).astype(BF16), wdown_ref[...]).astype(BF16)
    gather_gu = gather_ring(p, links, 45, gu_cols, lambda f: gu_ref.at[:, lanes_of(f)])
    next(gather_gu)

    def down_slot(f):
        return downall.at[pl.ds(pl.multiple_of(f * 48, 16), 48)]

    gather_down = gather_ring(p, links, 83, down_rows, down_slot)
    next(gather_down)
    own_h.wait()
    next(gather_wq)
    ready += next(gather_h)
    next(gather_wq)
    locals_ = [
        pltpu.make_async_copy(dy_ref, dyall.at[p.t], local.at[6]),
        pltpu.make_async_copy(
            wout_ref, woutall.at[pl.ds(pl.multiple_of(p.f * 128, 128), 128)], local.at[8]
        ),
        pltpu.make_async_copy(down_rows, down_slot(p.f), local.at[3]),
    ]
    for copy in locals_:
        copy.start()
    gu_ref[:, lanes] = gu_cols[...]
    next(gather_out)
    saves = []

    def project(b):
        gain = wq_ref[pl.ds(192, 1), :].astype(F32)

        def norm(i, _):
            r = pl.ds(pl.multiple_of(i * 32, 32), 32)
            xhat, _unused = normalize(hall[b, r, :].astype(F32))
            n1[b, r, :] = (xhat * gain).astype(BF16)
            return 0

        lax.fori_loop(0, 4, norm, 0)
        proj = nt(wq_ref[pl.ds(0, 192), :], n1[b])
        at = pl.ds(pl.multiple_of(b * 128, 128), 128)
        cos, sin = cos_ref[:, at], sin_ref[:, at]
        q = rope_t(proj[:64], cos, sin).astype(BF16) * jnp.asarray(0.125, BF16)
        k = rope_t(proj[64:128], cos, sin).astype(BF16)
        v = proj[128:192].astype(BF16)
        qt_ref[:, at] = q
        kt_ref[:, at] = k
        vt_ref[:, at] = v
        qr_ref[at, :] = q.astype(F32).T.astype(BF16)
        kr_ref[at, :] = k.astype(F32).T.astype(BF16)
        vr_ref[at, :] = v.astype(F32).T.astype(BF16)
        copy = pltpu.make_async_copy(n1.at[b], n1_ref.at[b], local.at[10 + len(saves)])
        copy.start()
        saves.append(copy)

    for b in ready:
        project(b)
    for b in next(gather_h):
        project(b)
    ready = next(gather_h)
    gather_dy = gather_column(p, links, 19, dy_ref, dyall, 128)
    next(gather_dy)
    for b in ready:
        project(b)
    while ready is not None:
        ready = next(gather_h, None)
        for b in ready or ():
            project(b)
    next(gather_out)
    next(gather_gu)
    next(gather_down)
    plan = {1: gather_dy, 2: gather_gu, 3: gather_down, 4: gather_out, 5: gather_dy}

    def attend(i, _):
        j = (p.c // 2 + i) % 8
        at = pl.ds(pl.multiple_of(j * Q_BLOCK, Q_BLOCK), Q_BLOCK)
        scores = nn(kr_ref[...], qt_ref[:, at])
        top = jnp.max(scores, axis=0, keepdims=True)
        weights = jnp.exp(scores - top)
        total = jnp.sum(weights, axis=0, keepdims=True)
        mixed = nn(vt_ref[...], weights.astype(BF16)) / total
        ot_ref[:, at] = mixed
        lse_ref[:, at] = top + jnp.log(total)
        ob[:, at] = mixed.astype(BF16)

        @pl.when(i > 0)
        def _():
            for e in range(2):
                to = 2 * j + e
                piece = ob.at[:, pl.ds(pl.multiple_of(to * 128, 128), 128)]
                links.copy(67 + 2 * i + e - p.k, piece, att_ref.at[p.c], on_ctx(to)).start()

        @pl.when(i == 0)
        def _():
            piece = ob.at[:, pl.ds(pl.multiple_of(p.c * 128, 128), 128)]
            copy = pltpu.make_async_copy(piece, att_ref.at[p.c], local.at[9])
            copy.start()
            copy.wait()
            piece = ob.at[:, pl.ds(pl.multiple_of(p.other * 128, 128), 128)]
            links.copy(67 + (p.other - p.c + 16) % 16, piece, att_ref.at[p.c], on_ctx(p.other)).start()

        for s, stages in plan.items():

            @pl.when(i == s)
            def _():
                next(stages)

        return 0

    lax.fori_loop(0, 8, attend, 0)
    saves += [
        pltpu.make_async_copy(src, dst, local.at[26 + n])
        for n, (src, dst) in enumerate((
            (qt_ref, qt_out), (kt_ref, kt_out), (qr_ref, qr_out), (kr_ref, kr_out),
            (vr_ref, vr_out), (ot_ref, ot_out), (lse_ref, lse_out),
        ))
    ]
    for copy in saves[16:]:
        copy.start()
    others = [p.twin] + [p.planes[d] for d in (3, 1, 2)] + [p.twin_planes[d] for d in (3, 1, 2)]
    for i, f in enumerate(others):
        links.put(60 + i, out_half(f, p.k), out_half(f, p.k), on_ctx(p.other))
    for d in range(1, 16):
        links.got(67 + d, att_ref.at[p.ring[16 - d]])
        links.open.append((67 + d, ob.at[:, pl.ds(0, 128)]))
    for copy in locals_:
        copy.wait()
    for i, f in enumerate(others):
        links.got(60 + i, out_half(f, 1 - p.k))

    gain = wq_ref[pl.ds(193, 1), :].astype(F32)
    att = att_ref[...].reshape(1024, 128)
    h1 = h_ref[...].astype(F32) + tn(att, woutall[...])
    h1_ref[...] = h1
    xhat, _unused = normalize(h1)
    nall[p.t] = (xhat * gain).astype(BF16)
    gather = gather_column(p, links, 90, nall.at[p.t], nall, 128)
    ready = next(gather)
    next(gather_gu)
    next(gather_down)
    pick = iota((UNITS, 384), 1)
    row = iota((UNITS, 1), 0)
    want = jnp.where(row < 328, row + 7 * shard_of(row), -1)
    down_w[...] = nn(jnp.where(pick == want, 1.0, 0.0).astype(BF16), downall[...]).astype(BF16)
    for _ in gather_dy:
        pass

    def feed(b, other):
        n2 = jnp.concatenate([nall[b], nall[other]], axis=0)
        gu = nt(gu_ref[...], n2)
        d_act = nt(down_w[...], jnp.concatenate([dyall[b], dyall[other]], axis=0))
        gate, up = gu[:UNITS], gu[UNITS:]
        cdf = 0.5 * (1.0 + lax.erf(gate * 2.0 ** (-0.5)))
        gelu = gate * cdf
        pdf = jnp.exp(-0.5 * gate * gate) * (2.0 * np.pi) ** (-0.5)
        d_gate = d_act * up * (cdf + gate * pdf)
        d_gu = jnp.concatenate([d_gate, d_act * gelu], axis=0).astype(BF16)
        activated = (gelu * up).astype(BF16)
        d_n2 = tn(d_gu, gu_ref[...]).astype(BF16)
        for i, block in enumerate((b, other)):
            at = pl.ds(pl.multiple_of(block * 128, 128), 128)
            act[:, at] = activated[:, 128 * i : 128 * i + 128]
            dgu[:, at] = d_gu[:, 128 * i : 128 * i + 128]
            part[block] = d_n2[128 * i : 128 * i + 128]

    waiting = list(ready)
    for found in gather:
        waiting += found
        while len(waiting) > 1:
            feed(waiting.pop(0), waiting.pop(0))
    scatter = scatter_column(p, links, 109, part, total, core_in, far, 128)
    next(scatter)
    next(scatter)
    ggain = []
    for half in range(2):
        cols = pl.ds(512 * half, 512)
        g = nn(dgu[...], nall[:, :, cols].reshape(1024, 512))
        ggu[:, cols] = g.astype(BF16)
        ggain.append(jnp.sum(g * gu_ref[:, cols].astype(F32), axis=0, keepdims=True))
    ggain_ref[...] = jnp.concatenate(ggain, axis=1) / gain
    sum_gu = scatter_fsdp(
        p, links, 140, lambda f: ggu.at[:, lanes_of(f)], gu_along, gu_across, gu_keep,
        gusum_ref, 2 * UNITS,
    )
    next(sum_gu)
    next(scatter)
    row = iota((384, 1), 0)
    shard = row // 48
    place = row - 48 * shard
    want = jnp.where(place < 41, 41 * shard + place, -1)
    spread = jnp.where(iota((384, UNITS), 1) == want, 1.0, 0.0).astype(BF16)
    for half in range(2):
        cols = pl.ds(512 * half, 512)
        g = nn(act[...], dyall[:, :, cols].reshape(1024, 512)).astype(BF16)
        gdown_ref[:, cols] = nn(spread, g).astype(BF16)

    def down(b, _):
        at = pl.ds(pl.multiple_of(b * 128, 128), 128)
        downsum[b] = tn(act[:, at], down_w[...]).astype(BF16)
        return 0

    lax.fori_loop(0, 8, down, 0)
    sum_down = scatter_column(p, links, 147, downsum, down_total, core_down, far_down, 128)
    next(sum_down)
    next(scatter, None)
    h1 = h1_ref[...]
    xhat, inv = normalize(h1)
    d_h1 = dy_ref[...].astype(F32) + norm_back(total[...], xhat, inv, gain)
    dh1_ref[...] = d_h1
    d_h1_b = d_h1.astype(BF16)
    dat[...] = nt(woutall[...], d_h1_b).astype(BF16).reshape(16, 64, 128)
    lanes = pl.ds(pl.multiple_of(p.c * 128, 128), 128)
    for d in range(1, 16):
        links.put(124 + d, dat.at[p.ring[d]], dot_ref.at[:, lanes], on_ctx(p.ring[d]))
    dot_ref[:, lanes] = dat[p.c]
    next(sum_down)
    att = att_ref[...]
    for g in range(4):
        rows = att[4 * g : 4 * g + 4].reshape(256, 128)
        block = nn(rows, d_h1_b).reshape(2, 16, 8, 1024).transpose(1, 0, 2, 3)
        gout_ref[:, pl.ds(16 * g, 16), :] = block.reshape(16, 16, 1024).astype(BF16)
    next(sum_down)
    next(sum_gu)
    for d in range(1, 16):
        links.got(124 + d, dot_ref.at[:, pl.ds(pl.multiple_of(p.ring[16 - d] * 128, 128), 128)])
    next(sum_down, None)
    result_ref[...] = (h1_ref[...] + down_total[...]).astype(BF16)
    next(sum_gu, None)
    for copy in saves:
        copy.wait()
    links.close()


def shape(dims, dtype=BF16):
    return jax.ShapeDtypeStruct(dims, dtype)


def front(hidden, grad, wqkv, wout, wgu, wdown, g1, g2, cos, sin):
    heads = [
        shape((64, 2048)), shape((64, 2048)), shape((2048, 64)), shape((2048, 64)),
        shape((2048, 64)), shape((64, 2048), F32), shape((1, 2048), F32),
    ]
    blocks = pltpu.VMEM((16, 128, 1024), BF16)
    column = pltpu.VMEM((8, 128, 1024), BF16)
    return pl.pallas_call(
        front_kernel,
        name="front",
        out_shape=(
            shape((208, 1024)), shape((128, 1024)), shape((128, 1024), F32),
            shape((64, 2048)), shape((2 * UNITS, 128)), shape((384, 1024)),
            shape((1, 1024), F32), shape((16, 64, 1024)), shape((16, 128, 1024)), *heads,
        ),
        in_specs=[VMEM, VMEM, ANY] + [VMEM] * 7,
        out_specs=(VMEM,) * 8 + (ANY,) * 8,
        scratch_shapes=[
            blocks, blocks, column, column, column, column,
            pltpu.VMEM((64, 2048), BF16),
            pltpu.VMEM((64, 2048), BF16),
            pltpu.VMEM((64, 2048), BF16),
            pltpu.VMEM((2048, 64), BF16),
            pltpu.VMEM((2048, 64), BF16),
            pltpu.VMEM((2048, 64), BF16),
            pltpu.VMEM((64, 2048), F32),
            pltpu.VMEM((1, 2048), F32),
            pltpu.VMEM((3, 128, 128), BF16),
            pltpu.VMEM((UNITS, 128), F32),
            pltpu.VMEM((208, 128), BF16),
            pltpu.VMEM((2 * UNITS, 128), BF16),
            pltpu.VMEM((48, 1024), BF16),
            pltpu.VMEM((64, 2048), BF16),
            pltpu.VMEM((16, 64, 128), BF16),
            pltpu.VMEM((16, 64, 128), BF16),
            pltpu.VMEM((1024, 1024), BF16),
            pltpu.VMEM((2 * UNITS, 1024), BF16),
            pltpu.VMEM((384, 1024), BF16),
            pltpu.VMEM((UNITS, 1024), BF16),
            pltpu.VMEM((UNITS, 1024), BF16),
            pltpu.VMEM((2 * UNITS, 1024), BF16),
            pltpu.VMEM((128, 1024), F32),
        ] + column_scratch(128, 1024) + [pltpu.VMEM((2 * UNITS, 1024), BF16)]
        + fsdp_scratch(2 * UNITS, 128)
        + [pltpu.VMEM((128, 1024), F32), pltpu.VMEM((128, 1024), F32)]
        + column_scratch(128, 1024) + [dma(155), dma(155), dma(33)],
        compiler_params=params(1),
    )(hidden, grad, wqkv, wout, wgu, wdown, g1, g2, cos, sin)


LATE = 288


def backward_kernel(
    k_ref, v_ref, kt_ref, qt_ref, q_ref, dot_ref, ot_ref, lse_ref, cos_ref, sin_ref,
    n1_ref, wq_ref, h_ref, dh1_ref, gu_sum, gdown_ref, ggain_ref, gout_ref,
    dinput_ref, gupieces_ref, rowpieces_ref, latepieces_ref,
    n1, gsum, dproj, dk, dv, part, late, gu_pair, gu_mine, row_pair, row_mine,
    total, gout, row_sum, late_sum, *rest,
):
    (
        core_b, far_b, core_c, far_c,
        row_along, row_across, row_keep,
        late_along, late_across, late_keep, send, recv, local,
    ) = rest
    p = Place()
    links = Links(
        send, recv, on_ctx(p.other),
        [part.at[0], part.at[0, pl.ds(0, 64)], part.at[0, pl.ds(0, 32)], row_keep,
         gu_mine, gu_mine.at[pl.ds(0, 176)], row_mine, row_mine.at[pl.ds(0, 48)], late_keep, late_keep.at[pl.ds(0, LATE // 2)]],
    )
    loads = [
        pltpu.make_async_copy(gout_ref, gsum, local.at[5]),
        pltpu.make_async_copy(n1_ref, n1, local.at[1]),
    ]
    for copy in loads:
        copy.start()
    greet(ctx_peers(p) + p.fsdp_peers)
    loads[0].wait()
    sum_out = scatter_ctx(p, links, 16, gsum, gout, core_b, far_b, 64)
    next(sum_out)
    sum_rows = scatter_fsdp(
        p, links, 55, lambda f: gdown_ref.at[pl.ds(pl.multiple_of(f * 48, 16), 48)],
        row_along, row_across, row_keep, row_sum, 48,
    )
    next(sum_rows)
    all_gu = gather_ctx(p, links, 69, gu_mine, gupieces_ref, UNITS)
    mine = [
        pltpu.make_async_copy(gu_mine, gupieces_ref.at[p.c], local.at[2]),
        pltpu.make_async_copy(row_mine, rowpieces_ref.at[p.c], local.at[3]),
        pltpu.make_async_copy(late_sum, latepieces_ref.at[p.c], local.at[4]),
    ]

    other_half = pl.ds(pl.multiple_of(UNITS * (1 - p.xl), 16), UNITS)
    own_half = pl.ds(pl.multiple_of(UNITS * p.xl, 16), UNITS)
    other_cols = pl.ds(pl.multiple_of(512 * (1 - p.xl), 128), 512)
    to_x = on_ctx(p.same("X"))

    links.put(142, gu_sum.at[other_half], gu_pair, to_x)

    def begin_gu():
        links.got(142, gu_pair)
        add_rows(gu_mine, [(gu_sum.at[own_half], 0), (gu_pair, 0)], UNITS)
        next(all_gu)

    def swap_rows():
        next(sum_rows, None)
        links.put(143, row_sum.at[:, other_cols], row_pair, to_x)

    def step(stages):
        return lambda: next(stages, None)

    plan = {
        0: [step(sum_out)], 1: [begin_gu], 3: [step(sum_out)], 4: [step(sum_out), step(sum_rows)],
        5: [step(sum_out), step(all_gu)], 6: [step(sum_out), swap_rows], 7: [step(all_gu)],
    }
    dk[...] = jnp.zeros_like(dk)
    dv[...] = jnp.zeros_like(dv)

    def attend(i, _):
        at = pl.ds(pl.multiple_of(i * Q_BLOCK, Q_BLOCK), Q_BLOCK)
        scores = nn(k_ref[...], qt_ref[:, at])
        prob = jnp.exp(scores - lse_ref[:, at])
        dout = dot_ref[:, at]
        d_prob = nn(v_ref[...], dout)
        delta = jnp.sum(dout.astype(F32) * ot_ref[:, at], axis=0, keepdims=True)
        d_scores = (prob * (d_prob - delta)).astype(BF16)
        d_query = nn(kt_ref[...], d_scores) * 0.125
        dproj[pl.ds(0, 64), at] = unrope_t(d_query, cos_ref[:, at], sin_ref[:, at]).astype(BF16)
        dk[...] += nn(d_scores, q_ref[at, :])
        dv[...] += nn(prob.astype(BF16), dout.astype(F32).T.astype(BF16))
        for n, steps in plan.items():

            @pl.when(i == n)
            def _():
                for run in steps:
                    run()

        return 0

    lax.fori_loop(0, 8, attend, 0)

    def project(b, _):
        at = pl.ds(pl.multiple_of(b * 128, 128), 128)
        d_key = unrope_t(dk[at, :].T, cos_ref[:, at], sin_ref[:, at])
        dproj[pl.ds(64, 64), at] = d_key.astype(BF16)
        dproj[pl.ds(128, 64), at] = dv[at, :].T.astype(BF16)
        part[b] = tn(dproj[:, at], wq_ref[pl.ds(0, 192), :]).astype(BF16)
        return 0

    lax.fori_loop(0, 16, project, 0)
    back = lockstep(
        scatter_ctx(p, links, 32, part, total, core_c, far_c, 64, 0),
        scatter_ctx(p, links, 126, part, total, core_c, far_c, 64, 64),
    )
    next(back)
    next(back)
    next(all_gu)
    links.got(143, row_pair)
    for half in range(2):
        own_lanes = pl.ds(pl.multiple_of(512 * p.xl + 256 * half, 128), 256)
        add_rows(
            row_mine.at[pl.ds(48 * half, 48)],
            [(row_sum.at[:, own_lanes], 0), (row_pair.at[:, pl.ds(256 * half, 256)], 0)], 48,
        )
    all_rows = gather_ctx(p, links, 88, row_mine, rowpieces_ref, 96)
    next(all_rows)
    loads[1].wait()
    gain = wq_ref[pl.ds(192, 1), :].astype(F32)
    late[...] = jnp.zeros_like(late)
    ggain = []
    for half in range(2):
        cols = pl.ds(512 * half, 512)
        g = nn(dproj[...], n1[:, :, cols].reshape(2048, 512))
        late[pl.ds(0, 192), cols] = g.astype(BF16)
        ggain.append(jnp.sum(g * wq_ref[pl.ds(0, 192), cols].astype(F32), axis=0, keepdims=True))
    gain_row = jnp.concatenate(ggain, axis=1) / gain
    row = iota((16, 1024), 0)
    gains = jnp.where(row == 0, gain_row, 0.0)
    late[pl.ds(192, 16), :] = jnp.where(row == 1, ggain_ref[...], gains).astype(BF16)
    for f in range(8):
        for g in range(4):
            pair = gout[pl.ds(8 * f, 8), pl.ds(256 * g, 256)]
            late[pl.ds(208 + 16 * g, 16), pl.ds(128 * f, 128)] = jnp.concatenate(
                [pair[:, :128], pair[:, 128:]], axis=0
            ).astype(BF16)
    sum_late = scatter_fsdp(
        p, links, 62, lambda f: late.at[:, lanes_of(f)],
        late_along, late_across, late_keep, late_sum, LATE,
    )
    next(sum_late)
    next(back)
    next(all_gu)
    next(all_rows)
    next(back)
    next(sum_late)
    next(back)
    next(all_gu)
    next(all_rows)
    next(sum_late, None)
    all_late = gather_ctx(p, links, 107, late_sum, latepieces_ref, LATE)
    next(all_late)
    next(back, None)
    xhat, inv = normalize(h_ref[...].astype(F32))
    d_in = norm_back(total[...], xhat, inv, gain)
    dinput_ref[...] = (dh1_ref[...] + d_in).astype(BF16)
    for copy in mine:
        copy.start()
    run_all([all_gu, all_late, all_rows])
    for copy in mine:
        copy.wait()
    links.close()


def backward(*args):
    return pl.pallas_call(
        backward_kernel,
        name="backward",
        out_shape=(
            shape((128, 1024)), shape((16, UNITS, 128)),
            shape((16, 96, 256)), shape((16, LATE, 128)),
        ),
        in_specs=[VMEM] * 10 + [ANY] + [VMEM] * 6 + [ANY],
        out_specs=(VMEM, ANY, ANY, ANY),
        scratch_shapes=[
            pltpu.VMEM((16, 128, 1024), BF16),
            pltpu.VMEM((16, 64, 1024), BF16),
            pltpu.VMEM((192, 2048), BF16),
            pltpu.VMEM((2048, 64), F32),
            pltpu.VMEM((2048, 64), F32),
            pltpu.VMEM((16, 128, 1024), BF16),
            pltpu.VMEM((LATE, 1024), BF16),
            pltpu.VMEM((UNITS, 128), BF16),
            pltpu.VMEM((UNITS, 128), BF16),
            pltpu.VMEM((48, 512), BF16),
            pltpu.VMEM((96, 256), BF16),
            pltpu.VMEM((128, 1024), F32),
            pltpu.VMEM((64, 1024), F32),
            pltpu.VMEM((48, 1024), BF16),
            pltpu.VMEM((LATE, 128), BF16),
        ] + scatter_scratch(64, 1024) + scatter_scratch(128, 1024)
        + fsdp_scratch(48, 1024) + fsdp_scratch(LATE, 128)
        + [dma(144), dma(144), dma(6)],
        compiler_params=params(3),
    )(*args)


def fsdp_scratch(rows, cols):
    return [
        pltpu.VMEM((6, rows, cols), BF16),
        pltpu.VMEM((2, rows, cols), BF16),
        pltpu.VMEM((rows, cols), BF16),
    ]


def nt(a, b):
    return lax.dot_general(a, b, (((1,), (1,)), ((), ())), preferred_element_type=F32)


def tn(a, b):
    return lax.dot_general(a, b, (((0,), (0,)), ((), ())), preferred_element_type=F32)


def nn(a, b):
    return jnp.dot(a, b, preferred_element_type=F32)


def normalize(v):
    centered = v - jnp.mean(v, axis=-1, keepdims=True)
    inv = lax.rsqrt(jnp.mean(centered * centered, axis=-1, keepdims=True) + EPSILON)
    return centered * inv, inv


def norm_back(e, xhat, inv, gain):
    eg = e * gain
    return inv * (
        eg - jnp.mean(eg, axis=-1, keepdims=True)
        - xhat * jnp.mean(eg * xhat, axis=-1, keepdims=True)
    )


def rope_t(v, cos, sin):
    a, b = v[:32], v[32:]
    return jnp.concatenate([a * cos - b * sin, b * cos + a * sin], axis=0)


def unrope_t(v, cos, sin):
    a, b = v[:32], v[32:]
    return jnp.concatenate([a * cos + b * sin, b * cos - a * sin], axis=0)


def rope_tables():
    inverse = np.float32(ROPE_BASE) ** (-(np.arange(32, dtype=np.float32) * 2.0) / 64)
    angles = inverse[:, None].astype(np.float32) * np.arange(2048, dtype=np.float32)[None, :]
    return np.cos(angles).astype(np.float32), np.sin(angles).astype(np.float32)


def body(
    hidden_in, qkv_weight, out_weight, gate_up_weight, down_weight, attn_gain, mlp_gain, out_grad
):
    hidden_b, grad_b = hidden_in[0], out_grad[0]
    cos, sin = rope_tables()
    cos, sin = jnp.asarray(cos), jnp.asarray(sin)
    (
        w_q, result, d_h1, do_t, gu_sum, g_down, g_gain_two, g_out,
        n1, q_t, k_t, queries, keys, values, o_t, lse,
    ) = front(
        hidden_b, grad_b, qkv_weight, out_weight, gate_up_weight, down_weight,
        attn_gain[None], mlp_gain[None], cos, sin,
    )
    input_grad, gu_pieces, row_pieces, late_pieces = backward(
        keys, values, k_t, q_t, queries, do_t, o_t, lse, cos, sin,
        n1, w_q, hidden_b, d_h1, gu_sum, g_down, g_gain_two, g_out,
    )
    late_pieces = late_pieces.astype(F32)
    qkv_grad = (
        late_pieces[:, :192].reshape(16, 3, 64, 128).transpose(3, 1, 0, 2).reshape(128, 3072)
    )
    gain_grads = jnp.sum(late_pieces[:, 192:194], axis=0)
    gate_up = gu_pieces.reshape(2, 8, UNITS, 128)[:, :, :328].transpose(0, 2, 1, 3)
    gate_up_grad = gate_up.reshape(5248, 128).astype(F32).T
    down_rows = row_pieces.reshape(2, 8, 2, 48, 256)[:, :, :, :41].transpose(3, 1, 0, 2, 4)
    down_grad = down_rows.reshape(328, 1024).astype(F32)
    out_rows = late_pieces[:, 208:272].reshape(16, 8, 8, 128).transpose(0, 2, 1, 3)
    out_weight_grad = out_rows.reshape(128, 1024)
    return (
        result[None], input_grad[None], qkv_grad, out_weight_grad, gate_up_grad, down_grad,
        gain_grads[0], gain_grads[1],
    )


def solution(mesh):
    return jax.shard_map(
        body,
        mesh=mesh,
        in_specs=(
            P("fsdp", "ctx", None), P("fsdp", None), P("fsdp", None), P("fsdp", None),
            P("fsdp", None), P("fsdp"), P("fsdp"), P("fsdp", "ctx", None),
        ),
        out_specs=(
            P("fsdp", "ctx", None), P("fsdp", "ctx", None), P("fsdp", None), P("fsdp", None),
            P("fsdp", None), P("fsdp", None), P("fsdp"), P("fsdp"),
        ),
        check_vma=False,
    )
```

```python
import jax
import jax.numpy as jnp
import numpy as np
from jax import lax
from jax.experimental import pallas as pl
from jax.experimental.pallas import tpu as pltpu
from jax.sharding import PartitionSpec as P

HEADS = 16
EPSILON = 1e-05
ROPE_BASE = 160000.0
F32 = jnp.float32
BF16 = jnp.bfloat16
MESH = pl.DeviceIdType.MESH
ANY = pl.BlockSpec(memory_space=pl.ANY)
VMEM = pl.BlockSpec(memory_space=pltpu.VMEM)
MIB = 1024 * 1024


class Place:
    def __init__(self):
        c = lax.axis_index("ctx")
        self.c = c
        self.f = lax.axis_index("fsdp")
        k = c % 2
        y = (c // 2) % 4
        xl = c // 8
        self.k = k

        def at(x, row):
            return x * 4 + row % 4

        ox = 1 - xl
        self.other = c + 1 - 2 * k
        self.chip = {
            "S": at(xl, y),
            "P": at(xl, y + 1),
            "M": at(xl, y + 3),
            "F": at(xl, y + 2),
            "X": at(ox, y),
            "XP": at(ox, y + 1),
            "XM": at(ox, y + 3),
            "XF": at(ox, y + 2),
        }

        self.same_core = {name: chip * 2 + k for name, chip in self.chip.items()}
        self.cross_core = {name: chip * 2 + 1 - k for name, chip in self.chip.items()}
        self.xl = xl
        self.t = c % 8
        self.column = {name: chip % 4 * 2 + k for name, chip in self.chip.items()}
        self.cross_column = {name: chip % 4 * 2 + 1 - k for name, chip in self.chip.items()}
        self.ring = [(c + d) % 16 for d in range(16)]
        z, xh = self.f // 2, self.f % 2
        self.twin = z * 2 + 1 - xh
        self.planes = [(z + d) % 4 * 2 + xh for d in range(4)]
        self.twin_planes = [(z + d) % 4 * 2 + 1 - xh for d in range(4)]
        self.fsdp_peers = [{"fsdp": i} for i in [self.twin] + self.planes[1:]]

    def same(self, name):
        return self.same_core[name]

    def cross(self, name):
        return self.cross_core[name]


def lanes_of(f):
    return pl.ds(pl.multiple_of(f * 128, 128), 128)


def on_ctx(index):
    return {"ctx": index}


def greet(peers):
    barrier = pltpu.get_barrier_semaphore()
    for peer in peers:
        pl.semaphore_signal(barrier, inc=1, device_id=peer, device_id_type=MESH)
    pl.semaphore_wait(barrier, len(peers))


class Links:
    def __init__(self, send, recv, peer, like=()):
        self.send, self.recv, self.peer = send, recv, peer
        self.like = {ref.shape: ref for ref in like}
        self.open = []

    def copy(self, i, src, dst, peer):
        return pltpu.make_async_remote_copy(
            src_ref=src, dst_ref=dst, send_sem=self.send.at[i], recv_sem=self.recv.at[i],
            device_id=peer, device_id_type=MESH,
        )

    def put(self, i, src, dst, peer):
        self.copy(i, src, dst, peer).start()
        self.open.append((i, self.like.get(src.shape, src)))

    def got(self, i, dst):
        self.copy(i, dst, dst, self.peer).wait_recv()

    def close(self, below=1000):
        for i, ref in self.open:
            if i < below:
                self.copy(i, ref, ref, self.peer).wait_send()
        self.open = [(i, ref) for i, ref in self.open if i >= below]


def ctx_peers(p):
    return [on_ctx(p.other), on_ctx(p.same("P")), on_ctx(p.same("M")), on_ctx(p.same("X"))]


GATHER_COPIES = 19


def gather_ctx(p, links, base, own, out, rows, off=None):
    half = rows // 2
    top, bottom = pl.ds(0, half), pl.ds(half, half)
    to_p, to_m, to_x, to_k = (
        on_ctx(p.same("P")), on_ctx(p.same("M")), on_ctx(p.same("X")), on_ctx(p.other),
    )

    def rows_of(ref):
        return ref if off is None else ref.at[pl.ds(off, rows)]

    own = rows_of(own)
    mine = rows_of(out.at[p.c])

    def put(i, src, dst, peer):
        links.put(base + i, src, dst, peer)

    def got(i, dst):
        links.got(base + i, dst)

    def block(name):
        return rows_of(out.at[p.same(name)])

    def cross(name):
        return rows_of(out.at[p.cross(name)])

    put(0, own, mine, to_p)
    put(1, own, mine, to_m)
    put(2, own, mine, to_x)
    put(3, own, mine, to_k)
    yield [p.same("S")]
    got(0, block("M"))
    put(4, block("M").at[top], block("M").at[top], to_p)
    put(10, block("M"), block("M"), to_k)
    got(1, block("P"))
    put(5, block("P").at[bottom], block("P").at[bottom], to_m)
    put(11, block("P"), block("P"), to_k)
    got(2, block("X"))
    put(6, block("X"), block("X"), to_p)
    put(7, block("X"), block("X"), to_m)
    put(12, block("X"), block("X"), to_k)
    got(3, cross("S"))
    yield [p.same("M"), p.same("P"), p.same("X"), p.cross("S")]
    for i, part, to_core in ((4, top, 13), (5, bottom, 14)):
        piece = block("F").at[part]
        got(i, piece)
        put(4 + i, piece, piece, to_x)
        put(to_core, piece, piece, to_k)
    got(10, cross("M"))
    got(11, cross("P"))
    yield [p.same("F"), p.cross("M"), p.cross("P")]
    got(6, block("XM"))
    put(15, block("XM"), block("XM"), to_k)
    got(7, block("XP"))
    put(16, block("XP"), block("XP"), to_k)
    got(12, cross("X"))
    got(13, cross("F").at[top])
    got(14, cross("F").at[bottom])
    yield [p.same("XM"), p.same("XP"), p.cross("X"), p.cross("F")]
    for i, part, to_core in ((8, top, 17), (9, bottom, 18)):
        piece = block("XF").at[part]
        got(i, piece)
        put(to_core, piece, piece, to_k)
    got(15, cross("XM"))
    got(16, cross("XP"))
    yield [p.same("XF"), p.cross("XM"), p.cross("XP")]
    got(17, cross("XF").at[top])
    got(18, cross("XF").at[bottom])
    yield [p.cross("XF")]


def gather_column(p, links, base, own, out, rows):
    half = rows // 2
    top, bottom = pl.ds(0, half), pl.ds(half, half)
    to_p, to_m, to_k = on_ctx(p.same("P")), on_ctx(p.same("M")), on_ctx(p.other)
    same, cross = p.column, p.cross_column

    def put(i, src, dst, peer):
        links.put(base + i, src, dst, peer)

    def got(i, dst):
        links.got(base + i, dst)

    mine = out.at[same["S"]]
    put(0, own, mine, to_p)
    put(1, own, mine, to_m)
    put(2, own, mine, to_k)
    yield [same["S"]]
    got(0, out.at[same["M"]])
    put(3, out.at[same["M"], top], out.at[same["M"], top], to_p)
    put(5, out.at[same["M"]], out.at[same["M"]], to_k)
    got(1, out.at[same["P"]])
    put(4, out.at[same["P"], bottom], out.at[same["P"], bottom], to_m)
    put(6, out.at[same["P"]], out.at[same["P"]], to_k)
    got(2, out.at[cross["S"]])
    yield [cross["S"], same["M"], same["P"]]
    got(5, out.at[cross["M"]])
    got(3, out.at[same["F"], top])
    put(7, out.at[same["F"], top], out.at[same["F"], top], to_k)
    got(4, out.at[same["F"], bottom])
    put(8, out.at[same["F"], bottom], out.at[same["F"], bottom], to_k)
    got(6, out.at[cross["P"]])
    yield [same["F"], cross["M"], cross["P"]]
    got(7, out.at[cross["F"], top])
    got(8, out.at[cross["F"], bottom])
    yield [cross["F"]]


def scatter_column(p, links, base, part, total, core_in, far, rows):
    half = rows // 2
    whole, top, bottom = pl.ds(0, rows), pl.ds(0, half), pl.ds(half, half)
    to_p, to_m, to_k = on_ctx(p.same("P")), on_ctx(p.same("M")), on_ctx(p.other)
    order = ("F", "P", "M", "S")
    mid = [part.at[p.column[name]] for name in order]

    def put(i, src, dst, peer):
        links.put(base + i, src, dst, peer)

    def got(i, dst):
        links.got(base + i, dst)

    for i, name in enumerate(order):
        put(i, part.at[p.cross_column[name]], core_in.at[i], to_k)
    yield

    def pair(i):
        got(i, core_in.at[i])
        return [(mid[i], 0), (core_in.at[i], 0)]

    add_rows(mid[0], pair(0), rows)
    put(4, mid[0].at[top], far.at[0, top], to_p)
    put(5, mid[0].at[bottom], far.at[0, bottom], to_m)
    yield
    terms = pair(1)
    got(4, far.at[0, top])
    add_rows(mid[1], terms + [(far.at[0], 0)], half)
    add_rows(mid[1], terms, half, half)
    put(6, mid[1], far.at[1], to_p)
    terms = pair(2)
    got(5, far.at[0, bottom])
    add_rows(mid[2], terms, half)
    add_rows(mid[2], terms + [(far.at[0], 0)], half, half)
    put(7, mid[2], far.at[2], to_m)
    yield
    terms = pair(3)
    got(6, far.at[1])
    got(7, far.at[2])
    add_rows(total, terms + [(far.at[1], 0), (far.at[2], 0)], rows)


def gather_fsdp(p, links, base, own, slot):
    links.put(base, own, slot(p.f), {"fsdp": p.twin})
    for d in (1, 3, 2):
        links.put(base + d, own, slot(p.f), {"fsdp": p.planes[d]})
    yield []
    twin = slot(p.twin)
    links.got(base, twin)
    for d in (1, 3, 2):
        links.put(base + 3 + d, twin, twin, {"fsdp": p.planes[d]})
    yield [p.twin]
    for d in (1, 3, 2):
        links.got(base + d, slot(p.planes[4 - d]))
    for d in (1, 3, 2):
        links.got(base + 3 + d, slot(p.twin_planes[4 - d]))
    yield [p.planes[d] for d in (3, 1, 2)] + [p.twin_planes[d] for d in (3, 1, 2)]


def gather_ring(p, links, base, own, slot):
    up, down = {"fsdp": p.planes[1]}, {"fsdp": p.planes[3]}
    links.put(base + 1, own, slot(p.f), up)
    links.put(base + 2, own, slot(p.f), down)
    links.put(base, own, slot(p.f), {"fsdp": p.twin})
    yield []
    links.got(base, slot(p.twin))
    links.put(base + 4, slot(p.twin), slot(p.twin), up)
    links.put(base + 5, slot(p.twin), slot(p.twin), down)
    below = slot(p.planes[3])
    links.got(base + 1, below)
    links.put(base + 3, below, below, up)
    yield []
    above = slot(p.twin_planes[1])
    links.got(base + 5, above)
    links.put(base + 6, above, above, down)
    yield []
    links.got(base + 2, slot(p.planes[1]))
    links.got(base + 3, slot(p.planes[2]))
    links.got(base + 4, slot(p.twin_planes[3]))
    links.got(base + 6, slot(p.twin_planes[2]))
    yield []


def scatter_fsdp(p, links, base, part, along, across, keep, total, rows):
    for n, d in enumerate((1, 3, 2)):
        links.put(base + n, part(p.planes[d]), along.at[n], {"fsdp": p.planes[d]})
        links.put(base + 3 + n, part(p.twin_planes[d]), along.at[3 + n], {"fsdp": p.planes[d]})
    yield
    for n in range(6):
        links.got(base + n, along.at[n])
    terms = [(along.at[3 + n], 0) for n in range(3)]
    add_rows(across.at[0], [(part(p.twin), 0)] + terms, rows)
    links.put(base + 6, across.at[0], across.at[1], {"fsdp": p.twin})
    add_rows(keep, [(part(p.f), 0)] + [(along.at[n], 0) for n in range(3)], rows)
    yield
    links.got(base + 6, across.at[1])
    add_rows(total, [(keep, 0), (across.at[1], 0)], rows)


def run_all(stages):
    live = list(stages)
    while live:
        left = []
        for stage in live:
            try:
                next(stage)
                left.append(stage)
            except StopIteration:
                pass
        live = left


SCATTER_COPIES = 16
SCATTER_ORDER = ("XF", "XP", "XM", "F", "X", "P", "M", "S")


def add_rows(dst, terms, rows, at=0):
    step = 16

    def one(i, _):
        r = pl.ds(pl.multiple_of(i * step, step) + at, step)
        total = None
        for ref, _unused in terms:
            part = ref[r, :].astype(F32)
            total = part if total is None else total + part
        dst[r, :] = total.astype(dst.dtype)
        return 0

    lax.fori_loop(0, rows // step, one, 0)


def lockstep(*stages):
    while True:
        found = []
        ended = 0
        for one in stages:
            try:
                found += next(one) or []
            except StopIteration:
                ended += 1
        if ended == len(stages):
            return
        yield found


def scatter_ctx(p, links, base, part, total, core_in, far, rows, off=0):
    half = rows // 2
    to_p, to_m, to_x, to_k = (
        on_ctx(p.same("P")), on_ctx(p.same("M")), on_ctx(p.same("X")), on_ctx(p.other),
    )

    def put(i, src, dst, peer):
        links.put(base + i, src, dst, peer)

    def got(i, dst):
        links.got(base + i, dst)

    whole = pl.ds(off, rows)
    top, bottom = pl.ds(off, half), pl.ds(off + half, half)
    mid = [part.at[p.same(name)] for name in SCATTER_ORDER]
    for i, name in enumerate(SCATTER_ORDER):
        put(i, part.at[p.cross(name), whole], core_in.at[i, whole], to_k)
    yield

    def pair(i):
        got(i, core_in.at[i, whole])
        return [(mid[i], 0), (core_in.at[i], 0)]

    for i, peer in ((0, to_x), (1, to_p), (2, to_m)):
        add_rows(mid[i], pair(i), rows, off)
        put(8 + i, mid[i].at[whole], far.at[i, whole], peer)
    yield
    terms = pair(3)
    got(8, far.at[0, whole])
    add_rows(mid[3], terms + [(far.at[0], 0)], rows, off)
    put(11, mid[3].at[top], far.at[3, top], to_p)
    put(12, mid[3].at[bottom], far.at[3, bottom], to_m)
    yield
    terms = pair(4)
    got(9, far.at[1, whole])
    got(10, far.at[2, whole])
    add_rows(mid[4], terms + [(far.at[1], 0), (far.at[2], 0)], rows, off)
    put(13, mid[4].at[whole], far.at[4, whole], to_x)
    yield
    terms = pair(5)
    got(11, far.at[3, top])
    add_rows(mid[5], terms + [(far.at[3], 0)], half, off)
    add_rows(mid[5], terms, half, off + half)
    put(14, mid[5].at[whole], far.at[5, whole], to_p)
    terms = pair(6)
    got(12, far.at[3, bottom])
    add_rows(mid[6], terms, half, off)
    add_rows(mid[6], terms + [(far.at[3], 0)], half, off + half)
    put(15, mid[6].at[whole], far.at[6, whole], to_m)
    yield
    terms = pair(7)
    got(13, far.at[4, whole])
    got(14, far.at[5, whole])
    got(15, far.at[6, whole])
    add_rows(total, terms + [(far.at[4], 0), (far.at[5], 0), (far.at[6], 0)], rows, off)


def scatter_scratch(rows, cols):
    return [
        pltpu.VMEM((8, rows, cols), BF16),
        pltpu.VMEM((7, rows, cols), BF16),
    ]


def column_scratch(rows, cols):
    return [pltpu.VMEM((4, rows, cols), BF16), pltpu.VMEM((3, rows, cols), BF16)]


def dma(n):
    return pltpu.SemaphoreType.DMA((n,))


def params(cid, mib=60):
    return pltpu.CompilerParams(
        collective_id=cid, has_side_effects=True, vmem_limit_bytes=mib * MIB
    )


Q_BLOCK = 256
UNITS = 352
LATE = 288
B = 155


def pick_rows(select, matrix):
    return nt(select.astype(BF16), matrix).astype(BF16)


def ones_at(rows, cols, shift, valid):
    row = lax.broadcasted_iota(jnp.int32, (rows, cols), 0)
    col = lax.broadcasted_iota(jnp.int32, (rows, cols), 1)
    return jnp.where((col == row + shift) & (row < valid), 1.0, 0.0)


def shard_of(row):
    return sum(((row >= 41 * n).astype(jnp.int32) for n in range(1, 8)), 0)


def iota(dims, axis):
    return lax.broadcasted_iota(jnp.int32, dims, axis)


def layer_kernel(
    h_ref, dy_ref, wqkv_ref, wout_ref, wgu_ref, wdown_ref, g1_ref, g2_ref, cos_ref, sin_ref,
    result_ref, dinput_ref, gupieces_ref, rowpieces_ref, latepieces_ref,
    wq_ref, dh1, dout_t, gu_sum, gdown, ggain_two, gsum,
    hall, n1, dyall, nall, part, downsum, qt_ref, kt_ref, vt_ref, qr_ref, kr_ref, vr_ref, ot_ref, lse_ref,
    qkv_win, gu_acc, qkv_cols, gu_cols, down_rows, ob, att_ref, dat,
    woutall, gu_ref, downall, down_w, act, dgu, total, core_in, far, ggu, gu_along, gu_across, gu_keep,
    h1_keep, down_total, core_down, far_down,
    dproj, dk, dv, late, gu_pair, gu_mine, row_pair, row_mine, gout, row_sum, late_sum,
    core_b, far_b, core_c, far_c, row_along, row_across, row_keep, late_along, late_across, late_keep,
    send, recv, local,
):
    p = Place()
    links = Links(
        send, recv, on_ctx(p.other),
        [gu_keep, hall.at[0], hall.at[0, pl.ds(0, 64)], hall.at[0, pl.ds(0, 32)], qkv_cols, gu_cols,
         down_rows, ob.at[:, pl.ds(0, 128)], gu_mine, gu_mine.at[pl.ds(0, 176)], row_mine,
         row_mine.at[pl.ds(0, 48)], late_keep, late_keep.at[pl.ds(0, LATE // 2)]],
    )
    wins = [
        pltpu.make_async_copy(
            wqkv_ref.at[:, pl.ds(pl.multiple_of(part * 1024 + (p.c // 2) * 128, 128), 128)],
            qkv_win.at[part], local.at[part],
        )
        for part in range(3)
    ]
    own_h = pltpu.make_async_copy(h_ref, hall.at[p.c], local.at[5])
    for copy in wins:
        copy.start()
    own_h.start()
    for i in range(3):
        wins[i].wait()
        qkv_cols[pl.ds(64 * i, 64), :] = pick_rows(
            ones_at(64, 128, (p.c % 2) * 64, 64), qkv_win[i]
        )
    row = iota((16, 128), 0)
    gains = jnp.where(row == 0, g1_ref[...].astype(F32), 0.0)
    gains = jnp.where(row == 1, g2_ref[...].astype(F32), gains)
    qkv_cols[pl.ds(192, 16), :] = gains.astype(BF16)
    greet([on_ctx(p.ring[d]) for d in range(1, 16)] + p.fsdp_peers)
    gather_wq = gather_fsdp(p, links, 38, qkv_cols, lambda f: wq_ref.at[:, lanes_of(f)])
    next(gather_wq)
    gather_h = gather_ctx(p, links, 0, h_ref, hall, 128)
    ready = next(gather_h)
    lanes = lanes_of(p.f)
    half = pl.ds(pl.multiple_of(p.k * 64, 64), 64)

    def out_half(f, k):
        return woutall.at[pl.ds(pl.multiple_of(f * 128 + k * 64, 64), 64)]

    gather_out = gather_ring(p, links, 53, wout_ref.at[half], lambda f: out_half(f, p.k))
    next(gather_out)
    wq_ref[:, lanes] = qkv_cols[...]
    for half in range(2):
        row = iota((UNITS, 1), 0)
        want = jnp.where(row < 328, 8 * row + p.t + 64 * half, -1)
        gu_acc[...] = jnp.zeros_like(gu_acc)

        def pick(i, _):
            cols = pl.ds(pl.multiple_of(2560 * half + i * 896, 128), 896)
            select = jnp.where(iota((UNITS, 896), 1) + i * 896 == want, 1.0, 0.0)
            gu_acc[...] += nt(select.astype(BF16), wgu_ref[:, cols])
            return 0

        lax.fori_loop(0, 3, pick, 0)
        gu_cols[pl.ds(UNITS * half, UNITS), :] = gu_acc[...].astype(BF16)
    place = iota((48, 328), 0)
    select = (iota((48, 328), 1) == 8 * place + p.t) & (place < 41)
    down_rows[...] = nn(jnp.where(select, 1.0, 0.0).astype(BF16), wdown_ref[...]).astype(BF16)
    gather_gu = gather_ring(p, links, 45, gu_cols, lambda f: gu_ref.at[:, lanes_of(f)])
    next(gather_gu)

    def down_slot(f):
        return downall.at[pl.ds(pl.multiple_of(f * 48, 16), 48)]

    gather_down = gather_ring(p, links, 83, down_rows, down_slot)
    next(gather_down)
    own_h.wait()
    next(gather_wq)
    ready += next(gather_h)
    next(gather_wq)
    locals_ = [
        pltpu.make_async_copy(dy_ref, dyall.at[p.t], local.at[6]),
        pltpu.make_async_copy(
            wout_ref, woutall.at[pl.ds(pl.multiple_of(p.f * 128, 128), 128)], local.at[8]
        ),
        pltpu.make_async_copy(down_rows, down_slot(p.f), local.at[3]),
    ]
    for copy in locals_:
        copy.start()
    gu_ref[:, lanes] = gu_cols[...]
    next(gather_out)

    def project(b):
        gain = wq_ref[pl.ds(192, 1), :].astype(F32)

        def norm(i, _):
            r = pl.ds(pl.multiple_of(i * 32, 32), 32)
            xhat, _unused = normalize(hall[b, r, :].astype(F32))
            n1[b, r, :] = (xhat * gain).astype(BF16)
            return 0

        lax.fori_loop(0, 4, norm, 0)
        proj = nt(wq_ref[pl.ds(0, 192), :], n1[b])
        at = pl.ds(pl.multiple_of(b * 128, 128), 128)
        cos, sin = cos_ref[:, at], sin_ref[:, at]
        q = rope_t(proj[:64], cos, sin).astype(BF16) * jnp.asarray(0.125, BF16)
        k = rope_t(proj[64:128], cos, sin).astype(BF16)
        v = proj[128:192].astype(BF16)
        qt_ref[:, at] = q
        kt_ref[:, at] = k
        vt_ref[:, at] = v
        qr_ref[at, :] = q.astype(F32).T.astype(BF16)
        kr_ref[at, :] = k.astype(F32).T.astype(BF16)
        vr_ref[at, :] = v.astype(F32).T.astype(BF16)

    for b in ready:
        project(b)
    for b in next(gather_h):
        project(b)
    ready = next(gather_h)
    gather_dy = gather_column(p, links, 19, dy_ref, dyall, 128)
    next(gather_dy)
    for b in ready:
        project(b)
    while ready is not None:
        ready = next(gather_h, None)
        for b in ready or ():
            project(b)
    next(gather_out)
    next(gather_gu)
    next(gather_down)
    plan = {1: gather_dy, 2: gather_gu, 3: gather_down, 4: gather_out, 5: gather_dy}

    def attend(i, _):
        j = (p.c // 2 + i) % 8
        at = pl.ds(pl.multiple_of(j * Q_BLOCK, Q_BLOCK), Q_BLOCK)
        scores = nn(kr_ref[...], qt_ref[:, at])
        top = jnp.max(scores, axis=0, keepdims=True)
        weights = jnp.exp(scores - top)
        total = jnp.sum(weights, axis=0, keepdims=True)
        mixed = nn(vt_ref[...], weights.astype(BF16)) / total
        ot_ref[:, at] = mixed
        lse_ref[:, at] = top + jnp.log(total)
        ob[:, at] = mixed.astype(BF16)

        @pl.when(i > 0)
        def _():
            for e in range(2):
                to = 2 * j + e
                piece = ob.at[:, pl.ds(pl.multiple_of(to * 128, 128), 128)]
                links.copy(67 + 2 * i + e - p.k, piece, att_ref.at[p.c], on_ctx(to)).start()

        @pl.when(i == 0)
        def _():
            piece = ob.at[:, pl.ds(pl.multiple_of(p.c * 128, 128), 128)]
            copy = pltpu.make_async_copy(piece, att_ref.at[p.c], local.at[9])
            copy.start()
            copy.wait()
            piece = ob.at[:, pl.ds(pl.multiple_of(p.other * 128, 128), 128)]
            links.copy(67 + (p.other - p.c + 16) % 16, piece, att_ref.at[p.c], on_ctx(p.other)).start()

        for s, stages in plan.items():

            @pl.when(i == s)
            def _():
                next(stages)

        return 0

    lax.fori_loop(0, 8, attend, 0)
    others = [p.twin] + [p.planes[d] for d in (3, 1, 2)] + [p.twin_planes[d] for d in (3, 1, 2)]
    for i, f in enumerate(others):
        links.put(60 + i, out_half(f, p.k), out_half(f, p.k), on_ctx(p.other))
    for d in range(1, 16):
        links.got(67 + d, att_ref.at[p.ring[16 - d]])
        links.open.append((67 + d, ob.at[:, pl.ds(0, 128)]))
    for copy in locals_:
        copy.wait()
    for i, f in enumerate(others):
        links.got(60 + i, out_half(f, 1 - p.k))

    gain = wq_ref[pl.ds(193, 1), :].astype(F32)
    att = att_ref[...].reshape(1024, 128)
    h1 = h_ref[...].astype(F32) + tn(att, woutall[...])
    h1_keep[...] = h1
    xhat, _unused = normalize(h1)
    nall[p.t] = (xhat * gain).astype(BF16)
    gather = gather_column(p, links, 90, nall.at[p.t], nall, 128)
    ready = next(gather)
    next(gather_gu)
    next(gather_down)
    pick = iota((UNITS, 384), 1)
    row = iota((UNITS, 1), 0)
    want = jnp.where(row < 328, row + 7 * shard_of(row), -1)
    down_w[...] = nn(jnp.where(pick == want, 1.0, 0.0).astype(BF16), downall[...]).astype(BF16)
    for _ in gather_dy:
        pass

    def feed(b, other):
        n2 = jnp.concatenate([nall[b], nall[other]], axis=0)
        gu = nt(gu_ref[...], n2)
        d_act = nt(down_w[...], jnp.concatenate([dyall[b], dyall[other]], axis=0))
        gate, up = gu[:UNITS], gu[UNITS:]
        cdf = 0.5 * (1.0 + lax.erf(gate * 2.0 ** (-0.5)))
        gelu = gate * cdf
        pdf = jnp.exp(-0.5 * gate * gate) * (2.0 * np.pi) ** (-0.5)
        d_gate = d_act * up * (cdf + gate * pdf)
        d_gu = jnp.concatenate([d_gate, d_act * gelu], axis=0).astype(BF16)
        activated = (gelu * up).astype(BF16)
        d_n2 = tn(d_gu, gu_ref[...]).astype(BF16)
        for i, block in enumerate((b, other)):
            at = pl.ds(pl.multiple_of(block * 128, 128), 128)
            act[:, at] = activated[:, 128 * i : 128 * i + 128]
            dgu[:, at] = d_gu[:, 128 * i : 128 * i + 128]
            part[block] = d_n2[128 * i : 128 * i + 128]

    waiting = list(ready)
    for found in gather:
        waiting += found
        while len(waiting) > 1:
            feed(waiting.pop(0), waiting.pop(0))
    scatter = scatter_column(p, links, 109, part, total, core_in, far, 128)
    next(scatter)
    next(scatter)
    ggain = []
    for half in range(2):
        cols = pl.ds(512 * half, 512)
        g = nn(dgu[...], nall[:, :, cols].reshape(1024, 512))
        ggu[:, cols] = g.astype(BF16)
        ggain.append(jnp.sum(g * gu_ref[:, cols].astype(F32), axis=0, keepdims=True))
    ggain_two[...] = jnp.concatenate(ggain, axis=1) / gain
    sum_gu = scatter_fsdp(
        p, links, 140, lambda f: ggu.at[:, lanes_of(f)], gu_along, gu_across, gu_keep,
        gu_sum, 2 * UNITS,
    )
    next(sum_gu)
    next(scatter)
    row = iota((384, 1), 0)
    shard = row // 48
    place = row - 48 * shard
    want = jnp.where(place < 41, 41 * shard + place, -1)
    spread = jnp.where(iota((384, UNITS), 1) == want, 1.0, 0.0).astype(BF16)
    for half in range(2):
        cols = pl.ds(512 * half, 512)
        g = nn(act[...], dyall[:, :, cols].reshape(1024, 512)).astype(BF16)
        gdown[:, cols] = nn(spread, g).astype(BF16)

    def down(b, _):
        at = pl.ds(pl.multiple_of(b * 128, 128), 128)
        downsum[b] = tn(act[:, at], down_w[...]).astype(BF16)
        return 0

    lax.fori_loop(0, 8, down, 0)
    sum_down = scatter_column(p, links, 147, downsum, down_total, core_down, far_down, 128)
    next(sum_down)
    next(scatter, None)
    h1 = h1_keep[...]
    xhat, inv = normalize(h1)
    d_h1 = dy_ref[...].astype(F32) + norm_back(total[...], xhat, inv, gain)
    dh1[...] = d_h1
    d_h1_b = d_h1.astype(BF16)
    dat[...] = nt(woutall[...], d_h1_b).astype(BF16).reshape(16, 64, 128)
    lanes = pl.ds(pl.multiple_of(p.c * 128, 128), 128)
    for d in range(1, 16):
        links.put(124 + d, dat.at[p.ring[d]], dout_t.at[:, lanes], on_ctx(p.ring[d]))
    dout_t[:, lanes] = dat[p.c]
    att = att_ref[...]
    for g in range(4):
        rows = att[4 * g : 4 * g + 4].reshape(256, 128)
        block = nn(rows, d_h1_b).reshape(2, 16, 8, 1024).transpose(1, 0, 2, 3)
        gsum[:, pl.ds(16 * g, 16), :] = block.reshape(16, 16, 1024).astype(BF16)
    next(sum_down)

    sum_out = scatter_ctx(p, links, B + 16, gsum, gout, core_b, far_b, 64)
    next(sum_out)
    for d in range(1, 16):
        links.got(124 + d, dout_t.at[:, pl.ds(pl.multiple_of(p.ring[16 - d] * 128, 128), 128)])
    sum_rows = scatter_fsdp(
        p, links, B + 55, lambda f: gdown.at[pl.ds(pl.multiple_of(f * 48, 16), 48)],
        row_along, row_across, row_keep, row_sum, 48,
    )
    next(sum_rows)
    all_gu = gather_ctx(p, links, B + 69, gu_mine, gupieces_ref, UNITS)
    mine_copies = [
        pltpu.make_async_copy(gu_mine, gupieces_ref.at[p.c], local.at[2]),
        pltpu.make_async_copy(row_mine, rowpieces_ref.at[p.c], local.at[3]),
        pltpu.make_async_copy(late_sum, latepieces_ref.at[p.c], local.at[4]),
    ]

    other_half = pl.ds(pl.multiple_of(UNITS * (1 - p.xl), 16), UNITS)
    own_half = pl.ds(pl.multiple_of(UNITS * p.xl, 16), UNITS)
    other_cols = pl.ds(pl.multiple_of(512 * (1 - p.xl), 128), 512)
    to_x = on_ctx(p.same("X"))

    def swap_gu():
        next(sum_gu, None)
        links.put(B + 142, gu_sum.at[other_half], gu_pair, to_x)

    def begin_gu():
        links.got(B + 142, gu_pair)
        add_rows(gu_mine, [(gu_sum.at[own_half], 0), (gu_pair, 0)], UNITS)
        next(all_gu)

    def swap_rows():
        next(sum_rows, None)
        links.put(B + 143, row_sum.at[:, other_cols], row_pair, to_x)

    def step(stages):
        return lambda: next(stages, None)

    plan = {
        0: [step(sum_out)], 1: [step(sum_gu), step(sum_down)], 2: [step(sum_out)],
        3: [swap_gu, step(sum_down)], 4: [step(sum_out)], 5: [step(sum_out), begin_gu],
        6: [step(sum_out), step(sum_rows)], 7: [step(all_gu), swap_rows],
    }
    dk[...] = jnp.zeros_like(dk)
    dv[...] = jnp.zeros_like(dv)

    def attend(i, _):
        at = pl.ds(pl.multiple_of(i * Q_BLOCK, Q_BLOCK), Q_BLOCK)
        scores = nn(kr_ref[...], qt_ref[:, at])
        prob = jnp.exp(scores - lse_ref[:, at])
        dout = dout_t[:, at]
        d_prob = nn(vr_ref[...], dout)
        delta = jnp.sum(dout.astype(F32) * ot_ref[:, at], axis=0, keepdims=True)
        d_scores = (prob * (d_prob - delta)).astype(BF16)
        d_query = nn(kt_ref[...], d_scores) * 0.125
        dproj[pl.ds(0, 64), at] = unrope_t(d_query, cos_ref[:, at], sin_ref[:, at]).astype(BF16)
        dk[...] += nn(d_scores, qr_ref[at, :])
        dv[...] += nn(prob.astype(BF16), dout.astype(F32).T.astype(BF16))
        for n, steps in plan.items():

            @pl.when(i == n)
            def _():
                for run in steps:
                    run()

        return 0

    lax.fori_loop(0, 8, attend, 0)

    result_ref[...] = (h1_keep[...] + down_total[...]).astype(BF16)
    links.close(B)

    def project(b, _):
        at = pl.ds(pl.multiple_of(b * 128, 128), 128)
        d_key = unrope_t(dk[at, :].T, cos_ref[:, at], sin_ref[:, at])
        dproj[pl.ds(64, 64), at] = d_key.astype(BF16)
        dproj[pl.ds(128, 64), at] = dv[at, :].T.astype(BF16)
        hall[b] = tn(dproj[:, at], wq_ref[pl.ds(0, 192), :]).astype(BF16)
        return 0

    lax.fori_loop(0, 16, project, 0)
    back = lockstep(
        scatter_ctx(p, links, B + 32, hall, total, core_c, far_c, 64, 0),
        scatter_ctx(p, links, B + 126, hall, total, core_c, far_c, 64, 64),
    )
    next(back)
    next(back)
    next(all_gu)
    links.got(B + 143, row_pair)
    for half in range(2):
        own_lanes = pl.ds(pl.multiple_of(512 * p.xl + 256 * half, 128), 256)
        add_rows(
            row_mine.at[pl.ds(48 * half, 48)],
            [(row_sum.at[:, own_lanes], 0), (row_pair.at[:, pl.ds(256 * half, 256)], 0)], 48,
        )
    all_rows = gather_ctx(p, links, B + 88, row_mine, rowpieces_ref, 96)
    next(all_rows)
    gain = wq_ref[pl.ds(192, 1), :].astype(F32)
    late[...] = jnp.zeros_like(late)
    ggain = []
    for half in range(2):
        cols = pl.ds(512 * half, 512)
        g = nn(dproj[...], n1[:, :, cols].reshape(2048, 512))
        late[pl.ds(0, 192), cols] = g.astype(BF16)
        ggain.append(jnp.sum(g * wq_ref[pl.ds(0, 192), cols].astype(F32), axis=0, keepdims=True))
    gain_row = jnp.concatenate(ggain, axis=1) / gain
    row = iota((16, 1024), 0)
    gains = jnp.where(row == 0, gain_row, 0.0)
    late[pl.ds(192, 16), :] = jnp.where(row == 1, ggain_two[...], gains).astype(BF16)
    for f in range(8):
        for g in range(4):
            pair = gout[pl.ds(8 * f, 8), pl.ds(256 * g, 256)]
            late[pl.ds(208 + 16 * g, 16), pl.ds(128 * f, 128)] = jnp.concatenate(
                [pair[:, :128], pair[:, 128:]], axis=0
            ).astype(BF16)
    sum_late = scatter_fsdp(
        p, links, B + 62, lambda f: late.at[:, lanes_of(f)],
        late_along, late_across, late_keep, late_sum, LATE,
    )
    next(sum_late)
    next(back)
    next(all_gu)
    next(all_rows)
    next(back)
    next(sum_late)
    next(back)
    next(all_gu)
    next(all_rows)
    next(sum_late, None)
    all_late = gather_ctx(p, links, B + 107, late_sum, latepieces_ref, LATE)
    next(all_late)
    next(back, None)
    xhat, inv = normalize(h_ref[...].astype(F32))
    d_in = norm_back(total[...], xhat, inv, gain)
    dinput_ref[...] = (dh1[...] + d_in).astype(BF16)
    for copy in mine_copies:
        copy.start()
    run_all([all_gu, all_late, all_rows])
    for copy in mine_copies:
        copy.wait()
    links.close()


def shape(dims, dtype=BF16):
    return jax.ShapeDtypeStruct(dims, dtype)


def fsdp_scratch(rows, cols):
    return [
        pltpu.VMEM((6, rows, cols), BF16),
        pltpu.VMEM((2, rows, cols), BF16),
        pltpu.VMEM((rows, cols), BF16),
    ]


def layer(*args):
    blocks = pltpu.VMEM((16, 128, 1024), BF16)
    column = pltpu.VMEM((8, 128, 1024), BF16)

    def held(*dims, dtype=BF16):
        return pltpu.VMEM(dims, dtype)

    return pl.pallas_call(
        layer_kernel,
        name="layer",
        out_shape=(
            shape((128, 1024)), shape((128, 1024)), shape((16, UNITS, 128)),
            shape((16, 96, 256)), shape((16, LATE, 128)),
        ),
        in_specs=[VMEM, VMEM, ANY] + [VMEM] * 7,
        out_specs=(VMEM, VMEM, ANY, ANY, ANY),
        scratch_shapes=[
            held(208, 1024), held(128, 1024, dtype=F32), held(64, 2048), held(2 * UNITS, 128),
            held(384, 1024), held(1, 1024, dtype=F32), held(16, 64, 1024),
            blocks, blocks, column, column, column, column,
            held(64, 2048), held(64, 2048), held(64, 2048),
            held(2048, 64), held(2048, 64), held(2048, 64),
            held(64, 2048, dtype=F32), held(1, 2048, dtype=F32),
            held(3, 128, 128), held(UNITS, 128, dtype=F32), held(208, 128), held(2 * UNITS, 128),
            held(48, 1024), held(64, 2048), held(16, 64, 128), held(16, 64, 128),
            held(1024, 1024), held(2 * UNITS, 1024), held(384, 1024), held(UNITS, 1024),
            held(UNITS, 1024), held(2 * UNITS, 1024), held(128, 1024, dtype=F32),
            *column_scratch(128, 1024), held(2 * UNITS, 1024), *fsdp_scratch(2 * UNITS, 128),
            held(128, 1024, dtype=F32), held(128, 1024, dtype=F32), *column_scratch(128, 1024),
            held(192, 2048), held(2048, 64, dtype=F32), held(2048, 64, dtype=F32),
            held(LATE, 1024), held(UNITS, 128), held(UNITS, 128), held(48, 512), held(96, 256),
            held(64, 1024, dtype=F32), held(48, 1024), held(LATE, 128),
            *scatter_scratch(64, 1024), *scatter_scratch(128, 1024),
            *fsdp_scratch(48, 1024), *fsdp_scratch(LATE, 128),
            dma(B + 144), dma(B + 144), dma(10),
        ],
        compiler_params=params(1),
    )(*args)


def nt(a, b):
    return lax.dot_general(a, b, (((1,), (1,)), ((), ())), preferred_element_type=F32)


def tn(a, b):
    return lax.dot_general(a, b, (((0,), (0,)), ((), ())), preferred_element_type=F32)


def nn(a, b):
    return jnp.dot(a, b, preferred_element_type=F32)


def normalize(v):
    centered = v - jnp.mean(v, axis=-1, keepdims=True)
    inv = lax.rsqrt(jnp.mean(centered * centered, axis=-1, keepdims=True) + EPSILON)
    return centered * inv, inv


def norm_back(e, xhat, inv, gain):
    eg = e * gain
    return inv * (
        eg - jnp.mean(eg, axis=-1, keepdims=True)
        - xhat * jnp.mean(eg * xhat, axis=-1, keepdims=True)
    )


def rope_t(v, cos, sin):
    a, b = v[:32], v[32:]
    return jnp.concatenate([a * cos - b * sin, b * cos + a * sin], axis=0)


def unrope_t(v, cos, sin):
    a, b = v[:32], v[32:]
    return jnp.concatenate([a * cos + b * sin, b * cos - a * sin], axis=0)


def rope_tables():
    inverse = np.float32(ROPE_BASE) ** (-(np.arange(32, dtype=np.float32) * 2.0) / 64)
    angles = inverse[:, None].astype(np.float32) * np.arange(2048, dtype=np.float32)[None, :]
    return np.cos(angles).astype(np.float32), np.sin(angles).astype(np.float32)


def body(
    hidden_in, qkv_weight, out_weight, gate_up_weight, down_weight, attn_gain, mlp_gain, out_grad
):
    hidden_b, grad_b = hidden_in[0], out_grad[0]
    cos, sin = rope_tables()
    cos, sin = jnp.asarray(cos), jnp.asarray(sin)
    result, input_grad, gu_pieces, row_pieces, late_pieces = layer(
        hidden_b, grad_b, qkv_weight, out_weight, gate_up_weight, down_weight,
        attn_gain[None], mlp_gain[None], cos, sin,
    )
    late_pieces = late_pieces.astype(F32)
    qkv_grad = (
        late_pieces[:, :192].reshape(16, 3, 64, 128).transpose(3, 1, 0, 2).reshape(128, 3072)
    )
    gain_grads = jnp.sum(late_pieces[:, 192:194], axis=0)
    gate_up = gu_pieces.reshape(2, 8, UNITS, 128)[:, :, :328].transpose(0, 2, 1, 3)
    gate_up_grad = gate_up.reshape(5248, 128).astype(F32).T
    down_rows = row_pieces.reshape(2, 8, 2, 48, 256)[:, :, :, :41].transpose(3, 1, 0, 2, 4)
    down_grad = down_rows.reshape(328, 1024).astype(F32)
    out_rows = late_pieces[:, 208:272].reshape(16, 8, 8, 128).transpose(0, 2, 1, 3)
    out_weight_grad = out_rows.reshape(128, 1024)
    return (
        result[None], input_grad[None], qkv_grad, out_weight_grad, gate_up_grad, down_grad,
        gain_grads[0], gain_grads[1],
    )


def solution(mesh):
    return jax.shard_map(
        body,
        mesh=mesh,
        in_specs=(
            P("fsdp", "ctx", None), P("fsdp", None), P("fsdp", None), P("fsdp", None),
            P("fsdp", None), P("fsdp"), P("fsdp"), P("fsdp", "ctx", None),
        ),
        out_specs=(
            P("fsdp", "ctx", None), P("fsdp", "ctx", None), P("fsdp", None), P("fsdp", None),
            P("fsdp", None), P("fsdp", None), P("fsdp"), P("fsdp"),
        ),
        check_vma=False,
    )
```

```python
import jax
import jax.numpy as jnp
import numpy as np
from jax import lax
from jax.experimental import pallas as pl
from jax.experimental.pallas import tpu as pltpu
from jax.sharding import PartitionSpec as P

HEADS = 16
EPSILON = 1e-05
ROPE_BASE = 160000.0
F32 = jnp.float32
BF16 = jnp.bfloat16
MESH = pl.DeviceIdType.MESH
ANY = pl.BlockSpec(memory_space=pl.ANY)
VMEM = pl.BlockSpec(memory_space=pltpu.VMEM)
MIB = 1024 * 1024


class Place:
    def __init__(self):
        c = lax.axis_index("ctx")
        self.c = c
        self.f = lax.axis_index("fsdp")
        k = c % 2
        y = (c // 2) % 4
        xl = c // 8
        self.k = k

        def at(x, row):
            return x * 4 + row % 4

        ox = 1 - xl
        self.other = c + 1 - 2 * k
        self.chip = {
            "S": at(xl, y),
            "P": at(xl, y + 1),
            "M": at(xl, y + 3),
            "F": at(xl, y + 2),
            "X": at(ox, y),
            "XP": at(ox, y + 1),
            "XM": at(ox, y + 3),
            "XF": at(ox, y + 2),
        }

        self.same_core = {name: chip * 2 + k for name, chip in self.chip.items()}
        self.cross_core = {name: chip * 2 + 1 - k for name, chip in self.chip.items()}
        self.xl = xl
        self.t = c % 8
        self.column = {name: chip % 4 * 2 + k for name, chip in self.chip.items()}
        self.cross_column = {name: chip % 4 * 2 + 1 - k for name, chip in self.chip.items()}
        self.ring = [(c + d) % 16 for d in range(16)]
        z, xh = self.f // 2, self.f % 2
        self.twin = z * 2 + 1 - xh
        self.planes = [(z + d) % 4 * 2 + xh for d in range(4)]
        self.twin_planes = [(z + d) % 4 * 2 + 1 - xh for d in range(4)]
        self.fsdp_peers = [{"fsdp": i} for i in [self.twin] + self.planes[1:]]

    def same(self, name):
        return self.same_core[name]

    def cross(self, name):
        return self.cross_core[name]


def lanes_of(f):
    return pl.ds(pl.multiple_of(f * 128, 128), 128)


def on_ctx(index):
    return {"ctx": index}


def greet(peers):
    barrier = pltpu.get_barrier_semaphore()
    for peer in peers:
        pl.semaphore_signal(barrier, inc=1, device_id=peer, device_id_type=MESH)
    pl.semaphore_wait(barrier, len(peers))


class Links:
    def __init__(self, send, recv, peer, like=()):
        self.send, self.recv, self.peer = send, recv, peer
        self.like = {ref.shape: ref for ref in like}
        self.open = []

    def copy(self, i, src, dst, peer):
        return pltpu.make_async_remote_copy(
            src_ref=src, dst_ref=dst, send_sem=self.send.at[i], recv_sem=self.recv.at[i],
            device_id=peer, device_id_type=MESH,
        )

    def put(self, i, src, dst, peer):
        self.copy(i, src, dst, peer).start()
        self.open.append((i, self.like.get(src.shape, src)))

    def got(self, i, dst):
        self.copy(i, dst, dst, self.peer).wait_recv()

    def close(self, below=1000):
        for i, ref in self.open:
            if i < below:
                self.copy(i, ref, ref, self.peer).wait_send()
        self.open = [(i, ref) for i, ref in self.open if i >= below]


def ctx_peers(p):
    return [on_ctx(p.other), on_ctx(p.same("P")), on_ctx(p.same("M")), on_ctx(p.same("X"))]


GATHER_COPIES = 19


def gather_ctx(p, links, base, own, out, rows, off=None):
    half = rows // 2
    top, bottom = pl.ds(0, half), pl.ds(half, half)
    to_p, to_m, to_x, to_k = (
        on_ctx(p.same("P")), on_ctx(p.same("M")), on_ctx(p.same("X")), on_ctx(p.other),
    )

    def rows_of(ref):
        return ref if off is None else ref.at[pl.ds(off, rows)]

    own = rows_of(own)
    mine = rows_of(out.at[p.c])

    def put(i, src, dst, peer):
        links.put(base + i, src, dst, peer)

    def got(i, dst):
        links.got(base + i, dst)

    def block(name):
        return rows_of(out.at[p.same(name)])

    def cross(name):
        return rows_of(out.at[p.cross(name)])

    put(0, own, mine, to_p)
    put(1, own, mine, to_m)
    put(2, own, mine, to_x)
    put(3, own, mine, to_k)
    yield [p.same("S")]
    got(0, block("M"))
    put(4, block("M").at[top], block("M").at[top], to_p)
    put(10, block("M"), block("M"), to_k)
    got(1, block("P"))
    put(5, block("P").at[bottom], block("P").at[bottom], to_m)
    put(11, block("P"), block("P"), to_k)
    got(2, block("X"))
    put(6, block("X"), block("X"), to_p)
    put(7, block("X"), block("X"), to_m)
    put(12, block("X"), block("X"), to_k)
    got(3, cross("S"))
    yield [p.same("M"), p.same("P"), p.same("X"), p.cross("S")]
    for i, part, to_core in ((4, top, 13), (5, bottom, 14)):
        piece = block("F").at[part]
        got(i, piece)
        put(4 + i, piece, piece, to_x)
        put(to_core, piece, piece, to_k)
    got(10, cross("M"))
    got(11, cross("P"))
    yield [p.same("F"), p.cross("M"), p.cross("P")]
    got(6, block("XM"))
    put(15, block("XM"), block("XM"), to_k)
    got(7, block("XP"))
    put(16, block("XP"), block("XP"), to_k)
    got(12, cross("X"))
    got(13, cross("F").at[top])
    got(14, cross("F").at[bottom])
    yield [p.same("XM"), p.same("XP"), p.cross("X"), p.cross("F")]
    for i, part, to_core in ((8, top, 17), (9, bottom, 18)):
        piece = block("XF").at[part]
        got(i, piece)
        put(to_core, piece, piece, to_k)
    got(15, cross("XM"))
    got(16, cross("XP"))
    yield [p.same("XF"), p.cross("XM"), p.cross("XP")]
    got(17, cross("XF").at[top])
    got(18, cross("XF").at[bottom])
    yield [p.cross("XF")]


def gather_column(p, links, base, own, out, rows):
    half = rows // 2
    top, bottom = pl.ds(0, half), pl.ds(half, half)
    to_p, to_m, to_k = on_ctx(p.same("P")), on_ctx(p.same("M")), on_ctx(p.other)
    same, cross = p.column, p.cross_column

    def put(i, src, dst, peer):
        links.put(base + i, src, dst, peer)

    def got(i, dst):
        links.got(base + i, dst)

    mine = out.at[same["S"]]
    put(0, own, mine, to_p)
    put(1, own, mine, to_m)
    put(2, own, mine, to_k)
    yield [same["S"]]
    got(0, out.at[same["M"]])
    put(3, out.at[same["M"], top], out.at[same["M"], top], to_p)
    put(5, out.at[same["M"]], out.at[same["M"]], to_k)
    got(1, out.at[same["P"]])
    put(4, out.at[same["P"], bottom], out.at[same["P"], bottom], to_m)
    put(6, out.at[same["P"]], out.at[same["P"]], to_k)
    got(2, out.at[cross["S"]])
    yield [cross["S"], same["M"], same["P"]]
    got(5, out.at[cross["M"]])
    got(3, out.at[same["F"], top])
    put(7, out.at[same["F"], top], out.at[same["F"], top], to_k)
    got(4, out.at[same["F"], bottom])
    put(8, out.at[same["F"], bottom], out.at[same["F"], bottom], to_k)
    got(6, out.at[cross["P"]])
    yield [same["F"], cross["M"], cross["P"]]
    got(7, out.at[cross["F"], top])
    got(8, out.at[cross["F"], bottom])
    yield [cross["F"]]


def scatter_column(p, links, base, part, total, core_in, far, rows, off=0):
    half = rows // 2
    whole, top, bottom = pl.ds(off, rows), pl.ds(off, half), pl.ds(off + half, half)
    to_p, to_m, to_k = on_ctx(p.same("P")), on_ctx(p.same("M")), on_ctx(p.other)
    order = ("F", "P", "M", "S")
    mid = [part.at[p.column[name]] for name in order]

    def put(i, src, dst, peer):
        links.put(base + i, src, dst, peer)

    def got(i, dst):
        links.got(base + i, dst)

    for i, name in enumerate(order):
        put(i, part.at[p.cross_column[name], whole], core_in.at[i, whole], to_k)
    yield

    def pair(i):
        got(i, core_in.at[i, whole])
        return [(mid[i], 0), (core_in.at[i], 0)]

    add_rows(mid[0], pair(0), rows, off)
    put(4, mid[0].at[top], far.at[0, top], to_p)
    put(5, mid[0].at[bottom], far.at[0, bottom], to_m)
    yield
    terms = pair(1)
    got(4, far.at[0, top])
    add_rows(mid[1], terms + [(far.at[0], 0)], half, off)
    add_rows(mid[1], terms, half, off + half)
    put(6, mid[1].at[whole], far.at[1, whole], to_p)
    terms = pair(2)
    got(5, far.at[0, bottom])
    add_rows(mid[2], terms, half, off)
    add_rows(mid[2], terms + [(far.at[0], 0)], half, off + half)
    put(7, mid[2].at[whole], far.at[2, whole], to_m)
    yield
    terms = pair(3)
    got(6, far.at[1, whole])
    got(7, far.at[2, whole])
    add_rows(total, terms + [(far.at[1], 0), (far.at[2], 0)], rows, off)


def gather_fsdp(p, links, base, own, slot):
    links.put(base, own, slot(p.f), {"fsdp": p.twin})
    for d in (1, 3, 2):
        links.put(base + d, own, slot(p.f), {"fsdp": p.planes[d]})
    yield []
    twin = slot(p.twin)
    links.got(base, twin)
    for d in (1, 3, 2):
        links.put(base + 3 + d, twin, twin, {"fsdp": p.planes[d]})
    yield [p.twin]
    for d in (1, 3, 2):
        links.got(base + d, slot(p.planes[4 - d]))
    for d in (1, 3, 2):
        links.got(base + 3 + d, slot(p.twin_planes[4 - d]))
    yield [p.planes[d] for d in (3, 1, 2)] + [p.twin_planes[d] for d in (3, 1, 2)]


def gather_ring(p, links, base, own, slot):
    up, down = {"fsdp": p.planes[1]}, {"fsdp": p.planes[3]}
    links.put(base + 1, own, slot(p.f), up)
    links.put(base + 2, own, slot(p.f), down)
    links.put(base, own, slot(p.f), {"fsdp": p.twin})
    yield []
    links.got(base, slot(p.twin))
    links.put(base + 4, slot(p.twin), slot(p.twin), up)
    links.put(base + 5, slot(p.twin), slot(p.twin), down)
    below = slot(p.planes[3])
    links.got(base + 1, below)
    links.put(base + 3, below, below, up)
    yield []
    above = slot(p.twin_planes[1])
    links.got(base + 5, above)
    links.put(base + 6, above, above, down)
    yield []
    links.got(base + 2, slot(p.planes[1]))
    links.got(base + 3, slot(p.planes[2]))
    links.got(base + 4, slot(p.twin_planes[3]))
    links.got(base + 6, slot(p.twin_planes[2]))
    yield []


def scatter_fsdp(p, links, base, part, along, across, keep, total, rows):
    for n, d in enumerate((1, 3, 2)):
        links.put(base + n, part(p.planes[d]), along.at[n], {"fsdp": p.planes[d]})
        links.put(base + 3 + n, part(p.twin_planes[d]), along.at[3 + n], {"fsdp": p.planes[d]})
    yield
    for n in range(6):
        links.got(base + n, along.at[n])
    terms = [(along.at[3 + n], 0) for n in range(3)]
    add_rows(across.at[0], [(part(p.twin), 0)] + terms, rows)
    links.put(base + 6, across.at[0], across.at[1], {"fsdp": p.twin})
    add_rows(keep, [(part(p.f), 0)] + [(along.at[n], 0) for n in range(3)], rows)
    yield
    links.got(base + 6, across.at[1])
    add_rows(total, [(keep, 0), (across.at[1], 0)], rows)


def run_all(stages):
    live = list(stages)
    while live:
        left = []
        for stage in live:
            try:
                next(stage)
                left.append(stage)
            except StopIteration:
                pass
        live = left


SCATTER_COPIES = 16
SCATTER_ORDER = ("XF", "XP", "XM", "F", "X", "P", "M", "S")


def add_rows(dst, terms, rows, at=0):
    step = 16

    def one(i, _):
        r = pl.ds(pl.multiple_of(i * step, step) + at, step)
        total = None
        for ref, _unused in terms:
            part = ref[r, :].astype(F32)
            total = part if total is None else total + part
        dst[r, :] = total.astype(dst.dtype)
        return 0

    lax.fori_loop(0, rows // step, one, 0)


def lockstep(*stages):
    while True:
        found = []
        ended = 0
        for one in stages:
            try:
                found += next(one) or []
            except StopIteration:
                ended += 1
        if ended == len(stages):
            return
        yield found


def scatter_ctx(p, links, base, part, total, core_in, far, rows, off=0):
    half = rows // 2
    to_p, to_m, to_x, to_k = (
        on_ctx(p.same("P")), on_ctx(p.same("M")), on_ctx(p.same("X")), on_ctx(p.other),
    )

    def put(i, src, dst, peer):
        links.put(base + i, src, dst, peer)

    def got(i, dst):
        links.got(base + i, dst)

    whole = pl.ds(off, rows)
    top, bottom = pl.ds(off, half), pl.ds(off + half, half)
    mid = [part.at[p.same(name)] for name in SCATTER_ORDER]
    for i, name in enumerate(SCATTER_ORDER):
        put(i, part.at[p.cross(name), whole], core_in.at[i, whole], to_k)
    yield

    def pair(i):
        got(i, core_in.at[i, whole])
        return [(mid[i], 0), (core_in.at[i], 0)]

    for i, peer in ((0, to_x), (1, to_p), (2, to_m)):
        add_rows(mid[i], pair(i), rows, off)
        put(8 + i, mid[i].at[whole], far.at[i, whole], peer)
    yield
    terms = pair(3)
    got(8, far.at[0, whole])
    add_rows(mid[3], terms + [(far.at[0], 0)], rows, off)
    put(11, mid[3].at[top], far.at[3, top], to_p)
    put(12, mid[3].at[bottom], far.at[3, bottom], to_m)
    yield
    terms = pair(4)
    got(9, far.at[1, whole])
    got(10, far.at[2, whole])
    add_rows(mid[4], terms + [(far.at[1], 0), (far.at[2], 0)], rows, off)
    put(13, mid[4].at[whole], far.at[4, whole], to_x)
    yield
    terms = pair(5)
    got(11, far.at[3, top])
    add_rows(mid[5], terms + [(far.at[3], 0)], half, off)
    add_rows(mid[5], terms, half, off + half)
    put(14, mid[5].at[whole], far.at[5, whole], to_p)
    terms = pair(6)
    got(12, far.at[3, bottom])
    add_rows(mid[6], terms, half, off)
    add_rows(mid[6], terms + [(far.at[3], 0)], half, off + half)
    put(15, mid[6].at[whole], far.at[6, whole], to_m)
    yield
    terms = pair(7)
    got(13, far.at[4, whole])
    got(14, far.at[5, whole])
    got(15, far.at[6, whole])
    add_rows(total, terms + [(far.at[4], 0), (far.at[5], 0), (far.at[6], 0)], rows, off)


def scatter_scratch(rows, cols):
    return [
        pltpu.VMEM((8, rows, cols), BF16),
        pltpu.VMEM((7, rows, cols), BF16),
    ]


def column_scratch(rows, cols):
    return [pltpu.VMEM((4, rows, cols), BF16), pltpu.VMEM((3, rows, cols), BF16)]


def dma(n):
    return pltpu.SemaphoreType.DMA((n,))


def params(cid, mib=60):
    return pltpu.CompilerParams(
        collective_id=cid, has_side_effects=True, vmem_limit_bytes=mib * MIB
    )


Q_BLOCK = 256
UNITS = 352
LATE = 288
B = 155


def pick_rows(select, matrix):
    return nt(select.astype(BF16), matrix).astype(BF16)


def ones_at(rows, cols, shift, valid):
    row = lax.broadcasted_iota(jnp.int32, (rows, cols), 0)
    col = lax.broadcasted_iota(jnp.int32, (rows, cols), 1)
    return jnp.where((col == row + shift) & (row < valid), 1.0, 0.0)


def shard_of(row):
    return sum(((row >= 41 * n).astype(jnp.int32) for n in range(1, 8)), 0)


def iota(dims, axis):
    return lax.broadcasted_iota(jnp.int32, dims, axis)


def layer_kernel(
    h_ref, dy_ref, wqkv_ref, wout_ref, wgu_ref, wdown_ref, g1_ref, g2_ref, cos_ref, sin_ref,
    result_ref, dinput_ref, gupieces_ref, rowpieces_ref, latepieces_ref,
    wq_ref, dh1, dout_t, gu_sum, gdown, ggain_two, gsum,
    hall, n1, dyall, nall, part, downsum, qt_ref, kt_ref, vt_ref, qr_ref, kr_ref, vr_ref, ot_ref, lse_ref,
    qkv_win, gu_acc, qkv_cols, gu_cols, down_rows, ob, att_ref, dat,
    woutall, gu_ref, downall, down_w, act, dgu, total, core_in, far, ggu, gu_along, gu_across, gu_keep,
    h1_keep, down_total, core_down, far_down,
    dproj, dk, dv, late, gu_pair, gu_mine, row_pair, row_mine, gout, row_sum, late_sum,
    core_b, far_b, core_c, far_c, row_along, row_across, row_keep, late_along, late_across, late_keep,
    send, recv, local,
):
    p = Place()
    links = Links(
        send, recv, on_ctx(p.other),
        [gu_keep, hall.at[0], hall.at[0, pl.ds(0, 64)], hall.at[0, pl.ds(0, 32)], qkv_cols, gu_cols,
         down_rows, ob.at[:, pl.ds(0, 128)], gu_mine, gu_mine.at[pl.ds(0, 176)], row_mine,
         row_mine.at[pl.ds(0, 48)], late_keep, late_keep.at[pl.ds(0, LATE // 2)]],
    )
    wins = [
        pltpu.make_async_copy(
            wqkv_ref.at[:, pl.ds(pl.multiple_of(part * 1024 + (p.c // 2) * 128, 128), 128)],
            qkv_win.at[part], local.at[part],
        )
        for part in range(3)
    ]
    own_h = pltpu.make_async_copy(h_ref, hall.at[p.c], local.at[5])
    for copy in wins:
        copy.start()
    own_h.start()
    for i in range(3):
        wins[i].wait()
        qkv_cols[pl.ds(64 * i, 64), :] = pick_rows(
            ones_at(64, 128, (p.c % 2) * 64, 64), qkv_win[i]
        )
    row = iota((16, 128), 0)
    gains = jnp.where(row == 0, g1_ref[...].astype(F32), 0.0)
    gains = jnp.where(row == 1, g2_ref[...].astype(F32), gains)
    qkv_cols[pl.ds(192, 16), :] = gains.astype(BF16)
    greet([on_ctx(p.ring[d]) for d in range(1, 16)] + p.fsdp_peers)
    gather_wq = gather_fsdp(p, links, 38, qkv_cols, lambda f: wq_ref.at[:, lanes_of(f)])
    next(gather_wq)
    gather_h = gather_ctx(p, links, 0, h_ref, hall, 128)
    ready = next(gather_h)
    lanes = lanes_of(p.f)
    half = pl.ds(pl.multiple_of(p.k * 64, 64), 64)

    def out_half(f, k):
        return woutall.at[pl.ds(pl.multiple_of(f * 128 + k * 64, 64), 64)]

    gather_out = gather_ring(p, links, 53, wout_ref.at[half], lambda f: out_half(f, p.k))
    next(gather_out)
    wq_ref[:, lanes] = qkv_cols[...]
    for half in range(2):
        row = iota((UNITS, 1), 0)
        want = jnp.where(row < 328, 8 * row + p.t + 64 * half, -1)
        gu_acc[...] = jnp.zeros_like(gu_acc)

        def pick(i, _):
            cols = pl.ds(pl.multiple_of(2560 * half + i * 896, 128), 896)
            select = jnp.where(iota((UNITS, 896), 1) + i * 896 == want, 1.0, 0.0)
            gu_acc[...] += nt(select.astype(BF16), wgu_ref[:, cols])
            return 0

        lax.fori_loop(0, 3, pick, 0)
        gu_cols[pl.ds(UNITS * half, UNITS), :] = gu_acc[...].astype(BF16)
    place = iota((48, 328), 0)
    select = (iota((48, 328), 1) == 8 * place + p.t) & (place < 41)
    down_rows[...] = nn(jnp.where(select, 1.0, 0.0).astype(BF16), wdown_ref[...]).astype(BF16)
    gather_gu = gather_ring(p, links, 45, gu_cols, lambda f: gu_ref.at[:, lanes_of(f)])
    next(gather_gu)

    def down_slot(f):
        return downall.at[pl.ds(pl.multiple_of(f * 48, 16), 48)]

    gather_down = gather_ring(p, links, 83, down_rows, down_slot)
    next(gather_down)
    own_h.wait()
    next(gather_wq)
    ready += next(gather_h)
    next(gather_wq)
    locals_ = [
        pltpu.make_async_copy(dy_ref, dyall.at[p.t], local.at[6]),
        pltpu.make_async_copy(
            wout_ref, woutall.at[pl.ds(pl.multiple_of(p.f * 128, 128), 128)], local.at[8]
        ),
        pltpu.make_async_copy(down_rows, down_slot(p.f), local.at[3]),
    ]
    for copy in locals_:
        copy.start()
    gu_ref[:, lanes] = gu_cols[...]
    next(gather_out)

    def project(b):
        gain = wq_ref[pl.ds(192, 1), :].astype(F32)

        def norm(i, _):
            r = pl.ds(pl.multiple_of(i * 32, 32), 32)
            xhat, _unused = normalize(hall[b, r, :].astype(F32))
            n1[b, r, :] = (xhat * gain).astype(BF16)
            return 0

        lax.fori_loop(0, 4, norm, 0)
        proj = nt(wq_ref[pl.ds(0, 192), :], n1[b])
        at = pl.ds(pl.multiple_of(b * 128, 128), 128)
        cos, sin = cos_ref[:, at], sin_ref[:, at]
        q = rope_t(proj[:64], cos, sin).astype(BF16) * jnp.asarray(0.125, BF16)
        k = rope_t(proj[64:128], cos, sin).astype(BF16)
        v = proj[128:192].astype(BF16)
        qt_ref[:, at] = q
        kt_ref[:, at] = k
        vt_ref[:, at] = v
        qr_ref[at, :] = q.astype(F32).T.astype(BF16)
        kr_ref[at, :] = k.astype(F32).T.astype(BF16)
        vr_ref[at, :] = v.astype(F32).T.astype(BF16)

    for b in ready:
        project(b)
    for b in next(gather_h):
        project(b)
    ready = next(gather_h)
    gather_dy = gather_column(p, links, 19, dy_ref, dyall, 128)
    next(gather_dy)
    for b in ready:
        project(b)
    while ready is not None:
        ready = next(gather_h, None)
        for b in ready or ():
            project(b)
    next(gather_out)
    next(gather_gu)
    next(gather_down)
    plan = {1: gather_dy, 2: gather_gu, 3: gather_down, 4: gather_out, 5: gather_dy}

    def attend(i, _):
        j = (p.c // 2 + i) % 8
        at = pl.ds(pl.multiple_of(j * Q_BLOCK, Q_BLOCK), Q_BLOCK)
        scores = nn(kr_ref[...], qt_ref[:, at])
        top = jnp.max(scores, axis=0, keepdims=True)
        weights = jnp.exp(scores - top)
        total = jnp.sum(weights, axis=0, keepdims=True)
        mixed = nn(vt_ref[...], weights.astype(BF16)) / total
        ot_ref[:, at] = mixed
        lse_ref[:, at] = top + jnp.log(total)
        ob[:, at] = mixed.astype(BF16)

        @pl.when(i > 0)
        def _():
            for e in range(2):
                to = 2 * j + e
                piece = ob.at[:, pl.ds(pl.multiple_of(to * 128, 128), 128)]
                links.copy(67 + 2 * i + e - p.k, piece, att_ref.at[p.c], on_ctx(to)).start()

        @pl.when(i == 0)
        def _():
            piece = ob.at[:, pl.ds(pl.multiple_of(p.c * 128, 128), 128)]
            copy = pltpu.make_async_copy(piece, att_ref.at[p.c], local.at[9])
            copy.start()
            copy.wait()
            piece = ob.at[:, pl.ds(pl.multiple_of(p.other * 128, 128), 128)]
            links.copy(67 + (p.other - p.c + 16) % 16, piece, att_ref.at[p.c], on_ctx(p.other)).start()

        for s, stages in plan.items():

            @pl.when(i == s)
            def _():
                next(stages)

        return 0

    lax.fori_loop(0, 8, attend, 0)
    others = [p.twin] + [p.planes[d] for d in (3, 1, 2)] + [p.twin_planes[d] for d in (3, 1, 2)]
    for i, f in enumerate(others):
        links.put(60 + i, out_half(f, p.k), out_half(f, p.k), on_ctx(p.other))
    for d in range(1, 16):
        links.got(67 + d, att_ref.at[p.ring[16 - d]])
        links.open.append((67 + d, ob.at[:, pl.ds(0, 128)]))
    for copy in locals_:
        copy.wait()
    for i, f in enumerate(others):
        links.got(60 + i, out_half(f, 1 - p.k))

    gain = wq_ref[pl.ds(193, 1), :].astype(F32)
    att = att_ref[...].reshape(1024, 128)
    h1 = h_ref[...].astype(F32) + tn(att, woutall[...])
    h1_keep[...] = h1
    xhat, _unused = normalize(h1)
    nall[p.t] = (xhat * gain).astype(BF16)
    gather = gather_column(p, links, 90, nall.at[p.t], nall, 128)
    ready = next(gather)
    next(gather_gu)
    next(gather_down)
    pick = iota((UNITS, 384), 1)
    row = iota((UNITS, 1), 0)
    want = jnp.where(row < 328, row + 7 * shard_of(row), -1)
    down_w[...] = nn(jnp.where(pick == want, 1.0, 0.0).astype(BF16), downall[...]).astype(BF16)
    for _ in gather_dy:
        pass

    def feed(b, other):
        n2 = jnp.concatenate([nall[b], nall[other]], axis=0)
        gu = nt(gu_ref[...], n2)
        d_act = nt(down_w[...], jnp.concatenate([dyall[b], dyall[other]], axis=0))
        gate, up = gu[:UNITS], gu[UNITS:]
        cdf = 0.5 * (1.0 + lax.erf(gate * 2.0 ** (-0.5)))
        gelu = gate * cdf
        pdf = jnp.exp(-0.5 * gate * gate) * (2.0 * np.pi) ** (-0.5)
        d_gate = d_act * up * (cdf + gate * pdf)
        d_gu = jnp.concatenate([d_gate, d_act * gelu], axis=0).astype(BF16)
        activated = (gelu * up).astype(BF16)
        d_n2 = tn(d_gu, gu_ref[...]).astype(BF16)
        for i, block in enumerate((b, other)):
            at = pl.ds(pl.multiple_of(block * 128, 128), 128)
            act[:, at] = activated[:, 128 * i : 128 * i + 128]
            dgu[:, at] = d_gu[:, 128 * i : 128 * i + 128]
            part[block] = d_n2[128 * i : 128 * i + 128]

    waiting = list(ready)
    for found in gather:
        waiting += found
        while len(waiting) > 1:
            feed(waiting.pop(0), waiting.pop(0))
    scatter = lockstep(
        scatter_column(p, links, 109, part, total, core_in, far, 64, 0),
        scatter_column(p, links, 117, part, total, core_in, far, 64, 64),
    )
    next(scatter)
    next(scatter)
    ggain = []
    for half in range(2):
        cols = pl.ds(512 * half, 512)
        g = nn(dgu[...], nall[:, :, cols].reshape(1024, 512))
        ggu[:, cols] = g.astype(BF16)
        ggain.append(jnp.sum(g * gu_ref[:, cols].astype(F32), axis=0, keepdims=True))
    ggain_two[...] = jnp.concatenate(ggain, axis=1) / gain
    sum_gu = scatter_fsdp(
        p, links, 140, lambda f: ggu.at[:, lanes_of(f)], gu_along, gu_across, gu_keep,
        gu_sum, 2 * UNITS,
    )
    next(sum_gu)
    next(scatter)
    row = iota((384, 1), 0)
    shard = row // 48
    place = row - 48 * shard
    want = jnp.where(place < 41, 41 * shard + place, -1)
    spread = jnp.where(iota((384, UNITS), 1) == want, 1.0, 0.0).astype(BF16)
    for half in range(2):
        cols = pl.ds(512 * half, 512)
        g = nn(act[...], dyall[:, :, cols].reshape(1024, 512)).astype(BF16)
        gdown[:, cols] = nn(spread, g).astype(BF16)

    def down(b, _):
        at = pl.ds(pl.multiple_of(b * 128, 128), 128)
        downsum[b] = tn(act[:, at], down_w[...]).astype(BF16)
        return 0

    lax.fori_loop(0, 8, down, 0)
    sum_down = scatter_column(p, links, 147, downsum, down_total, core_down, far_down, 128)
    next(sum_down)
    next(scatter, None)
    h1 = h1_keep[...]
    xhat, inv = normalize(h1)
    d_h1 = dy_ref[...].astype(F32) + norm_back(total[...], xhat, inv, gain)
    dh1[...] = d_h1
    d_h1_b = d_h1.astype(BF16)
    dat[...] = nt(woutall[...], d_h1_b).astype(BF16).reshape(16, 64, 128)
    lanes = pl.ds(pl.multiple_of(p.c * 128, 128), 128)
    for d in range(1, 16):
        links.put(124 + d, dat.at[p.ring[d]], dout_t.at[:, lanes], on_ctx(p.ring[d]))
    dout_t[:, lanes] = dat[p.c]
    att = att_ref[...]
    for g in range(4):
        rows = att[4 * g : 4 * g + 4].reshape(256, 128)
        block = nn(rows, d_h1_b).reshape(2, 16, 8, 1024).transpose(1, 0, 2, 3)
        gsum[:, pl.ds(16 * g, 16), :] = block.reshape(16, 16, 1024).astype(BF16)
    next(sum_down)

    sum_out = scatter_ctx(p, links, B + 16, gsum, gout, core_b, far_b, 64)
    next(sum_out)
    for d in range(1, 16):
        links.got(124 + d, dout_t.at[:, pl.ds(pl.multiple_of(p.ring[16 - d] * 128, 128), 128)])
    sum_rows = scatter_fsdp(
        p, links, B + 55, lambda f: gdown.at[pl.ds(pl.multiple_of(f * 48, 16), 48)],
        row_along, row_across, row_keep, row_sum, 48,
    )
    next(sum_rows)
    all_gu = gather_ctx(p, links, B + 69, gu_mine, gupieces_ref, UNITS)
    mine_copies = [
        pltpu.make_async_copy(gu_mine, gupieces_ref.at[p.c], local.at[2]),
        pltpu.make_async_copy(row_mine, rowpieces_ref.at[p.c], local.at[3]),
        pltpu.make_async_copy(late_sum, latepieces_ref.at[p.c], local.at[4]),
    ]

    other_half = pl.ds(pl.multiple_of(UNITS * (1 - p.xl), 16), UNITS)
    own_half = pl.ds(pl.multiple_of(UNITS * p.xl, 16), UNITS)
    other_cols = pl.ds(pl.multiple_of(512 * (1 - p.xl), 128), 512)
    to_x = on_ctx(p.same("X"))

    def swap_gu():
        next(sum_gu, None)
        links.put(B + 142, gu_sum.at[other_half], gu_pair, to_x)

    def begin_gu():
        links.got(B + 142, gu_pair)
        add_rows(gu_mine, [(gu_sum.at[own_half], 0), (gu_pair, 0)], UNITS)
        next(all_gu)

    def swap_rows():
        next(sum_rows, None)
        links.put(B + 143, row_sum.at[:, other_cols], row_pair, to_x)

    def step(stages):
        return lambda: next(stages, None)

    plan = {
        0: [step(sum_out), step(sum_gu)], 1: [step(sum_down)], 2: [swap_gu, step(sum_out)],
        3: [step(sum_down)], 4: [begin_gu, step(sum_out)], 5: [step(sum_out), step(sum_rows)],
        6: [step(sum_out), step(all_gu), swap_rows], 7: [step(all_gu)],
    }
    dk[...] = jnp.zeros_like(dk)
    dv[...] = jnp.zeros_like(dv)

    def attend(i, _):
        at = pl.ds(pl.multiple_of(i * Q_BLOCK, Q_BLOCK), Q_BLOCK)
        scores = nn(kr_ref[...], qt_ref[:, at])
        prob = jnp.exp(scores - lse_ref[:, at])
        dout = dout_t[:, at]
        d_prob = nn(vr_ref[...], dout)
        delta = jnp.sum(dout.astype(F32) * ot_ref[:, at], axis=0, keepdims=True)
        d_scores = (prob * (d_prob - delta)).astype(BF16)
        d_query = nn(kt_ref[...], d_scores) * 0.125
        dproj[pl.ds(0, 64), at] = unrope_t(d_query, cos_ref[:, at], sin_ref[:, at]).astype(BF16)
        dk[...] += nn(d_scores, qr_ref[at, :])
        dv[...] += nn(prob.astype(BF16), dout.astype(F32).T.astype(BF16))
        for n, steps in plan.items():

            @pl.when(i == n)
            def _():
                for run in steps:
                    run()

        return 0

    lax.fori_loop(0, 8, attend, 0)

    result_ref[...] = (h1_keep[...] + down_total[...]).astype(BF16)
    links.close(B)

    def project(b, _):
        at = pl.ds(pl.multiple_of(b * 128, 128), 128)
        d_key = unrope_t(dk[at, :].T, cos_ref[:, at], sin_ref[:, at])
        dproj[pl.ds(64, 64), at] = d_key.astype(BF16)
        dproj[pl.ds(128, 64), at] = dv[at, :].T.astype(BF16)
        hall[b] = tn(dproj[:, at], wq_ref[pl.ds(0, 192), :]).astype(BF16)
        return 0

    lax.fori_loop(0, 16, project, 0)
    back = lockstep(
        scatter_ctx(p, links, B + 32, hall, total, core_c, far_c, 64, 0),
        scatter_ctx(p, links, B + 126, hall, total, core_c, far_c, 64, 64),
    )
    next(back)
    next(back)
    next(all_gu)
    links.got(B + 143, row_pair)
    for half in range(2):
        own_lanes = pl.ds(pl.multiple_of(512 * p.xl + 256 * half, 128), 256)
        add_rows(
            row_mine.at[pl.ds(48 * half, 48)],
            [(row_sum.at[:, own_lanes], 0), (row_pair.at[:, pl.ds(256 * half, 256)], 0)], 48,
        )
    all_rows = gather_ctx(p, links, B + 88, row_mine, rowpieces_ref, 96)
    next(all_rows)
    gain = wq_ref[pl.ds(192, 1), :].astype(F32)
    late[...] = jnp.zeros_like(late)
    ggain = []
    for half in range(2):
        cols = pl.ds(512 * half, 512)
        g = nn(dproj[...], n1[:, :, cols].reshape(2048, 512))
        late[pl.ds(0, 192), cols] = g.astype(BF16)
        ggain.append(jnp.sum(g * wq_ref[pl.ds(0, 192), cols].astype(F32), axis=0, keepdims=True))
    gain_row = jnp.concatenate(ggain, axis=1) / gain
    row = iota((16, 1024), 0)
    gains = jnp.where(row == 0, gain_row, 0.0)
    late[pl.ds(192, 16), :] = jnp.where(row == 1, ggain_two[...], gains).astype(BF16)
    for f in range(8):
        for g in range(4):
            pair = gout[pl.ds(8 * f, 8), pl.ds(256 * g, 256)]
            late[pl.ds(208 + 16 * g, 16), pl.ds(128 * f, 128)] = jnp.concatenate(
                [pair[:, :128], pair[:, 128:]], axis=0
            ).astype(BF16)
    sum_late = scatter_fsdp(
        p, links, B + 62, lambda f: late.at[:, lanes_of(f)],
        late_along, late_across, late_keep, late_sum, LATE,
    )
    next(sum_late)
    next(back)
    next(all_gu)
    next(all_rows)
    next(back)
    next(sum_late)
    next(back)
    next(all_gu)
    next(all_rows)
    next(sum_late, None)
    all_late = gather_ctx(p, links, B + 107, late_sum, latepieces_ref, LATE)
    next(all_late)
    next(back, None)
    xhat, inv = normalize(h_ref[...].astype(F32))
    d_in = norm_back(total[...], xhat, inv, gain)
    dinput_ref[...] = (dh1[...] + d_in).astype(BF16)
    for copy in mine_copies:
        copy.start()
    run_all([all_gu, all_late, all_rows])
    for copy in mine_copies:
        copy.wait()
    links.close()


def shape(dims, dtype=BF16):
    return jax.ShapeDtypeStruct(dims, dtype)


def fsdp_scratch(rows, cols):
    return [
        pltpu.VMEM((6, rows, cols), BF16),
        pltpu.VMEM((2, rows, cols), BF16),
        pltpu.VMEM((rows, cols), BF16),
    ]


def layer(*args):
    blocks = pltpu.VMEM((16, 128, 1024), BF16)
    column = pltpu.VMEM((8, 128, 1024), BF16)

    def held(*dims, dtype=BF16):
        return pltpu.VMEM(dims, dtype)

    return pl.pallas_call(
        layer_kernel,
        name="layer",
        out_shape=(
            shape((128, 1024)), shape((128, 1024)), shape((16, UNITS, 128)),
            shape((16, 96, 256)), shape((16, LATE, 128)),
        ),
        in_specs=[VMEM, VMEM, ANY] + [VMEM] * 7,
        out_specs=(VMEM, VMEM, ANY, ANY, ANY),
        scratch_shapes=[
            held(208, 1024), held(128, 1024, dtype=F32), held(64, 2048), held(2 * UNITS, 128),
            held(384, 1024), held(1, 1024, dtype=F32), held(16, 64, 1024),
            blocks, blocks, column, column, column, column,
            held(64, 2048), held(64, 2048), held(64, 2048),
            held(2048, 64), held(2048, 64), held(2048, 64),
            held(64, 2048, dtype=F32), held(1, 2048, dtype=F32),
            held(3, 128, 128), held(UNITS, 128, dtype=F32), held(208, 128), held(2 * UNITS, 128),
            held(48, 1024), held(64, 2048), held(16, 64, 128), held(16, 64, 128),
            held(1024, 1024), held(2 * UNITS, 1024), held(384, 1024), held(UNITS, 1024),
            held(UNITS, 1024), held(2 * UNITS, 1024), held(128, 1024, dtype=F32),
            *column_scratch(128, 1024), held(2 * UNITS, 1024), *fsdp_scratch(2 * UNITS, 128),
            held(128, 1024, dtype=F32), held(128, 1024, dtype=F32), *column_scratch(128, 1024),
            held(192, 2048), held(2048, 64, dtype=F32), held(2048, 64, dtype=F32),
            held(LATE, 1024), held(UNITS, 128), held(UNITS, 128), held(48, 512), held(96, 256),
            held(64, 1024, dtype=F32), held(48, 1024), held(LATE, 128),
            *scatter_scratch(64, 1024), *scatter_scratch(128, 1024),
            *fsdp_scratch(48, 1024), *fsdp_scratch(LATE, 128),
            dma(B + 144), dma(B + 144), dma(10),
        ],
        compiler_params=params(1),
    )(*args)


def nt(a, b):
    return lax.dot_general(a, b, (((1,), (1,)), ((), ())), preferred_element_type=F32)


def tn(a, b):
    return lax.dot_general(a, b, (((0,), (0,)), ((), ())), preferred_element_type=F32)


def nn(a, b):
    return jnp.dot(a, b, preferred_element_type=F32)


def normalize(v):
    centered = v - jnp.mean(v, axis=-1, keepdims=True)
    inv = lax.rsqrt(jnp.mean(centered * centered, axis=-1, keepdims=True) + EPSILON)
    return centered * inv, inv


def norm_back(e, xhat, inv, gain):
    eg = e * gain
    return inv * (
        eg - jnp.mean(eg, axis=-1, keepdims=True)
        - xhat * jnp.mean(eg * xhat, axis=-1, keepdims=True)
    )


def rope_t(v, cos, sin):
    a, b = v[:32], v[32:]
    return jnp.concatenate([a * cos - b * sin, b * cos + a * sin], axis=0)


def unrope_t(v, cos, sin):
    a, b = v[:32], v[32:]
    return jnp.concatenate([a * cos + b * sin, b * cos - a * sin], axis=0)


def rope_tables():
    inverse = np.float32(ROPE_BASE) ** (-(np.arange(32, dtype=np.float32) * 2.0) / 64)
    angles = inverse[:, None].astype(np.float32) * np.arange(2048, dtype=np.float32)[None, :]
    return np.cos(angles).astype(np.float32), np.sin(angles).astype(np.float32)


def body(
    hidden_in, qkv_weight, out_weight, gate_up_weight, down_weight, attn_gain, mlp_gain, out_grad
):
    hidden_b, grad_b = hidden_in[0], out_grad[0]
    cos, sin = rope_tables()
    cos, sin = jnp.asarray(cos), jnp.asarray(sin)
    result, input_grad, gu_pieces, row_pieces, late_pieces = layer(
        hidden_b, grad_b, qkv_weight, out_weight, gate_up_weight, down_weight,
        attn_gain[None], mlp_gain[None], cos, sin,
    )
    qkv_grad = (
        late_pieces[:, :192].reshape(16, 3, 64, 128).transpose(3, 1, 0, 2).reshape(128, 3072)
    ).astype(F32)
    gain_grads = jnp.sum(late_pieces[:, 192:194].astype(F32), axis=0)
    gate_up = gu_pieces.reshape(2, 8, UNITS, 128)[:, :, :328].transpose(0, 2, 1, 3)
    gate_up_grad = gate_up.reshape(5248, 128).astype(F32).T
    down_rows = row_pieces.reshape(2, 8, 2, 48, 256)[:, :, :, :41].transpose(3, 1, 0, 2, 4)
    down_grad = down_rows.reshape(328, 1024).astype(F32)
    out_rows = late_pieces[:, 208:272].reshape(16, 8, 8, 128).transpose(0, 2, 1, 3)
    out_weight_grad = out_rows.reshape(128, 1024).astype(F32)
    return (
        result[None], input_grad[None], qkv_grad, out_weight_grad, gate_up_grad, down_grad,
        gain_grads[0], gain_grads[1],
    )


def solution(mesh):
    return jax.shard_map(
        body,
        mesh=mesh,
        in_specs=(
            P("fsdp", "ctx", None), P("fsdp", None), P("fsdp", None), P("fsdp", None),
            P("fsdp", None), P("fsdp"), P("fsdp"), P("fsdp", "ctx", None),
        ),
        out_specs=(
            P("fsdp", "ctx", None), P("fsdp", "ctx", None), P("fsdp", None), P("fsdp", None),
            P("fsdp", None), P("fsdp", None), P("fsdp"), P("fsdp"),
        ),
        check_vma=False,
    )
```
